32 devices in a mesh: groups: 2 (over y), seg: 4 (over z), slab: 2 (over x), comp: 2 (over core).
Axes of the slice: x: 2, y: 2, z: 4, core: 2. Of those that a mesh axis runs over, the one named last changes fastest.
Arguments:
- base: float32 [8, 3, 64, 4096], P(('groups', 'seg'), None, 'slab'), parts along dimension 0, may hold values from -6 to 6
- state: float32 [8, 2, 3, 64, 4096], P(('groups', 'seg'), 'comp', None, 'slab'), parts along dimension 0, may hold values from -6 to 6
- wavenumber: int32 [2], P('groups'), parts along dimension 0, may hold values from 1 to 4
- cutoff: int32 [6], P('groups'), parts along dimension 0, may hold values from 18 to 21, as said below
Outputs:
- base_gap: float32 [8, 3, 64, 4096], P(('groups', 'seg'), None, ('slab', 'comp')), parts along dimension 0
- state_gap: float32 [8, 2, 3, 64, 4096], P(('groups', 'seg'), 'comp', None, 'slab'), parts along dimension 0
The draws below stay inside these ranges and needn't reach their ends.
There are 2 independent parts, one for each index of `groups`. The reference program is written for one: setup_inputs(seed, part) draws one part's arguments, and reference() takes and returns one part's arrays. A program takes and returns all parts, laid end to end along the dimension named above; each array names one. Nothing has to cross between parts.
Inputs may be any that keep to these rules, and one draw needn't show every extreme that they name: `cutoff`: each entry is at most one third of 64, rounded down, and at least that minus three; one entry always equals it.
All inputs are finite; a program needn't handle non-finite values.
Results may differ from the reference program's by a relative error of at most 0.0001.
Values sent between devices are 32-bit elements; how exact they have to be, the bound alone decides.
A program may use at most 128 MiB of HBM per device.

```python
import jax
import jax.numpy as jnp
from jax import lax

N = 64
SEG = 4


def draw_cutoff(key, part):
    first_key, second_key = jax.random.split(jax.random.fold_in(key, 17))
    offsets = jax.random.randint(first_key, (3,), 0, 4)
    chosen = jax.random.randint(second_key, (), 0, 3)
    offsets = jnp.where(jnp.arange(3) == chosen, 0, offsets)
    return (N // 3 - offsets).astype(jnp.int32)


def levels(stream_key, shape, pieces, least, top_value):
    factor_of, own = 1.0, jax.random.fold_in(stream_key, 6)
    for dim, parts in pieces:
        steps = jnp.exp(jax.random.uniform(jax.random.fold_in(own, dim), (parts,), jnp.float32, least / len(pieces), top_value / len(pieces)))
        factor_of = factor_of * jnp.repeat(steps, shape[dim] // parts).reshape([-1 if axis == dim else 1 for axis in range(len(shape))])
    return factor_of


def noise(own_key, dims, width, most, shards=(), kind=jnp.bfloat16):
    result = width * jax.random.normal(own_key, dims, jnp.float32)
    if shards:
        result = result * levels(own_key, dims, shards, -0.22, 0.18)
    return jnp.clip(result, -most, most).astype(kind)


def setup_inputs(seed: int = 0, part: int = 0) -> dict:
    keys = jax.random.split(jax.random.key(seed), 5)
    own_keys = jax.random.split(jax.random.fold_in(keys[4], part), 5)
    base = noise(own_keys[0], (SEG, 3, N, N * N), 1.0, 6.0, ((0, 4), (2, 2)), jnp.float32)
    state = noise(own_keys[1], (SEG, 2, 3, N, N * N), 1.0, 6.0, ((0, 4), (1, 2), (3, 2)), jnp.float32)
    wavenumber = jax.random.randint(own_keys[2], (1,), 1, 5).astype(jnp.int32)
    cutoff = draw_cutoff(jax.random.fold_in(jax.random.fold_in(keys[4], part), 71), part)
    return dict(base=base, state=state, wavenumber=wavenumber, cutoff=cutoff)


viscosity = 0.025
time_step = 0.02
forcing_amp = 10.0


def wavenumbers(grid_points):
    position = jnp.arange(grid_points, dtype=jnp.int32)
    return jnp.where(position < grid_points // 2, position, position - grid_points)


def transform(field):
    return jnp.fft.fftn(field, axes=(-3, -2, -1))


def restore(modes):
    return jnp.real(jnp.fft.ifftn(modes, axes=(-3, -2, -1)))


def reference(base, state, wavenumber, cutoff):
    base = base.reshape(SEG, 3, N, N, N)
    state = state.reshape(SEG, 2, 3, N, N, N)
    spectrum = wavenumbers(N)
    wave_x = jnp.broadcast_to(spectrum[:, None, None], (N, N, N))
    wave_y = jnp.broadcast_to(spectrum[None, :, None], (N, N, N))
    wave_z = jnp.broadcast_to(spectrum[None, None, :], (N, N, N))
    inside = (jnp.abs(wave_x) <= cutoff[0]) & (jnp.abs(wave_y) <= cutoff[1]) & (jnp.abs(wave_z) <= cutoff[2])
    keep_mask = inside.astype(jnp.float32)
    float_x = wave_x.astype(jnp.float32)
    float_y = wave_y.astype(jnp.float32)
    float_z = wave_z.astype(jnp.float32)
    waves_stack = jnp.stack([float_x, float_y, float_z])
    ksquare = float_x * float_x + float_y * float_y + float_z * float_z
    safe_square = jnp.where(ksquare > 0, ksquare, jnp.ones_like(ksquare))
    damping = 1.0 / (1.0 + viscosity * time_step * ksquare)

    def project(field):
        divergence = (float_x * field[0] + float_y * field[1] + float_z * field[2]) / safe_square
        return jnp.stack([field[0] - float_x * divergence, field[1] - float_y * divergence, field[2] - float_z * divergence])

    grid_index = jnp.arange(N, dtype=jnp.int32)
    phase = jnp.mod(wavenumber[0] * grid_index, N).astype(jnp.float32) * (2.0 * jnp.pi / N)
    forcing = jnp.broadcast_to(forcing_amp * jnp.sin(phase)[None, :, None], (N, N, N))

    def advance(segment):
        flow, paired = segment
        flow_hat = transform(flow) * keep_mask
        gradient = restore(1j * waves_stack[None, :] * flow_hat[:, None])
        base_drive = jnp.sum(gradient * flow[None, :], axis=1)
        base_drive = jnp.concatenate([base_drive[:1] - forcing[None], base_drive[1:]], axis=0)
        flow_new = restore(damping * project(flow_hat - time_step * keep_mask * transform(base_drive)))
        results = []
        for branch, orient in ((0, 1.0), (1, -1.0)):
            field = paired[branch]
            field_hat = transform(field) * keep_mask
            flux_hat = transform(field[:, None] * flow[None, :])
            divergence = jnp.sum(1j * waves_stack[None, :] * flux_hat, axis=1)
            if branch == 0:
                matrix = gradient
            else:
                matrix = jnp.swapaxes(gradient, 0, 1)
            coupling = jnp.sum(matrix * field[None, :], axis=1)
            state_drive = keep_mask * (orient * divergence + transform(coupling))
            results.append(restore(damping * project(field_hat - time_step * state_drive)))
        return flow_new, jnp.stack(results)

    flow_next, state_next = lax.map(advance, (base, state))
    base_gap = flow_next - jnp.roll(base, -1, axis=0)
    tangent_gap = state_next[:, 0] - jnp.roll(state[:, 0], -1, axis=0)
    adjoint_gap = state_next[:, 1] - jnp.roll(state[:, 1], 1, axis=0)
    state_gap = jnp.stack([tangent_gap, adjoint_gap], axis=1)
    return base_gap.reshape(SEG, 3, N, N * N).astype(jnp.float32), state_gap.reshape(SEG, 2, 3, N, N * N).astype(jnp.float32)
```

```python
import functools

import jax
import jax.numpy as jnp
import ml_dtypes
import numpy as np
from jax import lax
from jax.experimental import pallas as pl
from jax.experimental.pallas import tpu as pltpu
from jax.sharding import PartitionSpec as P

N = 64
BACK, GRID, AHEAD, SPEC, Z1, Z2, Z3, Y1 = 4, 4, 4, 4, 8, 4, 8, 6
THIRD = N // 3
LOW = THIRD - 3
KZ = THIRD + 1
KP = 24
MP = 48
PAIRS = N // 2
FLUX = 14 * 10**9
HALF = KZ // 2
viscosity = 0.025
time_step = 0.02
forcing_amp = 10.0
f32 = jnp.float32
bf16 = jnp.bfloat16

NN = (((1,), (0,)), ((), ()))
NT = (((1,), (1,)), ((), ()))


def split(value):
    high = value.astype(bf16)
    return high, (value - high.astype(f32)).astype(bf16)


def dot3(left, right, dims):
    dot = functools.partial(lax.dot_general, dimension_numbers=dims, preferred_element_type=f32)
    return dot(left[0], right[0]) + (dot(left[0], right[1]) + dot(left[1], right[0]))


def table(values):
    values = np.asarray(values, np.float32)
    high = values.astype(ml_dtypes.bfloat16)
    low = (values - high.astype(np.float32)).astype(ml_dtypes.bfloat16)
    return np.stack([high, low], axis=-3)


def table3(values):
    high, low = np.moveaxis(table(values), -3, 0)
    return np.concatenate([high, high, low], axis=-1)


def left3(left, value, dims):
    high, low = split(value)
    deep = jnp.concatenate([high, low, high], axis=dims[0][1][0])
    return lax.dot_general(left, deep, dimension_numbers=dims, preferred_element_type=f32)


def signed():
    m = np.arange(2 * THIRD + 1)
    return np.where(m <= THIRD, m, m - (2 * THIRD + 1))


def angles(first, second):
    return np.mod(np.outer(first, second), N) * (2 * np.pi / N)


def cuts():
    return range(LOW, THIRD + 1)


def z_tables():
    plain, ik = [], []
    k = np.arange(KZ)
    a = angles(k, np.arange(N))
    for cut in cuts():
        keep = 1.0 * (k <= cut)[:, None]
        w = np.zeros((2, KP, N))
        v = np.zeros((2, KP, N))
        w[0, :KZ], w[1, :KZ] = keep * np.cos(a), -keep * np.sin(a)
        v[0, :KZ], v[1, :KZ] = keep * k[:, None] * np.sin(a), keep * k[:, None] * np.cos(a)
        plain.append(np.kron(np.eye(2), w.reshape(2 * KP, N)))
        ik.append(np.kron(np.eye(2), v.reshape(2 * KP, N)))
    return table3(np.stack([np.stack(plain), np.stack(ik)], axis=1))


def y_tables():
    out = []
    m = signed()
    count = len(m)
    a = angles(m, np.arange(N))
    for cut in cuts():
        keep = 1.0 * (np.abs(m) <= cut)[:, None]
        c, s = keep * np.cos(a), keep * np.sin(a)
        w = np.zeros((2, MP, N, 2))
        w[0, :count, :, 0], w[0, :count, :, 1] = c, s
        w[1, :count, :, 0], w[1, :count, :, 1] = -s, c
        v = np.zeros_like(w)
        v[0, :count] = -m[:, None, None] * w[1, :count]
        v[1, :count] = m[:, None, None] * w[0, :count]
        out.append(np.stack([w.reshape(2 * MP, 2 * N), v.reshape(2 * MP, 2 * N)]))
    return table3(np.stack(out))


def y_back():
    m = signed()
    count = len(m)
    a = angles(np.arange(N), m)
    c, s = np.cos(a) / N, np.sin(a) / N
    w = np.zeros((N, 2, 2, MP))
    w[:, 0, 0, :count], w[:, 0, 1, :count] = c, -s
    w[:, 1, 0, :count], w[:, 1, 1, :count] = s, c
    v = np.zeros_like(w)
    v[:, :, 0, :count] = m * w[:, :, 1, :count]
    v[:, :, 1, :count] = -m * w[:, :, 0, :count]
    return table3(np.stack([w.reshape(2 * N, 2 * MP), v.reshape(2 * N, 2 * MP)]))


def z_back():
    k = np.arange(KZ)
    a = angles(k, np.arange(N))
    weight = (np.where(k == 0, 1.0, 2.0) / N)[:, None]
    w = np.zeros((2, KP, N))
    w[0, :KZ], w[1, :KZ] = weight * np.cos(a), -weight * np.sin(a)
    v = np.zeros_like(w)
    v[0, :KZ] = k[:, None] * w[1, :KZ]
    v[1, :KZ] = -k[:, None] * w[0, :KZ]
    pair = lambda t: np.kron(np.eye(2), t.reshape(2 * KP, N))
    return table3(np.stack([pair(w).T, pair(v).T]))


def x_filters(slabs):
    rows = N // slabs
    out = []
    x = np.arange(N)
    for cut in cuts():
        n = np.arange(-cut, cut + 1)
        d = np.mod(x[:, None] - x[None, :], N)
        phase = 2 * np.pi / N * n[:, None, None] * -d
        plain = np.cos(phase).sum(0) / N
        deriv = (-n[:, None, None] * np.sin(phase)).sum(0) / N
        both = np.stack([plain, deriv]).reshape(2, slabs, rows, slabs, rows)
        wide = np.zeros((slabs, 2, slabs, 3, rows, 3, rows))
        for i in range(3):
            wide[:, :, :, i, :, i, :] = both.transpose(3, 0, 1, 2, 4)
        out.append(wide.reshape(slabs, 2, slabs, 3 * rows, 3 * rows))
    return table(np.stack(out))


def x_tables(slabs):
    rows = N // slabs
    n = signed()
    count = len(n)
    a = angles(np.arange(N), n).reshape(slabs, rows, count)
    out = []
    for cut in cuts():
        keep = 1.0 * (np.abs(n) <= cut)
        c, s = np.cos(a) * keep, np.sin(a) * keep
        w = np.zeros((slabs, 2, 2, 3, rows, 3, 2, 64))
        for i in range(3):
            w[:, 0, 0, i, :, i, 0, :count] = c
            w[:, 0, 0, i, :, i, 1, :count] = -s
            w[:, 0, 1, i, :, i, 0, :count] = s
            w[:, 0, 1, i, :, i, 1, :count] = c
        w[:, 1, :, :, :, :, 0, :count] = -n * w[:, 0, :, :, :, :, 1, :count]
        w[:, 1, :, :, :, :, 1, :count] = n * w[:, 0, :, :, :, :, 0, :count]
        out.append(w.reshape(slabs, 2, 2, 3 * rows, 384))
    return table(np.stack(out))


def x_back(slabs):
    rows = N // slabs
    n = signed()
    count = len(n)
    a = angles(n, np.arange(N)).reshape(count, slabs, rows).transpose(1, 0, 2)
    c, s = np.cos(a) / N, np.sin(a) / N
    w = np.zeros((slabs, 2, 3, 2, 64, 3, rows))
    for i in range(3):
        w[:, 0, i, 0, :count, i] = c
        w[:, 0, i, 1, :count, i] = -s
        w[:, 1, i, 0, :count, i] = s
        w[:, 1, i, 1, :count, i] = c
    return table(w.reshape(slabs, 2, 384, 3 * rows))


def both(ref, *index):
    return ref[(*index, 0)], ref[(*index, 1)]


def lanes(p):
    return pl.ds(pl.multiple_of(p * 128, 128), 128)


def pair_rows(p):
    return pl.ds(pl.multiple_of(p * 4 * KP, 8), 4 * KP)


def column(k):
    return pl.ds(k, 2 * N, stride=KP)


def flat(block):
    return block.reshape(block.shape[0] * block.shape[1], block.shape[2])


def loop(count, unroll, step):
    def go(i, carry):
        step(i)
        return carry

    lax.fori_loop(0, count, go, 0, unroll=unroll)


def clear_padding(*works):
    for k in range(KZ, KP):
        for work in works:
            work[column(k), :] = jnp.zeros((2 * N, work.shape[1]), f32)


def base_ahead(base_ref, wz_ref, wy_ref, out_ref, half_ref, work):
    def along_z(p):
        work[pair_rows(p), :] = left3(wz_ref[0], flat(base_ref[:, :, lanes(p)]), NT)

    loop(PAIRS, Z1, along_z)

    def along_y(k):
        out_ref[k] = left3(wy_ref[0], work[column(k), :], NN)

    loop(KZ, Y1, along_y)
    first = HALF * lax.axis_index("comp")

    def share(j):
        half_ref[j] = out_ref[first + j]

    loop(HALF, 1, share)


def sign_step():
    return jnp.where(lax.axis_index("comp") == 0, -time_step, time_step).astype(f32)


def flux_ahead(base_ref, state_ref, wz_ref, wy_ref, g_ref, work_a, work_b):
    scale = sign_step()

    def along_z(p):
        state = state_ref[:, :, lanes(p)]
        scaled = state * scale
        f1, f2 = (flat(scaled * base_ref[j, :, lanes(p)][None]) for j in (1, 2))
        plain = wz_ref[0]
        work_a[pair_rows(p), :] = left3(plain, flat(state), NT) + left3(wz_ref[1], f2, NT)
        work_b[pair_rows(p), :] = left3(plain, f1, NT)

    loop(PAIRS, Z2, along_z)

    def along_y(k):
        g_ref[k] = left3(wy_ref[0], work_a[column(k), :], NN) + left3(
            wy_ref[1], work_b[column(k), :], NN
        )

    loop(KZ, Y1, along_y)


def flux_x_ahead(base_ref, state_ref, wz_ref, wy_ref, f_ref, work):
    scale = sign_step()

    def along_z(p):
        f0 = flat(state_ref[:, :, lanes(p)] * scale * base_ref[0, :, lanes(p)][None])
        work[pair_rows(p), :] = left3(wz_ref[0], f0, NT)

    loop(PAIRS, Z2, along_z)

    def along_y(k):
        f_ref[k] = left3(wy_ref[0], work[column(k), :], NN)

    loop(KZ, Y1, along_y)


def gradients(
    slabs, count, *refs,
):
    got, rest = refs[:count], refs[count:]
    side = lax.axis_index("comp")
    if count == 1:
        visits = [(lambda j: (j, [got[0][s, j] for s in range(slabs)]), KZ)]
    else:
        own, mine, partner = got

        def visit(ref, first):
            return lambda j: (first + j, [own[first + j], ref[j]])

        visits = [
            (visit(mine, HALF * side), HALF),
            (visit(partner, HALF * (1 - side)), HALF),
        ]
    gradients_of(slabs, visits, *rest)


def gradients_of(
    slabs, visits, base_ref, state_ref, force_ref, pd_ref, yb_ref, zb_ref, wz_ref, wy_ref,
    xt_ref, base_out_ref, coupled_ref, work_0, work_1, work_2,
):
    tangent = lax.axis_index("comp") == 0

    def back_y(visit, j):
        k, sources = visit(j)
        sources = [split(source) for source in sources]

        def across(kind):
            total = dot3(sources[0], both(pd_ref, kind, 0), NN)
            for s in range(1, slabs):
                total = total + dot3(sources[s], both(pd_ref, kind, s), NN)
            return total

        plain, deriv = across(0), across(1)
        work_0[column(k), :] = left3(yb_ref[0], deriv, NN)
        work_1[column(k), :] = left3(yb_ref[1], plain, NN)
        work_2[column(k), :] = left3(yb_ref[0], plain, NN)

    clear_padding(work_0, work_1, work_2)
    for visit, count in visits:
        loop(count, BACK, functools.partial(back_y, visit))

    def grid_space(p):
        state = state_ref[:, :, lanes(p)]
        base = base_ref[:, :, lanes(p)]
        grad = []
        for work, kind in ((work_0, 0), (work_1, 0), (work_2, 1)):
            rows = left3(zb_ref[kind], work[pair_rows(p), :], NN).T
            grad.append(rows.reshape(base.shape))
        coupled, driven = [], []
        for i in range(3):
            total = 0.0
            drive = 0.0
            for j in range(3):
                total = total + jnp.where(tangent, grad[j][i], grad[i][j]) * state[j]
                drive = drive + grad[j][i] * base[j]
            if i == 0:
                drive = drive - force_ref[:, lanes(p)]
            coupled.append(-time_step * total)
            driven.append(base[i] - time_step * drive)
        plain = wz_ref[0]
        coupled_ref[pair_rows(p), :] = left3(plain, jnp.concatenate(coupled, axis=0), NT)
        work_1[pair_rows(p), :] = left3(plain, jnp.concatenate(driven, axis=0), NT)

    loop(PAIRS, GRID, grid_space)

    waves = plane_waves()
    first = HALF * lax.axis_index("comp")

    def base_ahead_x(step):
        j = HALF - 1 - step
        k = first + j
        driven = left3(wy_ref[0], work_1[column(k), :], NN)
        modes = 0.0
        for d in range(2):
            rows = slice(d * MP, (d + 1) * MP)
            modes = modes + dot3(split(driven[rows]), both(xt_ref, 0, d), NN)
        emit(waves, base_out_ref, j, HALF, modes, k)

    loop(HALF, AHEAD, base_ahead_x)


def emit(waves, ref, slot, last, modes, k):
    new = projected(waves, modes, k)
    ref[slot] = jnp.concatenate(new[:2], axis=1)
    ref[last] = jnp.concatenate([new[2], jnp.zeros_like(new[2])], axis=1)


def state_ahead_x(coupled_ref, wy_ref, xt_ref, g_ref, f_ref, out_ref):
    waves = plane_waves()

    def ahead_x(step):
        k = KZ - 1 - step
        total = g_ref[k] + left3(wy_ref[0], coupled_ref[column(k), :], NN)
        outer = f_ref[k]
        modes = 0.0
        for d in range(2):
            rows = slice(d * MP, (d + 1) * MP)
            modes = modes + dot3(split(total[rows]), both(xt_ref, 0, d), NN)
            modes = modes + dot3(split(outer[rows]), both(xt_ref, 1, d), NN)
        emit(waves, out_ref, k, KZ, modes, k)

    loop(KZ, AHEAD, ahead_x)


def plane_waves():
    column_n = lax.rem(lax.broadcasted_iota(jnp.int32, (MP, 128), 1), 64)
    row_m = lax.broadcasted_iota(jnp.int32, (MP, 128), 0)
    wrap = lambda v: jnp.where(v <= THIRD, v, v - (2 * THIRD + 1)).astype(f32)
    return wrap(column_n), wrap(row_m)


def projected(waves, modes, k):
    wave_x, wave_y = waves
    wave_z = jnp.asarray(k, jnp.int32).astype(f32)
    square = wave_x * wave_x + wave_y * wave_y + wave_z * wave_z
    safe = jnp.where(square > 0, square, 1.0)
    damping = 1.0 / (1.0 + viscosity * time_step * square)
    w = [modes[:, i * 128 : (i + 1) * 128] for i in range(3)]
    divergence = (wave_x * w[0] + wave_y * w[1] + wave_z * w[2]) / safe
    return [
        damping * (w[0] - wave_x * divergence),
        damping * (w[1] - wave_y * divergence),
        damping * (w[2] - wave_z * divergence),
    ]


def finish(count, halved, *refs):
    parts, (near_ref, xb_ref, yb_ref, zb_ref, out_ref, work) = refs[:count], refs[count:]
    wave_x, wave_y = plane_waves()
    clear_padding(work)

    def spectral(parts, first, last, j):
        k = first + j
        modes, third = 0.0, 0.0
        for part in parts:
            modes = modes + part[j]
            third = third + part[last, :, :128]
        w0, w1 = modes[:, :128], modes[:, 128:]
        whole = jnp.asarray(k, jnp.int32)
        inverse = 1.0 / jnp.maximum(whole, 1).astype(f32)
        w2 = jnp.where(whole == 0, third, -(wave_x * w0 + wave_y * w1) * inverse)
        new = split(jnp.concatenate([w0, w1, w2], axis=1))
        rows = [dot3(new, both(xb_ref, d), NN) for d in range(2)]
        work[column(k), :] = left3(yb_ref[0], jnp.concatenate(rows, axis=0), NN)

    if halved:
        side = lax.axis_index("comp")
        for part, place in zip(parts, (side, 1 - side)):
            loop(HALF, SPEC, functools.partial(spectral, [part], HALF * place, HALF))
    else:
        loop(KZ, SPEC, functools.partial(spectral, parts, 0, KZ))

    def along_z(p):
        rows = left3(zb_ref[0], work[pair_rows(p), :], NN).T
        near = near_ref[:, :, lanes(p)]
        out_ref[:, :, lanes(p)] = rows.reshape(near.shape) - near

    loop(PAIRS, Z3, along_z)


def call(kernel, out_shape, scratch, cost, *operands):
    return pl.pallas_call(
        kernel,
        out_shape=out_shape,
        in_specs=[pl.BlockSpec(memory_space=pltpu.VMEM)] * len(operands),
        out_specs=jax.tree.map(lambda _: pl.BlockSpec(memory_space=pltpu.VMEM), out_shape),
        scratch_shapes=scratch,
        compiler_params=pltpu.CompilerParams(vmem_limit_bytes=48 * 2**20),
        cost_estimate=pl.CostEstimate(flops=cost, bytes_accessed=2**10, transcendentals=0),
    )(*operands)


def body(base, state, wavenumber, cutoff):
    base, state = base[0], state[0, 0]
    slab_rows = base.shape[1]
    half = slab_rows // lax.axis_size("comp")
    slabs = lax.axis_size("slab")
    segs = lax.axis_size("seg")
    slab = lax.axis_index("slab")
    side = lax.axis_index("comp")
    width = 3 * slab_rows
    which = cutoff - LOW

    route = [((s, 0), ((s - 1) % segs, 0)) for s in range(segs)]
    route += [((s, 1), ((s + 1) % segs, 1)) for s in range(segs)]
    route = [(a * 2 + b, c * 2 + d) for (a, b), (c, d) in route]
    wz = lax.dynamic_index_in_dim(jnp.asarray(z_tables()), which[2], 0, False)
    wy = lax.dynamic_index_in_dim(jnp.asarray(y_tables()), which[1], 0, False)
    filters, ahead = jnp.asarray(x_filters(slabs)), jnp.asarray(x_tables(slabs))
    pick = lambda t: lax.dynamic_slice(
        t, (which[0], slab) + (0,) * (t.ndim - 2), (1, 1) + t.shape[2:]
    )[0, 0]
    pd, xt = pick(filters), pick(ahead)
    xb = lax.dynamic_index_in_dim(jnp.asarray(x_back(slabs)), slab, 0, False)
    yb, zb = jnp.asarray(y_back()), jnp.asarray(z_back())

    modes = jax.ShapeDtypeStruct((KZ, 2 * MP, width), f32)
    half_modes = jax.ShapeDtypeStruct((HALF, 2 * MP, width), f32)
    spectrum = jax.ShapeDtypeStruct((KZ + 1, MP, 256), f32)
    half_spectrum = jax.ShapeDtypeStruct((HALF + 1, MP, 256), f32)
    work = pltpu.VMEM((2 * N * KP, width), f32)
    own, share = call(base_ahead, (modes, half_modes), [work], 4 * 10**9, base, wz, wy)
    later, later_base, share = lax.optimization_barrier((state, base, share))
    near_state = lax.ppermute(later, ("seg", "comp"), route)
    base_half = lax.dynamic_slice_in_dim(later_base, side * half, half, 1)
    near_base = lax.ppermute(base_half, "seg", [((s + 1) % segs, s) for s in range(segs)])
    if slabs == 2:
        other = lax.ppermute(share, "slab", [(0, 1), (1, 0)])
        partner = lax.ppermute(other, "comp", [(0, 1), (1, 0)])
        first = slab == 0
        got = (own, other, partner)
        pd = jnp.where(first, pd, pd[:, ::-1])
    else:
        got = (lax.all_gather(own, "slab"),)
    g = call(flux_ahead, modes, [work] * 2, FLUX, base, state, wz, wy)
    f = call(flux_x_ahead, modes, [work], 10**9, base, state, wz, wy)

    *got, g, f = lax.optimization_barrier((*got, g, f))

    y = jnp.arange(N, dtype=jnp.int32)
    phase = jnp.mod(wavenumber[0] * y, N).astype(f32) * (2.0 * jnp.pi / N)
    force = jnp.repeat(forcing_amp * jnp.sin(phase), N)[None]
    lined = jax.ShapeDtypeStruct((2 * N * KP, width), f32)
    base_modes, coupled = call(
        functools.partial(gradients, slabs, len(got)), (half_spectrum, lined), [work] * 3,
        25 * 10**9, *got, base, state, force, pd, yb, zb, wz, wy, xt,
    )
    state_modes = call(state_ahead_x, spectrum, [], 3 * 10**9, coupled, wy, xt, g, f)
    near_state, near_base, state_modes = lax.optimization_barrier(
        (near_state, near_base, state_modes)
    )
    if slabs == 2:
        swap = lambda v: lax.ppermute(v, "slab", [(0, 1), (1, 0)])
        state_other = swap(state_modes)
        base_other, state_modes = lax.optimization_barrier((swap(base_modes), state_modes))
        base_sum = base_modes + base_other
        state_parts = (state_modes, state_other)
    else:
        base_sum = lax.psum(base_modes, "slab")
        state_parts = (lax.psum(state_modes, "slab"),)
    base_parts = (base_sum, lax.ppermute(base_sum, "comp", [(0, 1), (1, 0)]))

    shape = jax.ShapeDtypeStruct(base.shape, f32)
    last = functools.partial(finish, len(state_parts), False)
    last_base = functools.partial(finish, 2, True)
    near_wide = jnp.concatenate([near_base, near_base], axis=1)
    base_gap = call(last_base, shape, [work], 10**8, *base_parts, near_wide, xb, yb, zb)
    base_gap = lax.dynamic_slice_in_dim(base_gap, side * half, half, 1)
    state_gap = call(last, shape, [work], 10**10, *state_parts, near_state, xb, yb, zb)
    return base_gap[None], state_gap[None, None]


LANES = 128
QK = 24
SIDE_QUADS = 3
STATE_QUADS = 6


def lane_pad(values, axis, size=LANES):
    pad = [(0, 0)] * values.ndim
    pad[axis] = (0, size - values.shape[axis])
    return np.pad(values, pad)


def halves(values):
    values = np.asarray(values, np.float32)
    high = values.astype(ml_dtypes.bfloat16)
    return high, (values - high.astype(np.float32)).astype(ml_dtypes.bfloat16)


def filter_tables(slabs):
    rows = N // slabs
    x = np.arange(N)
    out = []
    for cut in cuts():
        n = np.arange(-cut, cut + 1)
        d = np.mod(x[:, None] - x[None, :], N)
        phase = 2 * np.pi / N * n[:, None, None] * -d
        plain = np.cos(phase).sum(0) / N
        deriv = (-n[:, None, None] * np.sin(phase)).sum(0) / N
        both_kinds = np.stack([plain, deriv]).reshape(2, slabs, rows, slabs, rows)
        per_slab = []
        for slab in range(slabs):
            blocks = []
            for source in (slab, 1 - slab):
                wide = np.zeros((3, rows, 2, LANES))
                for i in range(3):
                    wide[i, :, :, i * rows : (i + 1) * rows] = both_kinds[
                        :, source, :, slab
                    ].transpose(1, 0, 2)
                blocks.append(halves(lane_pad(wide.reshape(3 * rows, 2 * LANES), 0)))
            (own_high, own_low), (far_high, far_low) = blocks
            per_slab.append(
                np.concatenate([own_high, own_high, far_high, far_high, own_low, far_low])
            )
        out.append(np.stack(per_slab))
    return np.stack(out, axis=1)


def ahead_tables(slabs):
    rows = N // slabs
    n = signed()
    count = len(n)
    a = angles(np.arange(N), n).reshape(slabs, rows, count)
    c, s = np.cos(a), np.sin(a)
    w = np.zeros((slabs, 2, 2, 3, rows, 3, 2, 64))
    for i in range(3):
        w[:, 0, 0, i, :, i, 0, :count] = c
        w[:, 0, 0, i, :, i, 1, :count] = -s
        w[:, 0, 1, i, :, i, 0, :count] = s
        w[:, 0, 1, i, :, i, 1, :count] = c
    w[:, 1, :, :, :, :, 0, :count] = -n * w[:, 0, :, :, :, :, 1, :count]
    w[:, 1, :, :, :, :, 1, :count] = n * w[:, 0, :, :, :, :, 0, :count]
    high, low = halves(lane_pad(w.reshape(slabs, 2, 2, 3 * rows, 3 * LANES), 3))
    blocks = []
    for kind in range(2):
        h, l = high[:, kind], low[:, kind]
        blocks += [h[:, 0], h[:, 0], h[:, 1], h[:, 1], l[:, 0], l[:, 1]]
    return np.concatenate(blocks, axis=1)


def behind_tables(parts):
    rows = N // parts
    n = signed()
    count = len(n)
    a = angles(n, np.arange(N)).reshape(count, parts, rows).transpose(1, 0, 2)
    c, s = np.cos(a) / N, np.sin(a) / N
    w = np.zeros((parts, 3, 2, 64, 2, LANES))
    for i in range(3):
        place = slice(i * rows, (i + 1) * rows)
        w[:, i, 0, :count, 0, place] = c
        w[:, i, 1, :count, 0, place] = -s
        w[:, i, 0, :count, 1, place] = s
        w[:, i, 1, :count, 1, place] = c
    high, low = halves(w.reshape(parts, 3 * LANES, 2 * LANES))
    return np.concatenate([high, high, low], axis=1)


def force_table():
    wave = np.arange(1, 5)
    phase = np.mod(np.outer(wave, np.arange(N)), N).astype(np.float32) * np.float32(2 * np.pi / N)
    return np.repeat(np.float32(forcing_amp) * np.sin(phase), N, axis=1)[:, None].astype(np.float32)


def cat(values, axis):
    return jnp.concatenate(values, axis=axis)


def wide_rows(*fields):
    blank = jnp.zeros((LANES - fields[0].shape[0], LANES), f32)
    return cat([part for field in fields for part in (field, blank)], 0)


def matmul(left, right):
    return lax.dot_general(left, right, NN, preferred_element_type=f32)


def half_lane(shape):
    return lax.rem(lax.broadcasted_iota(jnp.int32, shape, 1), 64)


def turn(value, shift):
    return pltpu.roll(value, shift % LANES, 1)


GAP = 2 * THIRD + 1
STEP = 64 - GAP
PIECES = (GAP, GAP - STEP, GAP - 2 * STEP)


def pack_pair(first, second):
    gap = half_lane(first[0].shape) >= GAP
    carried = (first[0], second[0], first[1])
    return [jnp.where(gap, turn(second[1], by), held) for by, held in zip(PIECES, carried)]


def unpack_pair(tiles):
    lane = half_lane(tiles[0].shape)
    last = turn(tiles[2], -PIECES[2])
    last = jnp.where(lane < 2 * STEP, turn(tiles[1], -PIECES[1]), last)
    last = jnp.where(lane < STEP, turn(tiles[0], -PIECES[0]), last)
    return (tiles[0], tiles[2]), (tiles[1], last)


def pack_share(planes):
    lane = lax.broadcasted_iota(jnp.int32, planes[0].shape, 1)
    return [jnp.where(lane < 96, planes[i], turn(planes[3], 96 - 32 * i)) for i in range(3)]


def unpack_share(tiles):
    lane = lax.broadcasted_iota(jnp.int32, tiles[0].shape, 1)
    last = jnp.where(lane < 64, turn(tiles[1], 64), turn(tiles[2], 96))
    return [*tiles, jnp.where(lane < 32, turn(tiles[0], 32), last)]


def two_columns(work, k):
    return cat([work[column(k), :], work[column(k + 1), :]], 1)


def fused(
    base_hbm, state_hbm, cutoff_ref, wave_ref, wz_hbm, wy_hbm, pd_hbm, xt_hbm, xs_hbm, xb_hbm,
    yb_hbm, zb_hbm, force_hbm, base_gap_hbm, state_gap_hbm,
    base_v, state_v, near_base, near_state, wz, wy, pd, xt, xs, xb, yb, zb, force,
    w0, w1, w2, wa, wb, wc, own, share, other, partner, g, f,
    base_send, base_recv, base_sum, state_send, state_recv, out_base, out_state,
    local_sem, out_sem, near_send, near_recv, share_send, share_recv, pass_send, pass_recv,
    base_send_sem, base_recv_sem, sum_send, sum_recv, state_send_sem, state_recv_sem,
):
    side = lax.axis_index("comp")
    slab = lax.axis_index("slab")
    seg = lax.axis_index("seg")
    segs = lax.axis_size("seg")
    far = {"slab": 1 - slab}
    twin = {"comp": 1 - side}
    after, before = lax.rem(seg + 1, segs), lax.rem(seg + segs - 1, segs)
    half = near_base.shape[1]
    quarter = N * N // 4

    def local(index, src, dst):
        return pltpu.make_async_copy(src, dst, local_sem.at[index])

    def remote(src, dst, send, recv, device):
        return pltpu.make_async_remote_copy(
            src_ref=src, dst_ref=dst, send_sem=send, recv_sem=recv, device_id=device,
            device_id_type=pl.DeviceIdType.MESH,
        )

    barrier = pltpu.get_barrier_semaphore()
    for device in (far, twin, {"seg": after}, {"seg": before}):
        pl.semaphore_signal(
            barrier, inc=1, device_id=device, device_id_type=pl.DeviceIdType.MESH
        )

    def quarter_of(ref, i):
        return ref.at[:, :, pl.ds(i * quarter, quarter)]

    wz_copy = local(0, wz_hbm, wz)
    base_copies = [
        local(1 + i, quarter_of(base_hbm, i), quarter_of(base_v, i)) for i in range(4)
    ]
    wy_copy = local(5, wy_hbm, wy)
    state_copy = local(6, state_hbm, state_v)
    late_copies = [
        local(7, pd_hbm.at[slab], pd),
        local(8, yb_hbm, yb),
        local(9, zb_hbm, zb),
        local(10, force_hbm, force),
        local(11, xt_hbm.at[slab], xt),
        local(12, xs_hbm.at[slab], xs),
        local(13, xb_hbm.at[2 * slab + side], xb),
    ]
    for copy in (wz_copy, *base_copies, wy_copy, state_copy, *late_copies):
        copy.start()

    pl.semaphore_wait(barrier, 4)
    near_copies = [
        remote(
            state_hbm, near_state, near_send.at[0], near_recv.at[0],
            {"seg": jnp.where(side == 0, before, after)},
        ),
        remote(
            base_hbm.at[:, pl.ds(half * side, half), :], near_base, near_send.at[1],
            near_recv.at[1], {"seg": before},
        ),
    ]
    for copy in near_copies:
        copy.start()

    cut_x, cut_y, cut_z = (cutoff_ref[i] for i in range(3))
    at_x, at_y, at_z = (jnp.clip(cut - LOW, 0, THIRD - LOW) for cut in (cut_x, cut_y, cut_z))

    def base_ahead_z(p):
        w0[pair_rows(p), :] = left3(wz[at_z, 0], wide_rows(flat(base_v[:, :, lanes(p)])), NT)

    wz_copy.wait()
    for i, copy in enumerate(base_copies):
        copy.wait()
        loop(PAIRS // 4, Z1, lambda p, i=i: base_ahead_z(p + i * (PAIRS // 4)))
    wy_copy.wait()

    def base_planes(q):
        planes = []
        for j in (0, 2):
            both_planes = left3(wy[at_y, 0], two_columns(w0, 4 * q + j), NN)
            planes += [both_planes[:, :LANES], both_planes[:, LANES:]]
        for i in range(4):
            own[4 * q + i] = planes[i]
        return planes

    share_copies = []
    for t in range(SIDE_QUADS):
        for i, tile in enumerate(pack_share(base_planes(SIDE_QUADS * side + t))):
            share[3 * t + i] = tile
        rows = pl.ds(3 * t, 3)
        copy = remote(
            share.at[rows], other.at[rows], share_send.at[t], share_recv.at[t], far
        )
        copy.start()
        share_copies.append(copy)
    for t in range(SIDE_QUADS):
        base_planes(SIDE_QUADS * (1 - side) + t)

    pass_copies = []

    def pass_on(t):
        share_copies[t].wait_recv()
        rows = pl.ds(3 * t, 3)
        copy = remote(
            other.at[rows], partner.at[rows], pass_send.at[t], pass_recv.at[t], twin
        )
        copy.start()
        pass_copies.append(copy)

    state_copy.wait()
    scale = sign_step()

    def flux_z(t):
        first, second = [], []
        for i in range(2):
            p = 2 * t + i
            state = state_v[:, :, lanes(p)]
            scaled = state * scale
            f0, f1, f2 = (flat(scaled * base_v[j, :, lanes(p)][None]) for j in range(3))
            plain = left3(wz[at_z, 0], wide_rows(flat(state), f0), NT)
            wa[pair_rows(p), :] = plain[:, :LANES]
            wc[pair_rows(p), :] = plain[:, LANES:]
            first.append(f1)
            second.append(f2)
        along_y = left3(wz[at_z, 0], wide_rows(*first), NT)
        along_z = left3(wz[at_z, 1], wide_rows(*second), NT)
        for i in range(2):
            p = 2 * t + i
            mine = slice(i * LANES, (i + 1) * LANES)
            wb[pair_rows(p), :] = along_y[:, mine]
            wa[pair_rows(p), :] += along_z[:, mine]

    loop(PAIRS // 2, 2, flux_z)
    pass_on(0)

    def flux_y(t):
        k = 2 * t
        extra = left3(wy[at_y, 1], two_columns(wb, k), NN)
        for i in range(2):
            whole = left3(
                wy[at_y, 0], cat([wa[column(k + i), :], wc[column(k + i), :]], 1), NN
            )
            g[k + i] = whole[:, :LANES] + extra[:, i * LANES : (i + 1) * LANES]
            f[k + i] = whole[:, LANES:]

    loop(QK // 2, 2, flux_y)
    pass_on(1)

    for copy in late_copies:
        copy.wait()

    def back_y(ref, place, t):
        q = SIDE_QUADS * place + t
        planes = unpack_share([ref[3 * t + i] for i in range(3)])
        deep = []
        for i in range(4):
            own_high, own_low = split(own[4 * q + i])
            far_high, far_low = split(planes[i])
            deep.append(cat([own_high, own_low, far_high, far_low, own_high, far_high], 1))
        filtered = matmul(cat(deep, 0), pd[at_x])
        kinds = [filtered[96 * i : 96 * (i + 1)] for i in range(4)]
        for j in (0, 2):
            along = left3(yb[1], cat([kinds[j][:, :LANES], kinds[j + 1][:, :LANES]], 1), NN)
            for i in range(2):
                k = 4 * q + j + i
                whole = left3(yb[0], kinds[j + i], NN)
                w2[column(k), :] = whole[:, :LANES]
                w0[column(k), :] = whole[:, LANES:]
                w1[column(k), :] = along[:, i * LANES : (i + 1) * LANES]

    back_y(other, side, 0)
    back_y(other, side, 1)
    pass_on(2)
    back_y(other, side, 2)
    for t in range(SIDE_QUADS):
        pass_copies[t].wait_recv()
        back_y(partner, 1 - side, t)

    tangent = side == 0
    wave = jnp.clip(wave_ref[0] - 1, 0, 3)

    def grid_space(t):
        third = left3(
            zb[1], cat([w2[pair_rows(2 * t + i), :] for i in range(2)], 1), NN
        ).T
        for i in range(2):
            p = 2 * t + i
            state = state_v[:, :, lanes(p)]
            base = base_v[:, :, lanes(p)]
            pair = left3(zb[0], cat([w0[pair_rows(p), :], w1[pair_rows(p), :]], 1), NN).T
            grad = [
                pair[:96].reshape(base.shape),
                pair[LANES : LANES + 96].reshape(base.shape),
                third[i * LANES : i * LANES + 96].reshape(base.shape),
            ]
            coupled, driven = [], []
            for a in range(3):
                total = 0.0
                drive = 0.0
                for b in range(3):
                    total = total + jnp.where(tangent, grad[b][a], grad[a][b]) * state[b]
                    drive = drive + grad[b][a] * base[b]
                if a == 0:
                    drive = drive - force[wave, :, lanes(p)]
                coupled.append(-time_step * total)
                driven.append(base[a] - time_step * drive)
            out = left3(wz[at_z, 0], wide_rows(cat(coupled, 0), cat(driven, 0)), NT)
            wa[pair_rows(p), :] = out[:, :LANES]
            wb[pair_rows(p), :] = out[:, LANES:]

    loop(PAIRS // 2, 2, grid_space)

    waves = plane_waves()
    keep = jnp.where(jnp.abs(waves[0]) <= cut_x.astype(f32), 1.0, 0.0)

    def ahead_deep(plane):
        high, low = split(plane)
        return [high[:MP], low[:MP], high[MP:], low[MP:], high[:MP], high[MP:]]

    def emit_planes(ref, first_tile, first_k, modes, count, third):
        new = []
        for i in range(count):
            w = projected(waves, modes[MP * i : MP * (i + 1)], first_k + i)
            new.append([keep * part for part in w])
        if third:
            ref[0] = new[0][2]
        for j in range(0, count, 2):
            for i, tile in enumerate(pack_pair(new[j], new[j + 1])):
                ref[first_tile + 3 * (j // 2) + i] = tile

    def quad_tiles(q, pairs=2):
        return pl.ds(0, 7) if q == 0 else pl.ds(1 + 6 * q, 3 * pairs)

    base_copies = []
    for t in range(SIDE_QUADS):
        q = SIDE_QUADS * side + t
        deep = []
        for j in (0, 2):
            both_planes = left3(wy[at_y, 0], two_columns(wb, 4 * q + j), NN)
            for i in range(2):
                deep.append(cat(ahead_deep(both_planes[:, i * LANES : (i + 1) * LANES]), 1))
        modes = matmul(cat(deep, 0), xt[: 6 * LANES])
        emit_planes(base_send, 1 + 6 * t, 4 * q, modes, 4, t == 0)
        rows = quad_tiles(t)
        copy = remote(
            base_send.at[rows], base_recv.at[rows], base_send_sem.at[t], base_recv_sem.at[t],
            far,
        )
        copy.start()
        base_copies.append(copy)

    state_copies = []
    for q in range(STATE_QUADS):
        pairs = 2 if q < STATE_QUADS - 1 else 1
        deep = []
        for j in range(0, 2 * pairs, 2):
            both_planes = left3(wy[at_y, 0], two_columns(wa, 4 * q + j), NN)
            for i in range(2):
                k = 4 * q + j + i
                total = g[k] + both_planes[:, i * LANES : (i + 1) * LANES]
                deep.append(cat(ahead_deep(total) + ahead_deep(f[k]), 1))
        modes = matmul(cat(deep, 0), xt[...])
        emit_planes(state_send, 1 + 6 * q, 4 * q, modes, 2 * pairs, q == 0)
        rows = quad_tiles(q, pairs)
        copy = remote(
            state_send.at[rows], state_recv.at[rows], state_send_sem.at[q],
            state_recv_sem.at[q], far,
        )
        copy.start()
        state_copies.append(copy)

    def spectral(tiles, third, first_k, table_ref, work):
        deep = []
        wave_x, wave_y = waves
        for j in range(len(tiles) // 3):
            for i, (m0, m1) in enumerate(unpack_pair(tiles[3 * j : 3 * j + 3])):
                k = jnp.asarray(first_k + 2 * j + i, jnp.int32)
                inverse = 1.0 / jnp.maximum(k, 1).astype(f32)
                m2 = -(wave_x * m0 + wave_y * m1) * inverse
                if third is not None and j == 0 and i == 0:
                    m2 = jnp.where(k == 0, third, m2)
                high, low = split(cat([m0, m1, m2], 1))
                deep.append(cat([high, low, high], 1))
        rows = matmul(cat(deep, 0), table_ref[...])
        planes = []
        for i in range(len(deep)):
            mine = rows[MP * i : MP * (i + 1)]
            planes.append(cat([mine[:, :LANES], mine[:, LANES:]], 0))
        for j in range(0, len(deep), 2):
            out = left3(yb[0], cat(planes[j : j + 2], 1), NN)
            for i in range(2):
                work[column(first_k + j + i), :] = out[:, i * LANES : (i + 1) * LANES]

    span = base_sum.shape[0] // 2
    sum_copies = []
    for t in range(SIDE_QUADS):
        base_copies[t].wait_recv()
        for i in range(7 if t == 0 else 6):
            tile = i if t == 0 else 1 + 6 * t + i
            base_sum[span * side + tile] = base_send[tile] + base_recv[tile]
        start = 0 if t == 0 else 1 + 6 * t
        rows = pl.ds(span * side + start, 7 if t == 0 else 6)
        copy = remote(
            base_sum.at[rows], base_sum.at[rows], sum_send.at[t], sum_recv.at[t], twin
        )
        copy.start()
        sum_copies.append(copy)

    def base_back(place, t):
        first = span * place
        tiles = [base_sum[first + 1 + 6 * t + i] for i in range(6)]
        third = base_sum[first] if t == 0 else None
        spectral(tiles, third, 4 * (SIDE_QUADS * place + t), xb, w0)

    for t in range(SIDE_QUADS):
        base_back(side, t)
    for t in range(SIDE_QUADS):
        sum_copies[t].wait_recv()
        base_back(1 - side, t)

    for q in range(STATE_QUADS):
        state_copies[q].wait_recv()
        count = 6 if q < STATE_QUADS - 1 else 3
        both_tiles = lambda tile: state_send[tile] + state_recv[tile]
        tiles = [both_tiles(1 + 6 * q + i) for i in range(count)]
        spectral(tiles, both_tiles(0) if q == 0 else None, 4 * q, xs, wc)

    for copy in near_copies:
        copy.wait_recv()

    def finish_z(p):
        rows = left3(zb[0], cat([wc[pair_rows(p), :], w0[pair_rows(p), :]], 1), NN).T
        near = near_state[:, :, lanes(p)]
        out_state[:, :, lanes(p)] = rows[:96].reshape(near.shape) - near
        near = near_base[:, :, lanes(p)]
        out_base[:, :, lanes(p)] = rows[LANES : LANES + 48].reshape(near.shape) - near

    out_copies = []
    for i in range(4):
        loop(PAIRS // 4, 4, lambda p, i=i: finish_z(p + i * (PAIRS // 4)))
        for j, (src, dst) in enumerate(((out_state, state_gap_hbm), (out_base, base_gap_hbm))):
            copy = pltpu.make_async_copy(
                quarter_of(src, i), quarter_of(dst, i), out_sem.at[2 * i + j]
            )
            copy.start()
            out_copies.append(copy)

    sent = near_copies + share_copies + pass_copies + base_copies + sum_copies + state_copies
    for copy in sent:
        copy.wait_send()
    for copy in out_copies:
        copy.wait()


def fused_body(base, state, wavenumber, cutoff):
    base, state = base[0], state[0, 0]
    rows = base.shape[1]
    half = rows // lax.axis_size("comp")
    slabs = lax.axis_size("slab")
    tables = [
        z_tables(), y_tables(), filter_tables(slabs), ahead_tables(slabs), behind_tables(slabs),
        behind_tables(2 * slabs), y_back(), z_back(), force_table(),
    ]
    tables = [jnp.asarray(t) for t in tables]
    hbm = pl.BlockSpec(memory_space=pltpu.HBM)
    smem = pl.BlockSpec(memory_space=pltpu.SMEM)
    vmem = lambda *shape: pltpu.VMEM(shape, f32)
    dma = lambda count: pltpu.SemaphoreType.DMA((count,))
    held = lambda t: pltpu.VMEM(t.shape, t.dtype)
    held_one = lambda t: pltpu.VMEM(t.shape[1:], t.dtype)
    wz, wy, pd, xt, xs, xb, yb, zb, force = tables
    work = vmem(2 * N * KP, LANES)
    share = vmem(3 * SIDE_QUADS, 2 * MP, LANES)
    planes = vmem(QK, 2 * MP, LANES)
    base_tiles = vmem(1 + 6 * SIDE_QUADS, MP, LANES)
    state_tiles = vmem(4 + 6 * (STATE_QUADS - 1), MP, LANES)
    base_half = vmem(3, half, N * N)
    whole = vmem(3, rows, N * N)
    scratch = [
        whole, whole, base_half, whole, held(wz), held(wy), held_one(pd), held_one(xt),
        held_one(xs), held_one(xb), held(yb), held(zb), held(force),
        *[work] * 6, planes, share, share, share, planes, planes,
        base_tiles, base_tiles, vmem(2 + 12 * SIDE_QUADS, MP, LANES), state_tiles, state_tiles,
        base_half, whole,
        dma(14), dma(8), dma(2), dma(2), *[dma(SIDE_QUADS)] * 8, *[dma(STATE_QUADS)] * 2,
    ]
    base_gap, state_gap = pl.pallas_call(
        fused,
        out_shape=(
            jax.ShapeDtypeStruct((3, half, N * N), f32),
            jax.ShapeDtypeStruct((3, rows, N * N), f32),
        ),
        in_specs=[hbm, hbm, smem, smem, *[hbm] * len(tables)],
        out_specs=(hbm, hbm),
        scratch_shapes=scratch,
        compiler_params=pltpu.CompilerParams(
            vmem_limit_bytes=56 * 2**20, collective_id=0, has_side_effects=True
        ),
        cost_estimate=pl.CostEstimate(flops=10**10, bytes_accessed=10**7, transcendentals=0),
    )(base, state, cutoff, wavenumber, *tables)
    return base_gap[None], state_gap[None, None]


def solution(mesh):
    sizes = dict(mesh.shape)
    one_kernel = sizes["slab"] == 2 and sizes["comp"] == 2 and sizes["seg"] > 1
    return jax.shard_map(
        fused_body if one_kernel else body,
        mesh=mesh,
        in_specs=(
            P(("groups", "seg"), None, "slab", None),
            P(("groups", "seg"), "comp", None, "slab", None),
            P("groups"),
            P("groups"),
        ),
        out_specs=(
            P(("groups", "seg"), None, ("slab", "comp"), None),
            P(("groups", "seg"), "comp", None, "slab", None),
        ),
        check_vma=False,
    )
```

```python
import functools

import jax
import jax.numpy as jnp
import ml_dtypes
import numpy as np
from jax import lax
from jax.experimental import pallas as pl
from jax.experimental.pallas import tpu as pltpu
from jax.sharding import PartitionSpec as P

N = 64
BACK, GRID, AHEAD, SPEC, Z1, Z2, Z3, Y1 = 4, 4, 4, 4, 8, 4, 8, 6
THIRD = N // 3
LOW = THIRD - 3
KZ = THIRD + 1
KP = 24
MP = 48
PAIRS = N // 2
FLUX = 14 * 10**9
HALF = KZ // 2
viscosity = 0.025
time_step = 0.02
forcing_amp = 10.0
f32 = jnp.float32
bf16 = jnp.bfloat16

NN = (((1,), (0,)), ((), ()))
NT = (((1,), (1,)), ((), ()))


def split(value):
    high = value.astype(bf16)
    return high, (value - high.astype(f32)).astype(bf16)


def dot3(left, right, dims):
    dot = functools.partial(lax.dot_general, dimension_numbers=dims, preferred_element_type=f32)
    return dot(left[0], right[0]) + (dot(left[0], right[1]) + dot(left[1], right[0]))


def table(values):
    values = np.asarray(values, np.float32)
    high = values.astype(ml_dtypes.bfloat16)
    low = (values - high.astype(np.float32)).astype(ml_dtypes.bfloat16)
    return np.stack([high, low], axis=-3)


def table3(values):
    high, low = np.moveaxis(table(values), -3, 0)
    return np.concatenate([high, high, low], axis=-1)


def left3(left, value, dims):
    high, low = split(value)
    deep = jnp.concatenate([high, low, high], axis=dims[0][1][0])
    return lax.dot_general(left, deep, dimension_numbers=dims, preferred_element_type=f32)


def signed():
    m = np.arange(2 * THIRD + 1)
    return np.where(m <= THIRD, m, m - (2 * THIRD + 1))


def angles(first, second):
    return np.mod(np.outer(first, second), N) * (2 * np.pi / N)


def cuts():
    return range(LOW, THIRD + 1)


def z_tables():
    plain, ik = [], []
    k = np.arange(KZ)
    a = angles(k, np.arange(N))
    for cut in cuts():
        keep = 1.0 * (k <= cut)[:, None]
        w = np.zeros((2, KP, N))
        v = np.zeros((2, KP, N))
        w[0, :KZ], w[1, :KZ] = keep * np.cos(a), -keep * np.sin(a)
        v[0, :KZ], v[1, :KZ] = keep * k[:, None] * np.sin(a), keep * k[:, None] * np.cos(a)
        plain.append(np.kron(np.eye(2), w.reshape(2 * KP, N)))
        ik.append(np.kron(np.eye(2), v.reshape(2 * KP, N)))
    return table3(np.stack([np.stack(plain), np.stack(ik)], axis=1))


def y_tables():
    out = []
    m = signed()
    count = len(m)
    a = angles(m, np.arange(N))
    for cut in cuts():
        keep = 1.0 * (np.abs(m) <= cut)[:, None]
        c, s = keep * np.cos(a), keep * np.sin(a)
        w = np.zeros((2, MP, N, 2))
        w[0, :count, :, 0], w[0, :count, :, 1] = c, s
        w[1, :count, :, 0], w[1, :count, :, 1] = -s, c
        v = np.zeros_like(w)
        v[0, :count] = -m[:, None, None] * w[1, :count]
        v[1, :count] = m[:, None, None] * w[0, :count]
        out.append(np.stack([w.reshape(2 * MP, 2 * N), v.reshape(2 * MP, 2 * N)]))
    return table3(np.stack(out))


def y_back():
    m = signed()
    count = len(m)
    a = angles(np.arange(N), m)
    c, s = np.cos(a) / N, np.sin(a) / N
    w = np.zeros((N, 2, 2, MP))
    w[:, 0, 0, :count], w[:, 0, 1, :count] = c, -s
    w[:, 1, 0, :count], w[:, 1, 1, :count] = s, c
    v = np.zeros_like(w)
    v[:, :, 0, :count] = m * w[:, :, 1, :count]
    v[:, :, 1, :count] = -m * w[:, :, 0, :count]
    return table3(np.stack([w.reshape(2 * N, 2 * MP), v.reshape(2 * N, 2 * MP)]))


def z_back():
    k = np.arange(KZ)
    a = angles(k, np.arange(N))
    weight = (np.where(k == 0, 1.0, 2.0) / N)[:, None]
    w = np.zeros((2, KP, N))
    w[0, :KZ], w[1, :KZ] = weight * np.cos(a), -weight * np.sin(a)
    v = np.zeros_like(w)
    v[0, :KZ] = k[:, None] * w[1, :KZ]
    v[1, :KZ] = -k[:, None] * w[0, :KZ]
    pair = lambda t: np.kron(np.eye(2), t.reshape(2 * KP, N))
    return table3(np.stack([pair(w).T, pair(v).T]))


def x_filters(slabs):
    rows = N // slabs
    out = []
    x = np.arange(N)
    for cut in cuts():
        n = np.arange(-cut, cut + 1)
        d = np.mod(x[:, None] - x[None, :], N)
        phase = 2 * np.pi / N * n[:, None, None] * -d
        plain = np.cos(phase).sum(0) / N
        deriv = (-n[:, None, None] * np.sin(phase)).sum(0) / N
        both = np.stack([plain, deriv]).reshape(2, slabs, rows, slabs, rows)
        wide = np.zeros((slabs, 2, slabs, 3, rows, 3, rows))
        for i in range(3):
            wide[:, :, :, i, :, i, :] = both.transpose(3, 0, 1, 2, 4)
        out.append(wide.reshape(slabs, 2, slabs, 3 * rows, 3 * rows))
    return table(np.stack(out))


def x_tables(slabs):
    rows = N // slabs
    n = signed()
    count = len(n)
    a = angles(np.arange(N), n).reshape(slabs, rows, count)
    out = []
    for cut in cuts():
        keep = 1.0 * (np.abs(n) <= cut)
        c, s = np.cos(a) * keep, np.sin(a) * keep
        w = np.zeros((slabs, 2, 2, 3, rows, 3, 2, 64))
        for i in range(3):
            w[:, 0, 0, i, :, i, 0, :count] = c
            w[:, 0, 0, i, :, i, 1, :count] = -s
            w[:, 0, 1, i, :, i, 0, :count] = s
            w[:, 0, 1, i, :, i, 1, :count] = c
        w[:, 1, :, :, :, :, 0, :count] = -n * w[:, 0, :, :, :, :, 1, :count]
        w[:, 1, :, :, :, :, 1, :count] = n * w[:, 0, :, :, :, :, 0, :count]
        out.append(w.reshape(slabs, 2, 2, 3 * rows, 384))
    return table(np.stack(out))


def x_back(slabs):
    rows = N // slabs
    n = signed()
    count = len(n)
    a = angles(n, np.arange(N)).reshape(count, slabs, rows).transpose(1, 0, 2)
    c, s = np.cos(a) / N, np.sin(a) / N
    w = np.zeros((slabs, 2, 3, 2, 64, 3, rows))
    for i in range(3):
        w[:, 0, i, 0, :count, i] = c
        w[:, 0, i, 1, :count, i] = -s
        w[:, 1, i, 0, :count, i] = s
        w[:, 1, i, 1, :count, i] = c
    return table(w.reshape(slabs, 2, 384, 3 * rows))


def both(ref, *index):
    return ref[(*index, 0)], ref[(*index, 1)]


def lanes(p):
    return pl.ds(pl.multiple_of(p * 128, 128), 128)


def pair_rows(p):
    return pl.ds(pl.multiple_of(p * 4 * KP, 8), 4 * KP)


def column(k):
    return pl.ds(k, 2 * N, stride=KP)


def flat(block):
    return block.reshape(block.shape[0] * block.shape[1], block.shape[2])


def loop(count, unroll, step):
    def go(i, carry):
        step(i)
        return carry

    lax.fori_loop(0, count, go, 0, unroll=unroll)


def clear_padding(*works):
    for k in range(KZ, KP):
        for work in works:
            work[column(k), :] = jnp.zeros((2 * N, work.shape[1]), f32)


def base_ahead(base_ref, wz_ref, wy_ref, out_ref, half_ref, work):
    def along_z(p):
        work[pair_rows(p), :] = left3(wz_ref[0], flat(base_ref[:, :, lanes(p)]), NT)

    loop(PAIRS, Z1, along_z)

    def along_y(k):
        out_ref[k] = left3(wy_ref[0], work[column(k), :], NN)

    loop(KZ, Y1, along_y)
    first = HALF * lax.axis_index("comp")

    def share(j):
        half_ref[j] = out_ref[first + j]

    loop(HALF, 1, share)


def sign_step():
    return jnp.where(lax.axis_index("comp") == 0, -time_step, time_step).astype(f32)


def flux_ahead(base_ref, state_ref, wz_ref, wy_ref, g_ref, work_a, work_b):
    scale = sign_step()

    def along_z(p):
        state = state_ref[:, :, lanes(p)]
        scaled = state * scale
        f1, f2 = (flat(scaled * base_ref[j, :, lanes(p)][None]) for j in (1, 2))
        plain = wz_ref[0]
        work_a[pair_rows(p), :] = left3(plain, flat(state), NT) + left3(wz_ref[1], f2, NT)
        work_b[pair_rows(p), :] = left3(plain, f1, NT)

    loop(PAIRS, Z2, along_z)

    def along_y(k):
        g_ref[k] = left3(wy_ref[0], work_a[column(k), :], NN) + left3(
            wy_ref[1], work_b[column(k), :], NN
        )

    loop(KZ, Y1, along_y)


def flux_x_ahead(base_ref, state_ref, wz_ref, wy_ref, f_ref, work):
    scale = sign_step()

    def along_z(p):
        f0 = flat(state_ref[:, :, lanes(p)] * scale * base_ref[0, :, lanes(p)][None])
        work[pair_rows(p), :] = left3(wz_ref[0], f0, NT)

    loop(PAIRS, Z2, along_z)

    def along_y(k):
        f_ref[k] = left3(wy_ref[0], work[column(k), :], NN)

    loop(KZ, Y1, along_y)


def gradients(
    slabs, count, *refs,
):
    got, rest = refs[:count], refs[count:]
    side = lax.axis_index("comp")
    if count == 1:
        visits = [(lambda j: (j, [got[0][s, j] for s in range(slabs)]), KZ)]
    else:
        own, mine, partner = got

        def visit(ref, first):
            return lambda j: (first + j, [own[first + j], ref[j]])

        visits = [
            (visit(mine, HALF * side), HALF),
            (visit(partner, HALF * (1 - side)), HALF),
        ]
    gradients_of(slabs, visits, *rest)


def gradients_of(
    slabs, visits, base_ref, state_ref, force_ref, pd_ref, yb_ref, zb_ref, wz_ref, wy_ref,
    xt_ref, base_out_ref, coupled_ref, work_0, work_1, work_2,
):
    tangent = lax.axis_index("comp") == 0

    def back_y(visit, j):
        k, sources = visit(j)
        sources = [split(source) for source in sources]

        def across(kind):
            total = dot3(sources[0], both(pd_ref, kind, 0), NN)
            for s in range(1, slabs):
                total = total + dot3(sources[s], both(pd_ref, kind, s), NN)
            return total

        plain, deriv = across(0), across(1)
        work_0[column(k), :] = left3(yb_ref[0], deriv, NN)
        work_1[column(k), :] = left3(yb_ref[1], plain, NN)
        work_2[column(k), :] = left3(yb_ref[0], plain, NN)

    clear_padding(work_0, work_1, work_2)
    for visit, count in visits:
        loop(count, BACK, functools.partial(back_y, visit))

    def grid_space(p):
        state = state_ref[:, :, lanes(p)]
        base = base_ref[:, :, lanes(p)]
        grad = []
        for work, kind in ((work_0, 0), (work_1, 0), (work_2, 1)):
            rows = left3(zb_ref[kind], work[pair_rows(p), :], NN).T
            grad.append(rows.reshape(base.shape))
        coupled, driven = [], []
        for i in range(3):
            total = 0.0
            drive = 0.0
            for j in range(3):
                total = total + jnp.where(tangent, grad[j][i], grad[i][j]) * state[j]
                drive = drive + grad[j][i] * base[j]
            if i == 0:
                drive = drive - force_ref[:, lanes(p)]
            coupled.append(-time_step * total)
            driven.append(base[i] - time_step * drive)
        plain = wz_ref[0]
        coupled_ref[pair_rows(p), :] = left3(plain, jnp.concatenate(coupled, axis=0), NT)
        work_1[pair_rows(p), :] = left3(plain, jnp.concatenate(driven, axis=0), NT)

    loop(PAIRS, GRID, grid_space)

    waves = plane_waves()
    first = HALF * lax.axis_index("comp")

    def base_ahead_x(step):
        j = HALF - 1 - step
        k = first + j
        driven = left3(wy_ref[0], work_1[column(k), :], NN)
        modes = 0.0
        for d in range(2):
            rows = slice(d * MP, (d + 1) * MP)
            modes = modes + dot3(split(driven[rows]), both(xt_ref, 0, d), NN)
        emit(waves, base_out_ref, j, HALF, modes, k)

    loop(HALF, AHEAD, base_ahead_x)


def emit(waves, ref, slot, last, modes, k):
    new = projected(waves, modes, k)
    ref[slot] = jnp.concatenate(new[:2], axis=1)
    ref[last] = jnp.concatenate([new[2], jnp.zeros_like(new[2])], axis=1)


def state_ahead_x(coupled_ref, wy_ref, xt_ref, g_ref, f_ref, out_ref):
    waves = plane_waves()

    def ahead_x(step):
        k = KZ - 1 - step
        total = g_ref[k] + left3(wy_ref[0], coupled_ref[column(k), :], NN)
        outer = f_ref[k]
        modes = 0.0
        for d in range(2):
            rows = slice(d * MP, (d + 1) * MP)
            modes = modes + dot3(split(total[rows]), both(xt_ref, 0, d), NN)
            modes = modes + dot3(split(outer[rows]), both(xt_ref, 1, d), NN)
        emit(waves, out_ref, k, KZ, modes, k)

    loop(KZ, AHEAD, ahead_x)


def plane_waves():
    column_n = lax.rem(lax.broadcasted_iota(jnp.int32, (MP, 128), 1), 64)
    row_m = lax.broadcasted_iota(jnp.int32, (MP, 128), 0)
    wrap = lambda v: jnp.where(v <= THIRD, v, v - (2 * THIRD + 1)).astype(f32)
    return wrap(column_n), wrap(row_m)


def projected(waves, modes, k):
    wave_x, wave_y = waves
    wave_z = jnp.asarray(k, jnp.int32).astype(f32)
    square = wave_x * wave_x + wave_y * wave_y + wave_z * wave_z
    safe = jnp.where(square > 0, square, 1.0)
    damping = 1.0 / (1.0 + viscosity * time_step * square)
    w = [modes[:, i * 128 : (i + 1) * 128] for i in range(3)]
    divergence = (wave_x * w[0] + wave_y * w[1] + wave_z * w[2]) / safe
    return [
        damping * (w[0] - wave_x * divergence),
        damping * (w[1] - wave_y * divergence),
        damping * (w[2] - wave_z * divergence),
    ]


def finish(count, halved, *refs):
    parts, (near_ref, xb_ref, yb_ref, zb_ref, out_ref, work) = refs[:count], refs[count:]
    wave_x, wave_y = plane_waves()
    clear_padding(work)

    def spectral(parts, first, last, j):
        k = first + j
        modes, third = 0.0, 0.0
        for part in parts:
            modes = modes + part[j]
            third = third + part[last, :, :128]
        w0, w1 = modes[:, :128], modes[:, 128:]
        whole = jnp.asarray(k, jnp.int32)
        inverse = 1.0 / jnp.maximum(whole, 1).astype(f32)
        w2 = jnp.where(whole == 0, third, -(wave_x * w0 + wave_y * w1) * inverse)
        new = split(jnp.concatenate([w0, w1, w2], axis=1))
        rows = [dot3(new, both(xb_ref, d), NN) for d in range(2)]
        work[column(k), :] = left3(yb_ref[0], jnp.concatenate(rows, axis=0), NN)

    if halved:
        side = lax.axis_index("comp")
        for part, place in zip(parts, (side, 1 - side)):
            loop(HALF, SPEC, functools.partial(spectral, [part], HALF * place, HALF))
    else:
        loop(KZ, SPEC, functools.partial(spectral, parts, 0, KZ))

    def along_z(p):
        rows = left3(zb_ref[0], work[pair_rows(p), :], NN).T
        near = near_ref[:, :, lanes(p)]
        out_ref[:, :, lanes(p)] = rows.reshape(near.shape) - near

    loop(PAIRS, Z3, along_z)


def call(kernel, out_shape, scratch, cost, *operands):
    return pl.pallas_call(
        kernel,
        out_shape=out_shape,
        in_specs=[pl.BlockSpec(memory_space=pltpu.VMEM)] * len(operands),
        out_specs=jax.tree.map(lambda _: pl.BlockSpec(memory_space=pltpu.VMEM), out_shape),
        scratch_shapes=scratch,
        compiler_params=pltpu.CompilerParams(vmem_limit_bytes=48 * 2**20),
        cost_estimate=pl.CostEstimate(flops=cost, bytes_accessed=2**10, transcendentals=0),
    )(*operands)


def body(base, state, wavenumber, cutoff):
    base, state = base[0], state[0, 0]
    slab_rows = base.shape[1]
    half = slab_rows // lax.axis_size("comp")
    slabs = lax.axis_size("slab")
    segs = lax.axis_size("seg")
    slab = lax.axis_index("slab")
    side = lax.axis_index("comp")
    width = 3 * slab_rows
    which = cutoff - LOW

    route = [((s, 0), ((s - 1) % segs, 0)) for s in range(segs)]
    route += [((s, 1), ((s + 1) % segs, 1)) for s in range(segs)]
    route = [(a * 2 + b, c * 2 + d) for (a, b), (c, d) in route]
    wz = lax.dynamic_index_in_dim(jnp.asarray(z_tables()), which[2], 0, False)
    wy = lax.dynamic_index_in_dim(jnp.asarray(y_tables()), which[1], 0, False)
    filters, ahead = jnp.asarray(x_filters(slabs)), jnp.asarray(x_tables(slabs))
    pick = lambda t: lax.dynamic_slice(
        t, (which[0], slab) + (0,) * (t.ndim - 2), (1, 1) + t.shape[2:]
    )[0, 0]
    pd, xt = pick(filters), pick(ahead)
    xb = lax.dynamic_index_in_dim(jnp.asarray(x_back(slabs)), slab, 0, False)
    yb, zb = jnp.asarray(y_back()), jnp.asarray(z_back())

    modes = jax.ShapeDtypeStruct((KZ, 2 * MP, width), f32)
    half_modes = jax.ShapeDtypeStruct((HALF, 2 * MP, width), f32)
    spectrum = jax.ShapeDtypeStruct((KZ + 1, MP, 256), f32)
    half_spectrum = jax.ShapeDtypeStruct((HALF + 1, MP, 256), f32)
    work = pltpu.VMEM((2 * N * KP, width), f32)
    own, share = call(base_ahead, (modes, half_modes), [work], 4 * 10**9, base, wz, wy)
    later, later_base, share = lax.optimization_barrier((state, base, share))
    near_state = lax.ppermute(later, ("seg", "comp"), route)
    base_half = lax.dynamic_slice_in_dim(later_base, side * half, half, 1)
    near_base = lax.ppermute(base_half, "seg", [((s + 1) % segs, s) for s in range(segs)])
    if slabs == 2:
        other = lax.ppermute(share, "slab", [(0, 1), (1, 0)])
        partner = lax.ppermute(other, "comp", [(0, 1), (1, 0)])
        first = slab == 0
        got = (own, other, partner)
        pd = jnp.where(first, pd, pd[:, ::-1])
    else:
        got = (lax.all_gather(own, "slab"),)
    g = call(flux_ahead, modes, [work] * 2, FLUX, base, state, wz, wy)
    f = call(flux_x_ahead, modes, [work], 10**9, base, state, wz, wy)

    *got, g, f = lax.optimization_barrier((*got, g, f))

    y = jnp.arange(N, dtype=jnp.int32)
    phase = jnp.mod(wavenumber[0] * y, N).astype(f32) * (2.0 * jnp.pi / N)
    force = jnp.repeat(forcing_amp * jnp.sin(phase), N)[None]
    lined = jax.ShapeDtypeStruct((2 * N * KP, width), f32)
    base_modes, coupled = call(
        functools.partial(gradients, slabs, len(got)), (half_spectrum, lined), [work] * 3,
        25 * 10**9, *got, base, state, force, pd, yb, zb, wz, wy, xt,
    )
    state_modes = call(state_ahead_x, spectrum, [], 3 * 10**9, coupled, wy, xt, g, f)
    near_state, near_base, state_modes = lax.optimization_barrier(
        (near_state, near_base, state_modes)
    )
    if slabs == 2:
        swap = lambda v: lax.ppermute(v, "slab", [(0, 1), (1, 0)])
        state_other = swap(state_modes)
        base_other, state_modes = lax.optimization_barrier((swap(base_modes), state_modes))
        base_sum = base_modes + base_other
        state_parts = (state_modes, state_other)
    else:
        base_sum = lax.psum(base_modes, "slab")
        state_parts = (lax.psum(state_modes, "slab"),)
    base_parts = (base_sum, lax.ppermute(base_sum, "comp", [(0, 1), (1, 0)]))

    shape = jax.ShapeDtypeStruct(base.shape, f32)
    last = functools.partial(finish, len(state_parts), False)
    last_base = functools.partial(finish, 2, True)
    near_wide = jnp.concatenate([near_base, near_base], axis=1)
    base_gap = call(last_base, shape, [work], 10**8, *base_parts, near_wide, xb, yb, zb)
    base_gap = lax.dynamic_slice_in_dim(base_gap, side * half, half, 1)
    state_gap = call(last, shape, [work], 10**10, *state_parts, near_state, xb, yb, zb)
    return base_gap[None], state_gap[None, None]


LANES = 128
QK = 24
SIDE_QUADS = 3
STATE_QUADS = 6
FLUX_FIRST = 8


def lane_pad(values, axis, size=LANES):
    pad = [(0, 0)] * values.ndim
    pad[axis] = (0, size - values.shape[axis])
    return np.pad(values, pad)


def halves(values):
    values = np.asarray(values, np.float32)
    high = values.astype(ml_dtypes.bfloat16)
    return high, (values - high.astype(np.float32)).astype(ml_dtypes.bfloat16)


def filter_tables(slabs):
    rows = N // slabs
    x = np.arange(N)
    out = []
    for cut in cuts():
        n = np.arange(-cut, cut + 1)
        d = np.mod(x[:, None] - x[None, :], N)
        phase = 2 * np.pi / N * n[:, None, None] * -d
        plain = np.cos(phase).sum(0) / N
        deriv = (-n[:, None, None] * np.sin(phase)).sum(0) / N
        both_kinds = np.stack([plain, deriv]).reshape(2, slabs, rows, slabs, rows)
        per_slab = []
        for slab in range(slabs):
            blocks = []
            for source in (slab, 1 - slab):
                wide = np.zeros((3, rows, 2, LANES))
                for i in range(3):
                    wide[i, :, :, i * rows : (i + 1) * rows] = both_kinds[
                        :, source, :, slab
                    ].transpose(1, 0, 2)
                blocks.append(halves(lane_pad(wide.reshape(3 * rows, 2 * LANES), 0)))
            (own_high, own_low), (far_high, far_low) = blocks
            per_slab.append(
                np.concatenate([own_high, own_high, far_high, far_high, own_low, far_low])
            )
        out.append(np.stack(per_slab))
    return np.stack(out, axis=1)


def ahead_tables(slabs):
    rows = N // slabs
    n = signed()
    count = len(n)
    a = angles(np.arange(N), n).reshape(slabs, rows, count)
    c, s = np.cos(a), np.sin(a)
    w = np.zeros((slabs, 2, 2, 3, rows, 3, 2, 64))
    for i in range(3):
        w[:, 0, 0, i, :, i, 0, :count] = c
        w[:, 0, 0, i, :, i, 1, :count] = -s
        w[:, 0, 1, i, :, i, 0, :count] = s
        w[:, 0, 1, i, :, i, 1, :count] = c
    w[:, 1, :, :, :, :, 0, :count] = -n * w[:, 0, :, :, :, :, 1, :count]
    w[:, 1, :, :, :, :, 1, :count] = n * w[:, 0, :, :, :, :, 0, :count]
    high, low = halves(lane_pad(w.reshape(slabs, 2, 2, 3 * rows, 3 * LANES), 3))
    blocks = []
    for kind in range(2):
        h, l = high[:, kind], low[:, kind]
        blocks += [h[:, 0], h[:, 0], h[:, 1], h[:, 1], l[:, 0], l[:, 1]]
    return np.concatenate(blocks, axis=1)


def behind_tables(parts):
    rows = N // parts
    n = signed()
    count = len(n)
    a = angles(n, np.arange(N)).reshape(count, parts, rows).transpose(1, 0, 2)
    c, s = np.cos(a) / N, np.sin(a) / N
    w = np.zeros((parts, 3, 2, 64, 2, LANES))
    for i in range(3):
        place = slice(i * rows, (i + 1) * rows)
        w[:, i, 0, :count, 0, place] = c
        w[:, i, 1, :count, 0, place] = -s
        w[:, i, 0, :count, 1, place] = s
        w[:, i, 1, :count, 1, place] = c
    high, low = halves(w.reshape(parts, 3 * LANES, 2 * LANES))
    return np.concatenate([high, high, low], axis=1)


def table_groups():
    blocks = lambda t, height: t.reshape(-1, height, t.shape[-1])
    wide = [z_tables(), y_tables()]
    wide += [lane_pad(lane_pad(t, 1, 4 * MP), 2, 3 * LANES) for t in (y_back(), z_back())]
    wide.append(ahead_tables(2))
    narrow = [filter_tables(2), behind_tables(2), behind_tables(4)]
    return [blocks(t, 2 * MP) for t in wide], [blocks(t, 3 * LANES) for t in narrow]


def table_places():
    counts = (1, 1, 1, 1, 2), (2, 2, 4)
    places = []
    for group, shares in zip(table_groups(), counts):
        start, entries = 0, []
        for t, share in zip(group, shares):
            entries.append((start, len(t) // share))
            start += len(t)
        places.append(entries)
    return places


def quarter_sine(position):
    folded = lax.rem(position, N // 2)
    folded = jnp.minimum(folded, N // 2 - folded)
    angle = folded.astype(f32) * (2.0 * np.pi / N)
    square = angle * angle
    series = 1.0
    for order in (12, 10, 8, 6, 4, 2):
        series = 1.0 - series * square * (1.0 / (order * (order + 1)))
    return jnp.where(position < N // 2, 1.0, -1.0) * angle * series


def cat(values, axis):
    return jnp.concatenate(values, axis=axis)


def wide_rows(*fields):
    blank = jnp.zeros((LANES - fields[0].shape[0], LANES), f32)
    return cat([part for field in fields for part in (field, blank)], 0)


def matmul(left, right):
    return lax.dot_general(left, right, NN, preferred_element_type=f32)


def half_lane(shape):
    return lax.rem(lax.broadcasted_iota(jnp.int32, shape, 1), 64)


def turn(value, shift):
    return pltpu.roll(value, shift % LANES, 1)


GAP = 2 * THIRD + 1
STEP = 64 - GAP
PIECES = (GAP, GAP - STEP, GAP - 2 * STEP)
BODY = 40
PAIR_ROWS = 3 * BODY + 16
QUAD_ROWS = PAIR_ROWS + 3 * BODY + 8


def pack_pair(first, second):
    gap = half_lane(first[0].shape) >= GAP
    carried = (first[0], second[0], first[1])
    return [jnp.where(gap, turn(second[1], by), held) for by, held in zip(PIECES, carried)]


def unpack_pair(tiles):
    lane = half_lane(tiles[0].shape)
    last = turn(tiles[2], -PIECES[2])
    last = jnp.where(lane < 2 * STEP, turn(tiles[1], -PIECES[1]), last)
    last = jnp.where(lane < STEP, turn(tiles[0], -PIECES[0]), last)
    return (tiles[0], tiles[2]), (tiles[1], last)


def tails(first, second):
    low = lax.broadcasted_iota(jnp.int32, first.shape, 0) < 4
    return jnp.where(low, first, pltpu.roll(second, 4, 0))


def squeeze(tile):
    return cat([tile[:BODY], tile[MP : MP + BODY], tails(tile[BODY:MP], tile[MP + BODY :])], 0)


def unsqueeze(held):
    tail = held[2 * BODY :]
    return cat([held[:BODY], tail, held[BODY : 2 * BODY], pltpu.roll(tail, 4, 0)], 0)


def pack_quad(tiles):
    body = [tile[:BODY] for tile in tiles]
    tail = [tile[BODY:] for tile in tiles]
    if len(tiles) == 3:
        return cat([*body, tails(tail[0], tail[1]), tail[2]], 0)
    return cat(
        [
            *body[:3], tails(tail[0], tail[1]), tails(tail[2], tail[5]),
            *body[3:], tails(tail[3], tail[4]),
        ],
        0,
    )


def unpack_quad(held):
    part = lambda start, size: held[start : start + size]
    body = [part(BODY * i, BODY) for i in range(3)]
    first, second = part(3 * BODY, 8), part(3 * BODY + 8, 8)
    tail = [first, pltpu.roll(first, 4, 0), second]
    if held.shape[0] > PAIR_ROWS:
        body += [part(PAIR_ROWS + BODY * i, BODY) for i in range(3)]
        last = part(PAIR_ROWS + 3 * BODY, 8)
        tail += [last, pltpu.roll(last, 4, 0), pltpu.roll(second, 4, 0)]
    return [cat([b, t], 0) for b, t in zip(body, tail)]


def pack_share(planes):
    lane = lax.broadcasted_iota(jnp.int32, planes[0].shape, 1)
    tiles = [jnp.where(lane < 96, planes[i], turn(planes[3], 96 - 32 * i)) for i in range(3)]
    return [squeeze(tile) for tile in tiles]


def unpack_share(held):
    tiles = [unsqueeze(part) for part in held]
    lane = lax.broadcasted_iota(jnp.int32, tiles[0].shape, 1)
    last = jnp.where(lane < 64, turn(tiles[1], 64), turn(tiles[2], 96))
    return [*tiles, jnp.where(lane < 32, turn(tiles[0], 32), last)]


def two_columns(work, k):
    return cat([work[column(k), :], work[column(k + 1), :]], 1)


def fused(
    base_hbm, state_hbm, cutoff_ref, wave_ref, wide_hbm, narrow_hbm, out_base, out_state,
    base_v, state_v, near_base, near_state, wz_v, wy_v, pd_v, xt, xs, xb, yb_v, zb_v,
    w0, w1, w2, wa, wb, wc, wd, held_coupled, own, share, other, partner, g, f,
    base_send, base_recv, base_sum, state_send, state_recv, local_sem, near_send, near_recv, share_send, share_recv, pass_send, pass_recv,
    base_send_sem, base_recv_sem, sum_send, sum_recv, state_send_sem, state_recv_sem,
):
    side = lax.axis_index("comp")
    slab = lax.axis_index("slab")
    seg = lax.axis_index("seg")
    segs = lax.axis_size("seg")
    far = {"slab": 1 - slab}
    twin = {"comp": 1 - side}
    after, before = lax.rem(seg + 1, segs), lax.rem(seg + segs - 1, segs)
    half = near_base.shape[1]
    quarter = N * N // 4

    def local(index, src, dst):
        return pltpu.make_async_copy(src, dst, local_sem.at[index])

    def remote(src, dst, send, recv, device):
        return pltpu.make_async_remote_copy(
            src_ref=src, dst_ref=dst, send_sem=send, recv_sem=recv, device_id=device,
            device_id_type=pl.DeviceIdType.MESH,
        )

    barrier = pltpu.get_barrier_semaphore()
    for device in (far, twin, {"seg": after}, {"seg": before}):
        pl.semaphore_signal(
            barrier, inc=1, device_id=device, device_id_type=pl.DeviceIdType.MESH
        )

    def quarter_of(ref, i):
        return ref.at[:, :, pl.ds(i * quarter, quarter)]

    wide_places, narrow_places = table_places()

    def table_part(hbm, entry, index, dst):
        start, rows = entry
        return hbm.at[pl.ds(start + rows * index, rows)], dst

    wz_copy = local(0, *table_part(wide_hbm, wide_places[0], 0, wz_v))
    base_copies = [
        local(1 + i, quarter_of(base_hbm, i), quarter_of(base_v, i)) for i in range(4)
    ]
    wy_copy = local(5, *table_part(wide_hbm, wide_places[1], 0, wy_v))
    state_copy = local(6, state_hbm, state_v)
    late_copies = [
        local(7, *table_part(narrow_hbm, narrow_places[0], slab, pd_v)),
        local(8, *table_part(wide_hbm, wide_places[2], 0, yb_v)),
        local(9, *table_part(wide_hbm, wide_places[3], 0, zb_v)),
        local(10, *table_part(wide_hbm, wide_places[4], slab, xt)),
        local(11, *table_part(narrow_hbm, narrow_places[1], slab, xs)),
        local(12, *table_part(narrow_hbm, narrow_places[2], 2 * slab + side, xb)),
    ]
    for copy in (wz_copy, *base_copies, wy_copy, state_copy):
        copy.start()

    cut_x, cut_y, cut_z = (cutoff_ref[i] for i in range(3))
    at_x, at_y, at_z = (jnp.clip(cut - LOW, 0, THIRD - LOW) for cut in (cut_x, cut_y, cut_z))

    def back_table(ref, kind, depth):
        return ref[2 * kind : 2 * kind + 2].reshape(4 * MP, 3 * LANES)[: 2 * N, :depth]

    wz = lambda kind: wz_v[2 * at_z + kind]
    wy = lambda kind: wy_v[2 * at_y + kind]
    yb = lambda kind: back_table(yb_v, kind, 6 * MP)
    zb = lambda kind: back_table(zb_v, kind, 12 * KP)

    def base_ahead_z(p):
        w0[pair_rows(p), :] = left3(wz(0), wide_rows(flat(base_v[:, :, lanes(p)])), NT)

    wz_copy.wait()
    for i, copy in enumerate(base_copies):
        copy.wait()
        loop(PAIRS // 4, Z1, lambda p, i=i: base_ahead_z(p + i * (PAIRS // 4)))
    for copy in late_copies:
        copy.start()
    wy_copy.wait()

    def base_planes(q):
        planes = []
        for j in (0, 2):
            both_planes = left3(wy(0), two_columns(w0, 4 * q + j), NN)
            planes += [both_planes[:, :LANES], both_planes[:, LANES:]]
        for i in range(4):
            own[4 * q + i] = planes[i]
        return planes

    near_copies = [
        remote(
            state_hbm, near_state, near_send.at[0], near_recv.at[0],
            {"seg": jnp.where(side == 0, before, after)},
        ),
        remote(
            base_hbm.at[:, pl.ds(half * side, half), :], near_base, near_send.at[1],
            near_recv.at[1], {"seg": before},
        ),
    ]
    share_copies = []
    for t in range(SIDE_QUADS):
        for i, tile in enumerate(pack_share(base_planes(SIDE_QUADS * side + t))):
            share[3 * t + i] = tile
        if t == 0:
            pl.semaphore_wait(barrier, 4)
            for copy in near_copies:
                copy.start()
        rows = pl.ds(3 * t, 3)
        copy = remote(
            share.at[rows], other.at[rows], share_send.at[t], share_recv.at[t], far
        )
        copy.start()
        share_copies.append(copy)
    for t in range(SIDE_QUADS):
        base_planes(SIDE_QUADS * (1 - side) + t)

    pass_copies = []

    def pass_on(t):
        share_copies[t].wait_recv()
        rows = pl.ds(3 * t, 3)
        copy = remote(
            other.at[rows], partner.at[rows], pass_send.at[t], pass_recv.at[t], twin
        )
        copy.start()
        pass_copies.append(copy)

    state_copy.wait()
    scale = sign_step()

    def flux_z(t):
        first, second = [], []
        for i in range(2):
            p = 2 * t + i
            state = state_v[:, :, lanes(p)]
            scaled = state * scale
            f0, f1, f2 = (flat(scaled * base_v[j, :, lanes(p)][None]) for j in range(3))
            plain = left3(wz(0), wide_rows(flat(state), f0), NT)
            wa[pair_rows(p), :] = plain[:, :LANES]
            wc[pair_rows(p), :] = plain[:, LANES:]
            first.append(f1)
            second.append(f2)
        along_y = left3(wz(0), wide_rows(*first), NT)
        along_z = left3(wz(1), wide_rows(*second), NT)
        for i in range(2):
            p = 2 * t + i
            mine = slice(i * LANES, (i + 1) * LANES)
            wb[pair_rows(p), :] = along_y[:, mine]
            wa[pair_rows(p), :] += along_z[:, mine]

    for copy in late_copies:
        copy.wait()

    def back_y(ref, place, t):
        q = SIDE_QUADS * place + t
        planes = unpack_share([ref[3 * t + i] for i in range(3)])
        deep = []
        for i in range(4):
            own_high, own_low = split(own[4 * q + i])
            far_high, far_low = split(planes[i])
            deep.append(cat([own_high, own_low, far_high, far_low, own_high, far_high], 1))
        filtered = matmul(cat(deep, 0), cat([pd_v[2 * at_x], pd_v[2 * at_x + 1]], 0))
        kinds = [filtered[96 * i : 96 * (i + 1)] for i in range(4)]
        for j in (0, 2):
            along = left3(yb(1), cat([kinds[j][:, :LANES], kinds[j + 1][:, :LANES]], 1), NN)
            for i in range(2):
                k = 4 * q + j + i
                whole = left3(yb(0), kinds[j + i], NN)
                w2[column(k), :] = whole[:, :LANES]
                w0[column(k), :] = whole[:, LANES:]
                w1[column(k), :] = along[:, i * LANES : (i + 1) * LANES]

    loop(FLUX_FIRST, 4, flux_z)
    pass_on(0)
    back_y(other, side, 0)
    loop(PAIRS // 2 - FLUX_FIRST, 4, lambda t: flux_z(t + FLUX_FIRST))
    pass_on(1)
    back_y(other, side, 1)
    pass_copies[0].wait_recv()
    back_y(partner, 1 - side, 0)
    pass_on(2)
    back_y(other, side, 2)
    for t in (1, 2):
        pass_copies[t].wait_recv()
        back_y(partner, 1 - side, t)

    tangent = side == 0
    wave = wave_ref[0]

    def force(p):
        lane = lax.broadcasted_iota(jnp.int32, (1, LANES), 1)
        y = 2 * p + jnp.where(lane < 64, 0, 1)
        return forcing_amp * quarter_sine(lax.rem(wave * y, N))

    def grid_space(t):
        third = left3(
            zb(1), cat([w2[pair_rows(2 * t + i), :] for i in range(2)], 1), NN
        ).T
        driven_pair = []
        for i in range(2):
            p = 2 * t + i
            state = state_v[:, :, lanes(p)]
            base = base_v[:, :, lanes(p)]
            pair = left3(zb(0), cat([w0[pair_rows(p), :], w1[pair_rows(p), :]], 1), NN).T
            grad = [
                pair[:96].reshape(base.shape),
                pair[LANES : LANES + 96].reshape(base.shape),
                third[i * LANES : i * LANES + 96].reshape(base.shape),
            ]
            coupled, driven = [], []
            for a in range(3):
                total = 0.0
                drive = 0.0
                for b in range(3):
                    total = total + jnp.where(tangent, grad[b][a], grad[a][b]) * state[b]
                    drive = drive + grad[b][a] * base[b]
                if a == 0:
                    drive = drive - force(p)
                coupled.append(-time_step * total)
                driven.append(base[a] - time_step * drive)
            held_coupled[:, lanes(p)] = cat(coupled, 0)
            driven_pair.append(cat(driven, 0))
        out = left3(wz(0), wide_rows(*driven_pair), NT)
        for i in range(2):
            wd[pair_rows(2 * t + i), :] = out[:, i * LANES : (i + 1) * LANES]

    loop(PAIRS // 2, 4, grid_space)

    waves = plane_waves()
    keep = jnp.where(jnp.abs(waves[0]) <= cut_x.astype(f32), 1.0, 0.0)

    def ahead_deep(plane):
        high, low = split(plane)
        return [high[:MP], low[:MP], high[MP:], low[MP:], high[:MP], high[MP:]]

    row = lax.broadcasted_iota(jnp.int32, (MP, LANES), 0)
    upper = row > THIRD
    folded = jnp.where(upper, 0.0, jnp.where(row == 0, 1.0, 2.0))

    def emit_planes(ref, start, first_k, modes, count, fold):
        new = []
        for i in range(count):
            w = projected(waves, modes[MP * i : MP * (i + 1)], first_k + i)
            new.append([keep * part for part in w])
        if fold is not None:
            held = jnp.where(upper, pltpu.roll(new[0][2], THIRD + 1, 0), new[0][0])
            new[0][0] = jnp.where(fold, held, new[0][0])
        tiles = []
        for j in range(0, count, 2):
            tiles += pack_pair(new[j], new[j + 1])
        rows = QUAD_ROWS if count == 4 else PAIR_ROWS
        ref[start : start + rows, :] = pack_quad(tiles)

    def base_copy(t, rows):
        rows = pl.ds(QUAD_ROWS * t, rows)
        return remote(
            base_send.at[rows], base_recv.at[rows], base_send_sem.at[t], base_recv_sem.at[t],
            far,
        )

    def each_side(copies, act):
        if len(copies) == 1:
            act(copies[0])
        else:
            pl.when(side == 0)(lambda: act(copies[0]))
            pl.when(side == 1)(lambda: act(copies[1]))

    base_copies = []
    for t in range(SIDE_QUADS):
        q = SIDE_QUADS * side + t
        deep = []
        for j in (0, 2):
            both_planes = left3(wy(0), two_columns(wd, 4 * q + j), NN)
            for i in range(2):
                deep.append(cat(ahead_deep(both_planes[:, i * LANES : (i + 1) * LANES]), 1))
        modes = matmul(cat(deep, 0), flat(xt[:8]))
        emit_planes(base_send, QUAD_ROWS * t, 4 * q, modes, 4, side == 0 if t == 0 else None)
        copies = [base_copy(t, QUAD_ROWS)]
        if t == SIDE_QUADS - 1:
            copies.append(base_copy(t, PAIR_ROWS))
        base_copies.append(copies)
        each_side(copies, lambda copy: copy.start())

    def flux_y(t):
        k = 2 * t
        extra = left3(wy(1), two_columns(wb, k), NN)
        for i in range(2):
            whole = left3(
                wy(0), cat([wa[column(k + i), :], wc[column(k + i), :]], 1), NN
            )
            g[k + i] = whole[:, :LANES] + extra[:, i * LANES : (i + 1) * LANES]
            f[k + i] = whole[:, LANES:]

    loop(QK // 2, 4, flux_y)

    def coupled_z(t):
        rows = [held_coupled[:, lanes(2 * t + i)] for i in range(2)]
        out = left3(wz(0), wide_rows(*rows), NT)
        for i in range(2):
            wa[pair_rows(2 * t + i), :] = out[:, i * LANES : (i + 1) * LANES]

    loop(PAIRS // 2, 4, coupled_z)

    state_copies = []
    for q in range(STATE_QUADS):
        pairs = 2 if q < STATE_QUADS - 1 else 1
        deep = []
        for j in range(0, 2 * pairs, 2):
            both_planes = left3(wy(0), two_columns(wa, 4 * q + j), NN)
            for i in range(2):
                k = 4 * q + j + i
                total = g[k] + both_planes[:, i * LANES : (i + 1) * LANES]
                deep.append(cat(ahead_deep(total) + ahead_deep(f[k]), 1))
        modes = matmul(cat(deep, 0), flat(xt[...]))
        fold = True if q == 0 else None
        emit_planes(state_send, QUAD_ROWS * q, 4 * q, modes, 2 * pairs, fold)
        rows = pl.ds(QUAD_ROWS * q, QUAD_ROWS if pairs == 2 else PAIR_ROWS)
        copy = remote(
            state_send.at[rows], state_recv.at[rows], state_send_sem.at[q],
            state_recv_sem.at[q], far,
        )
        copy.start()
        state_copies.append(copy)

    def spectral(held, fold, first_k, table_ref, work):
        tiles = unpack_quad(held)
        deep = []
        wave_x, wave_y = waves
        for j in range(len(tiles) // 3):
            for i, (m0, m1) in enumerate(unpack_pair(tiles[3 * j : 3 * j + 3])):
                k = jnp.asarray(first_k + 2 * j + i, jnp.int32)
                inverse = 1.0 / jnp.maximum(k, 1).astype(f32)
                m2 = -(wave_x * m0 + wave_y * m1) * inverse
                if fold is not None and i == 0 and j == 0:
                    third = pltpu.roll(m0, MP - THIRD - 1, 0)
                    m2 = jnp.where(fold, folded * third, m2)
                    m0 = jnp.where(fold, folded * m0, m0)
                    m1 = jnp.where(fold, folded * m1, m1)
                high, low = split(cat([m0, m1, m2], 1))
                deep.append(cat([high, low, high], 1))
        rows = matmul(cat(deep, 0), flat(table_ref[...]))
        planes = []
        for i in range(len(deep)):
            mine = rows[MP * i : MP * (i + 1)]
            planes.append(cat([mine[:, :LANES], mine[:, LANES:]], 0))
        for j in range(0, len(deep), 2):
            out = left3(yb(0), cat(planes[j : j + 2], 1), NN)
            for i in range(2):
                work[column(first_k + j + i), :] = out[:, i * LANES : (i + 1) * LANES]

    span = base_sum.shape[0] // 2
    sum_copies = []
    for t in range(SIDE_QUADS):
        each_side(base_copies[t], lambda copy: copy.wait_recv())
        mine = slice(QUAD_ROWS * t, QUAD_ROWS * (t + 1))
        total = base_send[mine, :] + base_recv[mine, :]
        if t == SIDE_QUADS - 1:
            place = lax.broadcasted_iota(jnp.int32, total.shape, 0)
            total = jnp.where((side == 0) | (place < PAIR_ROWS), total, 0.0)
        rows = pl.ds(pl.multiple_of(span * side + QUAD_ROWS * t, 8), QUAD_ROWS)
        base_sum[rows, :] = total
        copy = remote(
            base_sum.at[rows], base_sum.at[rows], sum_send.at[t], sum_recv.at[t], twin
        )
        copy.start()
        sum_copies.append(copy)

    def base_back(place, t):
        rows = pl.ds(pl.multiple_of(span * place + QUAD_ROWS * t, 8), QUAD_ROWS)
        fold = place == 0 if t == 0 else None
        spectral(base_sum[rows, :], fold, 4 * (SIDE_QUADS * place + t), xb, w0)

    for t in range(SIDE_QUADS):
        base_back(side, t)
    for t in range(SIDE_QUADS):
        sum_copies[t].wait_recv()
        base_back(1 - side, t)

    def finish_base(p):
        rows = left3(zb(0), w0[pair_rows(p), :], NN).T
        out_base[:, :, lanes(p)] = rows[:48].reshape(3, half, LANES)

    loop(PAIRS, 8, finish_base)

    for q in range(STATE_QUADS):
        state_copies[q].wait_recv()
        rows = QUAD_ROWS if q < STATE_QUADS - 1 else PAIR_ROWS
        mine = slice(QUAD_ROWS * q, QUAD_ROWS * q + rows)
        total = state_send[mine, :] + state_recv[mine, :]
        spectral(total, True if q == 0 else None, 4 * q, xs, wc)

    def finish_state(p):
        rows = left3(zb(0), wc[pair_rows(p), :], NN).T
        near = near_state[:, :, lanes(p)]
        out_state[:, :, lanes(p)] = rows[:96].reshape(near.shape) - near

    near_copies[0].wait_recv()
    loop(PAIRS, 8, finish_state)

    def base_difference(i):
        span = pl.ds(pl.multiple_of(i * 512, 512), 512)
        out_base[:, :, span] -= near_base[:, :, span]

    near_copies[1].wait_recv()
    loop(N * N // 512, 4, base_difference)

    sent = near_copies + share_copies + pass_copies + sum_copies + state_copies
    for copy in sent:
        copy.wait_send()
    for copies in base_copies:
        each_side(copies, lambda copy: copy.wait_send())


def fused_body(base, state, wavenumber, cutoff):
    base, state = base[0], state[0, 0]
    rows = base.shape[1]
    half = rows // lax.axis_size("comp")
    slabs = lax.axis_size("slab")
    tables = [jnp.asarray(np.concatenate(group)) for group in table_groups()]
    hbm = pl.BlockSpec(memory_space=pltpu.HBM)
    smem = pl.BlockSpec(memory_space=pltpu.SMEM)
    vmem = lambda *shape: pltpu.VMEM(shape, f32)
    dma = lambda count: pltpu.SemaphoreType.DMA((count,))
    wide, narrow = table_places()
    wz, wy, yb, zb, xt = (pltpu.VMEM((entry[1], 2 * MP, 3 * LANES), bf16) for entry in wide)
    pd, xs, xb = (pltpu.VMEM((entry[1], 3 * LANES, 2 * LANES), bf16) for entry in narrow)
    work = vmem(2 * N * KP, LANES)
    share = vmem(3 * SIDE_QUADS, 2 * BODY + 8, LANES)
    planes = vmem(QK, 2 * MP, LANES)
    base_tiles = vmem(SIDE_QUADS * QUAD_ROWS, LANES)
    state_tiles = vmem((STATE_QUADS - 1) * QUAD_ROWS + PAIR_ROWS, LANES)
    base_half = vmem(3, half, N * N)
    whole = vmem(3, rows, N * N)
    scratch = [
        whole, whole, base_half, whole, wz, wy, pd, xt, xs, xb, yb, zb,
        *[work] * 7, vmem(3 * rows, N * N), planes, share, share, share, planes, planes,
        base_tiles, base_tiles, vmem(2 * SIDE_QUADS * QUAD_ROWS, LANES), state_tiles, state_tiles,
        dma(14), dma(2), dma(2), *[dma(SIDE_QUADS)] * 8, *[dma(STATE_QUADS)] * 2,
    ]
    base_gap, state_gap = pl.pallas_call(
        fused,
        out_shape=[
            jax.ShapeDtypeStruct((3, half, N * N), f32),
            jax.ShapeDtypeStruct((3, rows, N * N), f32),
        ],
        in_specs=[hbm, hbm, smem, smem, hbm, hbm],
        out_specs=[pl.BlockSpec(memory_space=pltpu.VMEM)] * 2,
        scratch_shapes=scratch,
        compiler_params=pltpu.CompilerParams(
            vmem_limit_bytes=51 * 2**20, collective_id=0, has_side_effects=True
        ),
        cost_estimate=pl.CostEstimate(flops=10**10, bytes_accessed=10**7, transcendentals=0),
    )(base, state, cutoff, wavenumber, *tables)
    return base_gap[None], state_gap[None, None]


def solution(mesh):
    sizes = dict(mesh.shape)
    one_kernel = sizes["slab"] == 2 and sizes["comp"] == 2 and sizes["seg"] > 1
    return jax.shard_map(
        fused_body if one_kernel else body,
        mesh=mesh,
        in_specs=(
            P(("groups", "seg"), None, "slab", None),
            P(("groups", "seg"), "comp", None, "slab", None),
            P("groups"),
            P("groups"),
        ),
        out_specs=(
            P(("groups", "seg"), None, ("slab", "comp"), None),
            P(("groups", "seg"), "comp", None, "slab", None),
        ),
        check_vma=False,
    )
```

```python
import functools

import jax
import jax.numpy as jnp
import ml_dtypes
import numpy as np
from jax import lax
from jax.experimental import pallas as pl
from jax.experimental.pallas import tpu as pltpu
from jax.sharding import PartitionSpec as P

N = 64
BACK, GRID, AHEAD, SPEC, Z1, Z2, Z3, Y1 = 4, 4, 4, 4, 8, 4, 8, 6
THIRD = N // 3
LOW = THIRD - 3
KZ = THIRD + 1
KP = 24
MP = 48
PAIRS = N // 2
FLUX = 14 * 10**9
HALF = KZ // 2
viscosity = 0.025
time_step = 0.02
forcing_amp = 10.0
f32 = jnp.float32
bf16 = jnp.bfloat16

NN = (((1,), (0,)), ((), ()))
NT = (((1,), (1,)), ((), ()))


def split(value):
    high = value.astype(bf16)
    return high, (value - high.astype(f32)).astype(bf16)


def dot3(left, right, dims):
    dot = functools.partial(lax.dot_general, dimension_numbers=dims, preferred_element_type=f32)
    return dot(left[0], right[0]) + (dot(left[0], right[1]) + dot(left[1], right[0]))


def table(values):
    values = np.asarray(values, np.float32)
    high = values.astype(ml_dtypes.bfloat16)
    low = (values - high.astype(np.float32)).astype(ml_dtypes.bfloat16)
    return np.stack([high, low], axis=-3)


def table3(values):
    high, low = np.moveaxis(table(values), -3, 0)
    return np.concatenate([high, high, low], axis=-1)


def left3(left, value, dims):
    high, low = split(value)
    deep = jnp.concatenate([high, low, high], axis=dims[0][1][0])
    return lax.dot_general(left, deep, dimension_numbers=dims, preferred_element_type=f32)


def signed():
    m = np.arange(2 * THIRD + 1)
    return np.where(m <= THIRD, m, m - (2 * THIRD + 1))


def angles(first, second):
    return np.mod(np.outer(first, second), N) * (2 * np.pi / N)


def cuts():
    return range(LOW, THIRD + 1)


def z_tables():
    plain, ik = [], []
    k = np.arange(KZ)
    a = angles(k, np.arange(N))
    for cut in cuts():
        keep = 1.0 * (k <= cut)[:, None]
        w = np.zeros((2, KP, N))
        v = np.zeros((2, KP, N))
        w[0, :KZ], w[1, :KZ] = keep * np.cos(a), -keep * np.sin(a)
        v[0, :KZ], v[1, :KZ] = keep * k[:, None] * np.sin(a), keep * k[:, None] * np.cos(a)
        plain.append(np.kron(np.eye(2), w.reshape(2 * KP, N)))
        ik.append(np.kron(np.eye(2), v.reshape(2 * KP, N)))
    return table3(np.stack([np.stack(plain), np.stack(ik)], axis=1))


def y_tables():
    out = []
    m = signed()
    count = len(m)
    a = angles(m, np.arange(N))
    for cut in cuts():
        keep = 1.0 * (np.abs(m) <= cut)[:, None]
        c, s = keep * np.cos(a), keep * np.sin(a)
        w = np.zeros((2, MP, N, 2))
        w[0, :count, :, 0], w[0, :count, :, 1] = c, s
        w[1, :count, :, 0], w[1, :count, :, 1] = -s, c
        v = np.zeros_like(w)
        v[0, :count] = -m[:, None, None] * w[1, :count]
        v[1, :count] = m[:, None, None] * w[0, :count]
        out.append(np.stack([w.reshape(2 * MP, 2 * N), v.reshape(2 * MP, 2 * N)]))
    return table3(np.stack(out))


def y_back():
    m = signed()
    count = len(m)
    a = angles(np.arange(N), m)
    c, s = np.cos(a) / N, np.sin(a) / N
    w = np.zeros((N, 2, 2, MP))
    w[:, 0, 0, :count], w[:, 0, 1, :count] = c, -s
    w[:, 1, 0, :count], w[:, 1, 1, :count] = s, c
    v = np.zeros_like(w)
    v[:, :, 0, :count] = m * w[:, :, 1, :count]
    v[:, :, 1, :count] = -m * w[:, :, 0, :count]
    return table3(np.stack([w.reshape(2 * N, 2 * MP), v.reshape(2 * N, 2 * MP)]))


def z_back():
    k = np.arange(KZ)
    a = angles(k, np.arange(N))
    weight = (np.where(k == 0, 1.0, 2.0) / N)[:, None]
    w = np.zeros((2, KP, N))
    w[0, :KZ], w[1, :KZ] = weight * np.cos(a), -weight * np.sin(a)
    v = np.zeros_like(w)
    v[0, :KZ] = k[:, None] * w[1, :KZ]
    v[1, :KZ] = -k[:, None] * w[0, :KZ]
    pair = lambda t: np.kron(np.eye(2), t.reshape(2 * KP, N))
    return table3(np.stack([pair(w).T, pair(v).T]))


def x_filters(slabs):
    rows = N // slabs
    out = []
    x = np.arange(N)
    for cut in cuts():
        n = np.arange(-cut, cut + 1)
        d = np.mod(x[:, None] - x[None, :], N)
        phase = 2 * np.pi / N * n[:, None, None] * -d
        plain = np.cos(phase).sum(0) / N
        deriv = (-n[:, None, None] * np.sin(phase)).sum(0) / N
        both = np.stack([plain, deriv]).reshape(2, slabs, rows, slabs, rows)
        wide = np.zeros((slabs, 2, slabs, 3, rows, 3, rows))
        for i in range(3):
            wide[:, :, :, i, :, i, :] = both.transpose(3, 0, 1, 2, 4)
        out.append(wide.reshape(slabs, 2, slabs, 3 * rows, 3 * rows))
    return table(np.stack(out))


def x_tables(slabs):
    rows = N // slabs
    n = signed()
    count = len(n)
    a = angles(np.arange(N), n).reshape(slabs, rows, count)
    out = []
    for cut in cuts():
        keep = 1.0 * (np.abs(n) <= cut)
        c, s = np.cos(a) * keep, np.sin(a) * keep
        w = np.zeros((slabs, 2, 2, 3, rows, 3, 2, 64))
        for i in range(3):
            w[:, 0, 0, i, :, i, 0, :count] = c
            w[:, 0, 0, i, :, i, 1, :count] = -s
            w[:, 0, 1, i, :, i, 0, :count] = s
            w[:, 0, 1, i, :, i, 1, :count] = c
        w[:, 1, :, :, :, :, 0, :count] = -n * w[:, 0, :, :, :, :, 1, :count]
        w[:, 1, :, :, :, :, 1, :count] = n * w[:, 0, :, :, :, :, 0, :count]
        out.append(w.reshape(slabs, 2, 2, 3 * rows, 384))
    return table(np.stack(out))


def x_back(slabs):
    rows = N // slabs
    n = signed()
    count = len(n)
    a = angles(n, np.arange(N)).reshape(count, slabs, rows).transpose(1, 0, 2)
    c, s = np.cos(a) / N, np.sin(a) / N
    w = np.zeros((slabs, 2, 3, 2, 64, 3, rows))
    for i in range(3):
        w[:, 0, i, 0, :count, i] = c
        w[:, 0, i, 1, :count, i] = -s
        w[:, 1, i, 0, :count, i] = s
        w[:, 1, i, 1, :count, i] = c
    return table(w.reshape(slabs, 2, 384, 3 * rows))


def both(ref, *index):
    return ref[(*index, 0)], ref[(*index, 1)]


def lanes(p):
    return pl.ds(pl.multiple_of(p * 128, 128), 128)


def pair_rows(p):
    return pl.ds(pl.multiple_of(p * 4 * KP, 8), 4 * KP)


def column(k):
    return pl.ds(k, 2 * N, stride=KP)


def flat(block):
    return block.reshape(block.shape[0] * block.shape[1], block.shape[2])


def loop(count, unroll, step):
    def go(i, carry):
        step(i)
        return carry

    lax.fori_loop(0, count, go, 0, unroll=unroll)


def clear_padding(*works):
    for k in range(KZ, KP):
        for work in works:
            work[column(k), :] = jnp.zeros((2 * N, work.shape[1]), f32)


def base_ahead(base_ref, wz_ref, wy_ref, out_ref, half_ref, work):
    def along_z(p):
        work[pair_rows(p), :] = left3(wz_ref[0], flat(base_ref[:, :, lanes(p)]), NT)

    loop(PAIRS, Z1, along_z)

    def along_y(k):
        out_ref[k] = left3(wy_ref[0], work[column(k), :], NN)

    loop(KZ, Y1, along_y)
    first = HALF * lax.axis_index("comp")

    def share(j):
        half_ref[j] = out_ref[first + j]

    loop(HALF, 1, share)


def sign_step():
    return jnp.where(lax.axis_index("comp") == 0, -time_step, time_step).astype(f32)


def flux_ahead(base_ref, state_ref, wz_ref, wy_ref, g_ref, work_a, work_b):
    scale = sign_step()

    def along_z(p):
        state = state_ref[:, :, lanes(p)]
        scaled = state * scale
        f1, f2 = (flat(scaled * base_ref[j, :, lanes(p)][None]) for j in (1, 2))
        plain = wz_ref[0]
        work_a[pair_rows(p), :] = left3(plain, flat(state), NT) + left3(wz_ref[1], f2, NT)
        work_b[pair_rows(p), :] = left3(plain, f1, NT)

    loop(PAIRS, Z2, along_z)

    def along_y(k):
        g_ref[k] = left3(wy_ref[0], work_a[column(k), :], NN) + left3(
            wy_ref[1], work_b[column(k), :], NN
        )

    loop(KZ, Y1, along_y)


def flux_x_ahead(base_ref, state_ref, wz_ref, wy_ref, f_ref, work):
    scale = sign_step()

    def along_z(p):
        f0 = flat(state_ref[:, :, lanes(p)] * scale * base_ref[0, :, lanes(p)][None])
        work[pair_rows(p), :] = left3(wz_ref[0], f0, NT)

    loop(PAIRS, Z2, along_z)

    def along_y(k):
        f_ref[k] = left3(wy_ref[0], work[column(k), :], NN)

    loop(KZ, Y1, along_y)


def gradients(
    slabs, count, *refs,
):
    got, rest = refs[:count], refs[count:]
    side = lax.axis_index("comp")
    if count == 1:
        visits = [(lambda j: (j, [got[0][s, j] for s in range(slabs)]), KZ)]
    else:
        own, mine, partner = got

        def visit(ref, first):
            return lambda j: (first + j, [own[first + j], ref[j]])

        visits = [
            (visit(mine, HALF * side), HALF),
            (visit(partner, HALF * (1 - side)), HALF),
        ]
    gradients_of(slabs, visits, *rest)


def gradients_of(
    slabs, visits, base_ref, state_ref, force_ref, pd_ref, yb_ref, zb_ref, wz_ref, wy_ref,
    xt_ref, base_out_ref, coupled_ref, work_0, work_1, work_2,
):
    tangent = lax.axis_index("comp") == 0

    def back_y(visit, j):
        k, sources = visit(j)
        sources = [split(source) for source in sources]

        def across(kind):
            total = dot3(sources[0], both(pd_ref, kind, 0), NN)
            for s in range(1, slabs):
                total = total + dot3(sources[s], both(pd_ref, kind, s), NN)
            return total

        plain, deriv = across(0), across(1)
        work_0[column(k), :] = left3(yb_ref[0], deriv, NN)
        work_1[column(k), :] = left3(yb_ref[1], plain, NN)
        work_2[column(k), :] = left3(yb_ref[0], plain, NN)

    clear_padding(work_0, work_1, work_2)
    for visit, count in visits:
        loop(count, BACK, functools.partial(back_y, visit))

    def grid_space(p):
        state = state_ref[:, :, lanes(p)]
        base = base_ref[:, :, lanes(p)]
        grad = []
        for work, kind in ((work_0, 0), (work_1, 0), (work_2, 1)):
            rows = left3(zb_ref[kind], work[pair_rows(p), :], NN).T
            grad.append(rows.reshape(base.shape))
        coupled, driven = [], []
        for i in range(3):
            total = 0.0
            drive = 0.0
            for j in range(3):
                total = total + jnp.where(tangent, grad[j][i], grad[i][j]) * state[j]
                drive = drive + grad[j][i] * base[j]
            if i == 0:
                drive = drive - force_ref[:, lanes(p)]
            coupled.append(-time_step * total)
            driven.append(base[i] - time_step * drive)
        plain = wz_ref[0]
        coupled_ref[pair_rows(p), :] = left3(plain, jnp.concatenate(coupled, axis=0), NT)
        work_1[pair_rows(p), :] = left3(plain, jnp.concatenate(driven, axis=0), NT)

    loop(PAIRS, GRID, grid_space)

    waves = plane_waves()
    first = HALF * lax.axis_index("comp")

    def base_ahead_x(step):
        j = HALF - 1 - step
        k = first + j
        driven = left3(wy_ref[0], work_1[column(k), :], NN)
        modes = 0.0
        for d in range(2):
            rows = slice(d * MP, (d + 1) * MP)
            modes = modes + dot3(split(driven[rows]), both(xt_ref, 0, d), NN)
        emit(waves, base_out_ref, j, HALF, modes, k)

    loop(HALF, AHEAD, base_ahead_x)


def emit(waves, ref, slot, last, modes, k):
    new = projected(waves, modes, k)
    ref[slot] = jnp.concatenate(new[:2], axis=1)
    ref[last] = jnp.concatenate([new[2], jnp.zeros_like(new[2])], axis=1)


def state_ahead_x(coupled_ref, wy_ref, xt_ref, g_ref, f_ref, out_ref):
    waves = plane_waves()

    def ahead_x(step):
        k = KZ - 1 - step
        total = g_ref[k] + left3(wy_ref[0], coupled_ref[column(k), :], NN)
        outer = f_ref[k]
        modes = 0.0
        for d in range(2):
            rows = slice(d * MP, (d + 1) * MP)
            modes = modes + dot3(split(total[rows]), both(xt_ref, 0, d), NN)
            modes = modes + dot3(split(outer[rows]), both(xt_ref, 1, d), NN)
        emit(waves, out_ref, k, KZ, modes, k)

    loop(KZ, AHEAD, ahead_x)


def plane_waves():
    column_n = lax.rem(lax.broadcasted_iota(jnp.int32, (MP, 128), 1), 64)
    row_m = lax.broadcasted_iota(jnp.int32, (MP, 128), 0)
    wrap = lambda v: jnp.where(v <= THIRD, v, v - (2 * THIRD + 1)).astype(f32)
    return wrap(column_n), wrap(row_m)


def projected(waves, modes, k):
    wave_x, wave_y = waves
    wave_z = jnp.asarray(k, jnp.int32).astype(f32)
    square = wave_x * wave_x + wave_y * wave_y + wave_z * wave_z
    safe = jnp.where(square > 0, square, 1.0)
    damping = 1.0 / (1.0 + viscosity * time_step * square)
    w = [modes[:, i * 128 : (i + 1) * 128] for i in range(3)]
    divergence = (wave_x * w[0] + wave_y * w[1] + wave_z * w[2]) / safe
    return [
        damping * (w[0] - wave_x * divergence),
        damping * (w[1] - wave_y * divergence),
        damping * (w[2] - wave_z * divergence),
    ]


def finish(count, halved, *refs):
    parts, (near_ref, xb_ref, yb_ref, zb_ref, out_ref, work) = refs[:count], refs[count:]
    wave_x, wave_y = plane_waves()
    clear_padding(work)

    def spectral(parts, first, last, j):
        k = first + j
        modes, third = 0.0, 0.0
        for part in parts:
            modes = modes + part[j]
            third = third + part[last, :, :128]
        w0, w1 = modes[:, :128], modes[:, 128:]
        whole = jnp.asarray(k, jnp.int32)
        inverse = 1.0 / jnp.maximum(whole, 1).astype(f32)
        w2 = jnp.where(whole == 0, third, -(wave_x * w0 + wave_y * w1) * inverse)
        new = split(jnp.concatenate([w0, w1, w2], axis=1))
        rows = [dot3(new, both(xb_ref, d), NN) for d in range(2)]
        work[column(k), :] = left3(yb_ref[0], jnp.concatenate(rows, axis=0), NN)

    if halved:
        side = lax.axis_index("comp")
        for part, place in zip(parts, (side, 1 - side)):
            loop(HALF, SPEC, functools.partial(spectral, [part], HALF * place, HALF))
    else:
        loop(KZ, SPEC, functools.partial(spectral, parts, 0, KZ))

    def along_z(p):
        rows = left3(zb_ref[0], work[pair_rows(p), :], NN).T
        near = near_ref[:, :, lanes(p)]
        out_ref[:, :, lanes(p)] = rows.reshape(near.shape) - near

    loop(PAIRS, Z3, along_z)


def call(kernel, out_shape, scratch, cost, *operands):
    return pl.pallas_call(
        kernel,
        out_shape=out_shape,
        in_specs=[pl.BlockSpec(memory_space=pltpu.VMEM)] * len(operands),
        out_specs=jax.tree.map(lambda _: pl.BlockSpec(memory_space=pltpu.VMEM), out_shape),
        scratch_shapes=scratch,
        compiler_params=pltpu.CompilerParams(vmem_limit_bytes=48 * 2**20),
        cost_estimate=pl.CostEstimate(flops=cost, bytes_accessed=2**10, transcendentals=0),
    )(*operands)


def body(base, state, wavenumber, cutoff):
    base, state = base[0], state[0, 0]
    slab_rows = base.shape[1]
    half = slab_rows // lax.axis_size("comp")
    slabs = lax.axis_size("slab")
    segs = lax.axis_size("seg")
    slab = lax.axis_index("slab")
    side = lax.axis_index("comp")
    width = 3 * slab_rows
    which = cutoff - LOW

    route = [((s, 0), ((s - 1) % segs, 0)) for s in range(segs)]
    route += [((s, 1), ((s + 1) % segs, 1)) for s in range(segs)]
    route = [(a * 2 + b, c * 2 + d) for (a, b), (c, d) in route]
    wz = lax.dynamic_index_in_dim(jnp.asarray(z_tables()), which[2], 0, False)
    wy = lax.dynamic_index_in_dim(jnp.asarray(y_tables()), which[1], 0, False)
    filters, ahead = jnp.asarray(x_filters(slabs)), jnp.asarray(x_tables(slabs))
    pick = lambda t: lax.dynamic_slice(
        t, (which[0], slab) + (0,) * (t.ndim - 2), (1, 1) + t.shape[2:]
    )[0, 0]
    pd, xt = pick(filters), pick(ahead)
    xb = lax.dynamic_index_in_dim(jnp.asarray(x_back(slabs)), slab, 0, False)
    yb, zb = jnp.asarray(y_back()), jnp.asarray(z_back())

    modes = jax.ShapeDtypeStruct((KZ, 2 * MP, width), f32)
    half_modes = jax.ShapeDtypeStruct((HALF, 2 * MP, width), f32)
    spectrum = jax.ShapeDtypeStruct((KZ + 1, MP, 256), f32)
    half_spectrum = jax.ShapeDtypeStruct((HALF + 1, MP, 256), f32)
    work = pltpu.VMEM((2 * N * KP, width), f32)
    own, share = call(base_ahead, (modes, half_modes), [work], 4 * 10**9, base, wz, wy)
    later, later_base, share = lax.optimization_barrier((state, base, share))
    near_state = lax.ppermute(later, ("seg", "comp"), route)
    base_half = lax.dynamic_slice_in_dim(later_base, side * half, half, 1)
    near_base = lax.ppermute(base_half, "seg", [((s + 1) % segs, s) for s in range(segs)])
    if slabs == 2:
        other = lax.ppermute(share, "slab", [(0, 1), (1, 0)])
        partner = lax.ppermute(other, "comp", [(0, 1), (1, 0)])
        first = slab == 0
        got = (own, other, partner)
        pd = jnp.where(first, pd, pd[:, ::-1])
    else:
        got = (lax.all_gather(own, "slab"),)
    g = call(flux_ahead, modes, [work] * 2, FLUX, base, state, wz, wy)
    f = call(flux_x_ahead, modes, [work], 10**9, base, state, wz, wy)

    *got, g, f = lax.optimization_barrier((*got, g, f))

    y = jnp.arange(N, dtype=jnp.int32)
    phase = jnp.mod(wavenumber[0] * y, N).astype(f32) * (2.0 * jnp.pi / N)
    force = jnp.repeat(forcing_amp * jnp.sin(phase), N)[None]
    lined = jax.ShapeDtypeStruct((2 * N * KP, width), f32)
    base_modes, coupled = call(
        functools.partial(gradients, slabs, len(got)), (half_spectrum, lined), [work] * 3,
        25 * 10**9, *got, base, state, force, pd, yb, zb, wz, wy, xt,
    )
    state_modes = call(state_ahead_x, spectrum, [], 3 * 10**9, coupled, wy, xt, g, f)
    near_state, near_base, state_modes = lax.optimization_barrier(
        (near_state, near_base, state_modes)
    )
    if slabs == 2:
        swap = lambda v: lax.ppermute(v, "slab", [(0, 1), (1, 0)])
        state_other = swap(state_modes)
        base_other, state_modes = lax.optimization_barrier((swap(base_modes), state_modes))
        base_sum = base_modes + base_other
        state_parts = (state_modes, state_other)
    else:
        base_sum = lax.psum(base_modes, "slab")
        state_parts = (lax.psum(state_modes, "slab"),)
    base_parts = (base_sum, lax.ppermute(base_sum, "comp", [(0, 1), (1, 0)]))

    shape = jax.ShapeDtypeStruct(base.shape, f32)
    last = functools.partial(finish, len(state_parts), False)
    last_base = functools.partial(finish, 2, True)
    near_wide = jnp.concatenate([near_base, near_base], axis=1)
    base_gap = call(last_base, shape, [work], 10**8, *base_parts, near_wide, xb, yb, zb)
    base_gap = lax.dynamic_slice_in_dim(base_gap, side * half, half, 1)
    state_gap = call(last, shape, [work], 10**10, *state_parts, near_state, xb, yb, zb)
    return base_gap[None], state_gap[None, None]


LANES = 128
QK = 24
SIDE_QUADS = 3
STATE_QUADS = 6
FLUX_FIRST = 8


def lane_pad(values, axis, size=LANES):
    pad = [(0, 0)] * values.ndim
    pad[axis] = (0, size - values.shape[axis])
    return np.pad(values, pad)


def halves(values):
    values = np.asarray(values, np.float32)
    high = values.astype(ml_dtypes.bfloat16)
    return high, (values - high.astype(np.float32)).astype(ml_dtypes.bfloat16)


def filter_tables(slabs):
    rows = N // slabs
    x = np.arange(N)
    out = []
    for cut in cuts():
        n = np.arange(-cut, cut + 1)
        d = np.mod(x[:, None] - x[None, :], N)
        phase = 2 * np.pi / N * n[:, None, None] * -d
        plain = np.cos(phase).sum(0) / N
        deriv = (-n[:, None, None] * np.sin(phase)).sum(0) / N
        both_kinds = np.stack([plain, deriv]).reshape(2, slabs, rows, slabs, rows)
        per_slab = []
        for slab in range(slabs):
            blocks = []
            for source in (slab, 1 - slab):
                wide = np.zeros((3, rows, 2, LANES))
                for i in range(3):
                    wide[i, :, :, i * rows : (i + 1) * rows] = both_kinds[
                        :, source, :, slab
                    ].transpose(1, 0, 2)
                blocks.append(halves(lane_pad(wide.reshape(3 * rows, 2 * LANES), 0)))
            (own_high, own_low), (far_high, far_low) = blocks
            per_slab.append(
                np.concatenate([own_high, own_high, far_high, far_high, own_low, far_low])
            )
        out.append(np.stack(per_slab))
    return np.stack(out, axis=1)


def ahead_tables(slabs):
    rows = N // slabs
    n = signed()
    count = len(n)
    a = angles(np.arange(N), n).reshape(slabs, rows, count)
    c, s = np.cos(a), np.sin(a)
    w = np.zeros((slabs, 2, 2, 3, rows, 3, 2, 64))
    for i in range(3):
        w[:, 0, 0, i, :, i, 0, :count] = c
        w[:, 0, 0, i, :, i, 1, :count] = -s
        w[:, 0, 1, i, :, i, 0, :count] = s
        w[:, 0, 1, i, :, i, 1, :count] = c
    w[:, 1, :, :, :, :, 0, :count] = -n * w[:, 0, :, :, :, :, 1, :count]
    w[:, 1, :, :, :, :, 1, :count] = n * w[:, 0, :, :, :, :, 0, :count]
    high, low = halves(lane_pad(w.reshape(slabs, 2, 2, 3 * rows, 3 * LANES), 3))
    blocks = []
    for kind in range(2):
        h, l = high[:, kind], low[:, kind]
        blocks += [h[:, 0], h[:, 0], h[:, 1], h[:, 1], l[:, 0], l[:, 1]]
    return np.concatenate(blocks, axis=1)


def behind_tables(parts):
    rows = N // parts
    n = signed()
    count = len(n)
    a = angles(n, np.arange(N)).reshape(count, parts, rows).transpose(1, 0, 2)
    c, s = np.cos(a) / N, np.sin(a) / N
    w = np.zeros((parts, 3, 2, 64, 2, LANES))
    for i in range(3):
        place = slice(i * rows, (i + 1) * rows)
        w[:, i, 0, :count, 0, place] = c
        w[:, i, 1, :count, 0, place] = -s
        w[:, i, 0, :count, 1, place] = s
        w[:, i, 1, :count, 1, place] = c
    high, low = halves(w.reshape(parts, 3 * LANES, 2 * LANES))
    return np.concatenate([high, high, low], axis=1)


def table_groups():
    blocks = lambda t, height: t.reshape(-1, height, t.shape[-1])
    wide = [z_tables(), y_tables()]
    wide += [lane_pad(lane_pad(t, 1, 4 * MP), 2, 3 * LANES) for t in (y_back(), z_back())]
    wide.append(ahead_tables(2))
    narrow = [filter_tables(2), behind_tables(2), behind_tables(4)]
    return [blocks(t, 2 * MP) for t in wide], [blocks(t, 3 * LANES) for t in narrow]


def table_places():
    counts = (1, 1, 1, 1, 2), (2, 2, 4)
    places = []
    for group, shares in zip(table_groups(), counts):
        start, entries = 0, []
        for t, share in zip(group, shares):
            entries.append((start, len(t) // share))
            start += len(t)
        places.append(entries)
    return places


def quarter_sine(position):
    folded = lax.rem(position, N // 2)
    folded = jnp.minimum(folded, N // 2 - folded)
    angle = folded.astype(f32) * (2.0 * np.pi / N)
    square = angle * angle
    series = 1.0
    for order in (12, 10, 8, 6, 4, 2):
        series = 1.0 - series * square * (1.0 / (order * (order + 1)))
    return jnp.where(position < N // 2, 1.0, -1.0) * angle * series


def cat(values, axis):
    return jnp.concatenate(values, axis=axis)


def wide_rows(*fields):
    blank = jnp.zeros((LANES - fields[0].shape[0], LANES), f32)
    return cat([part for field in fields for part in (field, blank)], 0)


def matmul(left, right):
    return lax.dot_general(left, right, NN, preferred_element_type=f32)


def half_lane(shape):
    return lax.rem(lax.broadcasted_iota(jnp.int32, shape, 1), 64)


def turn(value, shift):
    return pltpu.roll(value, shift % LANES, 1)


GAP = 2 * THIRD + 1
STEP = 64 - GAP
PIECES = (GAP, GAP - STEP, GAP - 2 * STEP)
BODY = 40
PAIR_ROWS = 3 * BODY + 16
QUAD_ROWS = PAIR_ROWS + 3 * BODY + 8


def pack_pair(first, second):
    gap = half_lane(first[0].shape) >= GAP
    carried = (first[0], second[0], first[1])
    return [jnp.where(gap, turn(second[1], by), held) for by, held in zip(PIECES, carried)]


def unpack_pair(tiles):
    lane = half_lane(tiles[0].shape)
    last = turn(tiles[2], -PIECES[2])
    last = jnp.where(lane < 2 * STEP, turn(tiles[1], -PIECES[1]), last)
    last = jnp.where(lane < STEP, turn(tiles[0], -PIECES[0]), last)
    return (tiles[0], tiles[2]), (tiles[1], last)


def tails(first, second):
    low = lax.broadcasted_iota(jnp.int32, first.shape, 0) < 4
    return jnp.where(low, first, pltpu.roll(second, 4, 0))


def squeeze(tile):
    return cat([tile[:BODY], tile[MP : MP + BODY], tails(tile[BODY:MP], tile[MP + BODY :])], 0)


def unsqueeze(held):
    tail = held[2 * BODY :]
    return cat([held[:BODY], tail, held[BODY : 2 * BODY], pltpu.roll(tail, 4, 0)], 0)


def pack_quad(tiles):
    body = [tile[:BODY] for tile in tiles]
    tail = [tile[BODY:] for tile in tiles]
    if len(tiles) == 3:
        return cat([*body, tails(tail[0], tail[1]), tail[2]], 0)
    return cat(
        [
            *body[:3], tails(tail[0], tail[1]), tails(tail[2], tail[5]),
            *body[3:], tails(tail[3], tail[4]),
        ],
        0,
    )


def unpack_quad(held):
    part = lambda start, size: held[start : start + size]
    body = [part(BODY * i, BODY) for i in range(3)]
    first, second = part(3 * BODY, 8), part(3 * BODY + 8, 8)
    tail = [first, pltpu.roll(first, 4, 0), second]
    if held.shape[0] > PAIR_ROWS:
        body += [part(PAIR_ROWS + BODY * i, BODY) for i in range(3)]
        last = part(PAIR_ROWS + 3 * BODY, 8)
        tail += [last, pltpu.roll(last, 4, 0), pltpu.roll(second, 4, 0)]
    return [cat([b, t], 0) for b, t in zip(body, tail)]


def pack_share(planes):
    lane = lax.broadcasted_iota(jnp.int32, planes[0].shape, 1)
    tiles = [jnp.where(lane < 96, planes[i], turn(planes[3], 96 - 32 * i)) for i in range(3)]
    return [squeeze(tile) for tile in tiles]


def unpack_share(held):
    tiles = [unsqueeze(part) for part in held]
    lane = lax.broadcasted_iota(jnp.int32, tiles[0].shape, 1)
    last = jnp.where(lane < 64, turn(tiles[1], 64), turn(tiles[2], 96))
    return [*tiles, jnp.where(lane < 32, turn(tiles[0], 32), last)]


def two_columns(work, k):
    return cat([work[column(k), :], work[column(k + 1), :]], 1)


def fused(
    base_hbm, state_hbm, cutoff_hbm, wave_ref, wide_hbm, narrow_hbm, out_base, out_state,
    base_v, state_v, near_base, near_state, cutoff_ref, wz_v, wy_v, pd_v, xt, xs, xb, yb_v, zb_v,
    w0, w1, w2, wa, wb, wc, wd, held_coupled, own, share, other, partner, g, f,
    base_send, base_recv, base_sum, state_send, state_recv, local_sem, near_send, near_recv, share_send, share_recv, pass_send, pass_recv,
    base_send_sem, base_recv_sem, sum_send, sum_recv, state_send_sem, state_recv_sem,
):
    side = lax.axis_index("comp")
    slab = lax.axis_index("slab")
    seg = lax.axis_index("seg")
    segs = lax.axis_size("seg")
    far = {"slab": 1 - slab}
    twin = {"comp": 1 - side}
    after, before = lax.rem(seg + 1, segs), lax.rem(seg + segs - 1, segs)
    half = near_base.shape[1]
    quarter = N * N // 4

    def local(index, src, dst):
        return pltpu.make_async_copy(src, dst, local_sem.at[index])

    def remote(src, dst, send, recv, device):
        return pltpu.make_async_remote_copy(
            src_ref=src, dst_ref=dst, send_sem=send, recv_sem=recv, device_id=device,
            device_id_type=pl.DeviceIdType.MESH,
        )

    barrier = pltpu.get_barrier_semaphore()
    for device in (far, twin, {"seg": after}, {"seg": before}):
        pl.semaphore_signal(
            barrier, inc=1, device_id=device, device_id_type=pl.DeviceIdType.MESH
        )

    def quarter_of(ref, i):
        return ref.at[:, :, pl.ds(i * quarter, quarter)]

    wide_places, narrow_places = table_places()

    def table_part(hbm, entry, index, dst):
        start, rows = entry
        return hbm.at[pl.ds(start + rows * index, rows)], dst

    cut_copy = local(13, cutoff_hbm, cutoff_ref)
    cut_copy.start()
    wz_copy = local(0, *table_part(wide_hbm, wide_places[0], 0, wz_v))
    base_copies = [
        local(1 + i, quarter_of(base_hbm, i), quarter_of(base_v, i)) for i in range(4)
    ]
    wy_copy = local(5, *table_part(wide_hbm, wide_places[1], 0, wy_v))
    state_copy = local(6, state_hbm, state_v)
    late_copies = [
        local(7, *table_part(narrow_hbm, narrow_places[0], slab, pd_v)),
        local(8, *table_part(wide_hbm, wide_places[2], 0, yb_v)),
        local(9, *table_part(wide_hbm, wide_places[3], 0, zb_v)),
        local(10, *table_part(wide_hbm, wide_places[4], slab, xt)),
        local(11, *table_part(narrow_hbm, narrow_places[1], slab, xs)),
        local(12, *table_part(narrow_hbm, narrow_places[2], 2 * slab + side, xb)),
    ]
    for copy in (wz_copy, *base_copies, wy_copy, state_copy):
        copy.start()

    near_copies = [
        remote(
            state_hbm, near_state, near_send.at[0], near_recv.at[0],
            {"seg": jnp.where(side == 0, before, after)},
        ),
        remote(
            base_hbm.at[:, pl.ds(half * side, half), :], near_base, near_send.at[1],
            near_recv.at[1], {"seg": before},
        ),
    ]
    cut_copy.wait()
    cut_x, cut_y, cut_z = (cutoff_ref[i] for i in range(3))
    at_x, at_y, at_z = (jnp.clip(cut - LOW, 0, THIRD - LOW) for cut in (cut_x, cut_y, cut_z))

    def back_table(ref, kind, depth):
        return ref[2 * kind : 2 * kind + 2].reshape(4 * MP, 3 * LANES)[: 2 * N, :depth]

    wz = lambda kind: wz_v[2 * at_z + kind]
    wy = lambda kind: wy_v[2 * at_y + kind]
    yb = lambda kind: back_table(yb_v, kind, 6 * MP)
    zb = lambda kind: back_table(zb_v, kind, 12 * KP)

    def base_ahead_z(p):
        w0[pair_rows(p), :] = left3(wz(0), wide_rows(flat(base_v[:, :, lanes(p)])), NT)

    wz_copy.wait()
    for i, copy in enumerate(base_copies):
        copy.wait()
        loop(PAIRS // 4, Z1, lambda p, i=i: base_ahead_z(p + i * (PAIRS // 4)))
        if i == 0:
            pl.semaphore_wait(barrier, 4)
            for near_copy in near_copies:
                near_copy.start()
    for copy in late_copies:
        copy.start()
    wy_copy.wait()

    def base_planes(q):
        planes = []
        for j in (0, 2):
            both_planes = left3(wy(0), two_columns(w0, 4 * q + j), NN)
            planes += [both_planes[:, :LANES], both_planes[:, LANES:]]
        for i in range(4):
            own[4 * q + i] = planes[i]
        return planes

    share_copies = []
    for t in range(SIDE_QUADS):
        for i, tile in enumerate(pack_share(base_planes(SIDE_QUADS * side + t))):
            share[3 * t + i] = tile
        rows = pl.ds(3 * t, 3)
        copy = remote(
            share.at[rows], other.at[rows], share_send.at[t], share_recv.at[t], far
        )
        copy.start()
        share_copies.append(copy)
    for t in range(SIDE_QUADS):
        base_planes(SIDE_QUADS * (1 - side) + t)

    pass_copies = []

    def pass_on(t):
        share_copies[t].wait_recv()
        rows = pl.ds(3 * t, 3)
        copy = remote(
            other.at[rows], partner.at[rows], pass_send.at[t], pass_recv.at[t], twin
        )
        copy.start()
        pass_copies.append(copy)

    state_copy.wait()
    scale = sign_step()

    def flux_z(t):
        first, second = [], []
        for i in range(2):
            p = 2 * t + i
            state = state_v[:, :, lanes(p)]
            scaled = state * scale
            f0, f1, f2 = (flat(scaled * base_v[j, :, lanes(p)][None]) for j in range(3))
            plain = left3(wz(0), wide_rows(flat(state), f0), NT)
            wa[pair_rows(p), :] = plain[:, :LANES]
            wc[pair_rows(p), :] = plain[:, LANES:]
            first.append(f1)
            second.append(f2)
        along_y = left3(wz(0), wide_rows(*first), NT)
        along_z = left3(wz(1), wide_rows(*second), NT)
        for i in range(2):
            p = 2 * t + i
            mine = slice(i * LANES, (i + 1) * LANES)
            wb[pair_rows(p), :] = along_y[:, mine]
            wa[pair_rows(p), :] += along_z[:, mine]

    for copy in late_copies:
        copy.wait()

    def back_y(ref, place, t):
        q = SIDE_QUADS * place + t
        planes = unpack_share([ref[3 * t + i] for i in range(3)])
        deep = []
        for i in range(4):
            own_high, own_low = split(own[4 * q + i])
            far_high, far_low = split(planes[i])
            deep.append(cat([own_high, own_low, far_high, far_low, own_high, far_high], 1))
        filtered = matmul(cat(deep, 0), cat([pd_v[2 * at_x], pd_v[2 * at_x + 1]], 0))
        kinds = [filtered[96 * i : 96 * (i + 1)] for i in range(4)]
        for j in (0, 2):
            along = left3(yb(1), cat([kinds[j][:, :LANES], kinds[j + 1][:, :LANES]], 1), NN)
            for i in range(2):
                k = 4 * q + j + i
                whole = left3(yb(0), kinds[j + i], NN)
                w2[column(k), :] = whole[:, :LANES]
                w0[column(k), :] = whole[:, LANES:]
                w1[column(k), :] = along[:, i * LANES : (i + 1) * LANES]

    loop(FLUX_FIRST, 4, flux_z)
    pass_on(0)
    back_y(other, side, 0)
    loop(PAIRS // 2 - FLUX_FIRST, 4, lambda t: flux_z(t + FLUX_FIRST))
    pass_on(1)
    back_y(other, side, 1)
    pass_copies[0].wait_recv()
    back_y(partner, 1 - side, 0)
    pass_on(2)
    back_y(other, side, 2)
    for t in (1, 2):
        pass_copies[t].wait_recv()
        back_y(partner, 1 - side, t)

    tangent = side == 0
    wave = wave_ref[0]

    def force(p):
        lane = lax.broadcasted_iota(jnp.int32, (1, LANES), 1)
        y = 2 * p + jnp.where(lane < 64, 0, 1)
        return forcing_amp * quarter_sine(lax.rem(wave * y, N))

    def grid_space(t):
        third = left3(
            zb(1), cat([w2[pair_rows(2 * t + i), :] for i in range(2)], 1), NN
        ).T
        driven_pair = []
        for i in range(2):
            p = 2 * t + i
            state = state_v[:, :, lanes(p)]
            base = base_v[:, :, lanes(p)]
            pair = left3(zb(0), cat([w0[pair_rows(p), :], w1[pair_rows(p), :]], 1), NN).T
            grad = [
                pair[:96].reshape(base.shape),
                pair[LANES : LANES + 96].reshape(base.shape),
                third[i * LANES : i * LANES + 96].reshape(base.shape),
            ]
            coupled, driven = [], []
            for a in range(3):
                total = 0.0
                drive = 0.0
                for b in range(3):
                    total = total + jnp.where(tangent, grad[b][a], grad[a][b]) * state[b]
                    drive = drive + grad[b][a] * base[b]
                if a == 0:
                    drive = drive - force(p)
                coupled.append(-time_step * total)
                driven.append(base[a] - time_step * drive)
            held_coupled[:, lanes(p)] = cat(coupled, 0)
            driven_pair.append(cat(driven, 0))
        out = left3(wz(0), wide_rows(*driven_pair), NT)
        for i in range(2):
            wd[pair_rows(2 * t + i), :] = out[:, i * LANES : (i + 1) * LANES]

    loop(PAIRS // 2, 4, grid_space)

    waves = plane_waves()
    keep = jnp.where(jnp.abs(waves[0]) <= cut_x.astype(f32), 1.0, 0.0)

    def ahead_deep(plane):
        high, low = split(plane)
        return [high[:MP], low[:MP], high[MP:], low[MP:], high[:MP], high[MP:]]

    row = lax.broadcasted_iota(jnp.int32, (MP, LANES), 0)
    upper = row > THIRD
    folded = jnp.where(upper, 0.0, jnp.where(row == 0, 1.0, 2.0))

    def emit_planes(ref, start, first_k, modes, count, fold):
        new = []
        for i in range(count):
            w = projected(waves, modes[MP * i : MP * (i + 1)], first_k + i)
            new.append([keep * part for part in w])
        if fold is not None:
            held = jnp.where(upper, pltpu.roll(new[0][2], THIRD + 1, 0), new[0][0])
            new[0][0] = jnp.where(fold, held, new[0][0])
        tiles = []
        for j in range(0, count, 2):
            tiles += pack_pair(new[j], new[j + 1])
        rows = QUAD_ROWS if count == 4 else PAIR_ROWS
        ref[start : start + rows, :] = pack_quad(tiles)

    def base_copy(t, rows):
        rows = pl.ds(QUAD_ROWS * t, rows)
        return remote(
            base_send.at[rows], base_recv.at[rows], base_send_sem.at[t], base_recv_sem.at[t],
            far,
        )

    def each_side(copies, act):
        if len(copies) == 1:
            act(copies[0])
        else:
            pl.when(side == 0)(lambda: act(copies[0]))
            pl.when(side == 1)(lambda: act(copies[1]))

    base_copies = []
    for t in range(SIDE_QUADS):
        q = SIDE_QUADS * side + t
        deep = []
        for j in (0, 2):
            both_planes = left3(wy(0), two_columns(wd, 4 * q + j), NN)
            for i in range(2):
                deep.append(cat(ahead_deep(both_planes[:, i * LANES : (i + 1) * LANES]), 1))
        modes = matmul(cat(deep, 0), flat(xt[:8]))
        emit_planes(base_send, QUAD_ROWS * t, 4 * q, modes, 4, side == 0 if t == 0 else None)
        copies = [base_copy(t, QUAD_ROWS)]
        if t == SIDE_QUADS - 1:
            copies.append(base_copy(t, PAIR_ROWS))
        base_copies.append(copies)
        each_side(copies, lambda copy: copy.start())

    def flux_y(t):
        k = 2 * t
        extra = left3(wy(1), two_columns(wb, k), NN)
        for i in range(2):
            whole = left3(
                wy(0), cat([wa[column(k + i), :], wc[column(k + i), :]], 1), NN
            )
            g[k + i] = whole[:, :LANES] + extra[:, i * LANES : (i + 1) * LANES]
            f[k + i] = whole[:, LANES:]

    loop(QK // 2, 4, flux_y)

    def coupled_z(t):
        rows = [held_coupled[:, lanes(2 * t + i)] for i in range(2)]
        out = left3(wz(0), wide_rows(*rows), NT)
        for i in range(2):
            wa[pair_rows(2 * t + i), :] = out[:, i * LANES : (i + 1) * LANES]

    loop(PAIRS // 2, 4, coupled_z)

    state_copies = []
    for q in range(STATE_QUADS):
        pairs = 2 if q < STATE_QUADS - 1 else 1
        deep = []
        for j in range(0, 2 * pairs, 2):
            both_planes = left3(wy(0), two_columns(wa, 4 * q + j), NN)
            for i in range(2):
                k = 4 * q + j + i
                total = g[k] + both_planes[:, i * LANES : (i + 1) * LANES]
                deep.append(cat(ahead_deep(total) + ahead_deep(f[k]), 1))
        modes = matmul(cat(deep, 0), flat(xt[...]))
        fold = True if q == 0 else None
        emit_planes(state_send, QUAD_ROWS * q, 4 * q, modes, 2 * pairs, fold)
        rows = pl.ds(QUAD_ROWS * q, QUAD_ROWS if pairs == 2 else PAIR_ROWS)
        copy = remote(
            state_send.at[rows], state_recv.at[rows], state_send_sem.at[q],
            state_recv_sem.at[q], far,
        )
        copy.start()
        state_copies.append(copy)

    def spectral(held, fold, first_k, table_ref, work):
        tiles = unpack_quad(held)
        deep = []
        wave_x, wave_y = waves
        for j in range(len(tiles) // 3):
            for i, (m0, m1) in enumerate(unpack_pair(tiles[3 * j : 3 * j + 3])):
                k = jnp.asarray(first_k + 2 * j + i, jnp.int32)
                inverse = 1.0 / jnp.maximum(k, 1).astype(f32)
                m2 = -(wave_x * m0 + wave_y * m1) * inverse
                if fold is not None and i == 0 and j == 0:
                    third = pltpu.roll(m0, MP - THIRD - 1, 0)
                    m2 = jnp.where(fold, folded * third, m2)
                    m0 = jnp.where(fold, folded * m0, m0)
                    m1 = jnp.where(fold, folded * m1, m1)
                high, low = split(cat([m0, m1, m2], 1))
                deep.append(cat([high, low, high], 1))
        rows = matmul(cat(deep, 0), flat(table_ref[...]))
        planes = []
        for i in range(len(deep)):
            mine = rows[MP * i : MP * (i + 1)]
            planes.append(cat([mine[:, :LANES], mine[:, LANES:]], 0))
        for j in range(0, len(deep), 2):
            out = left3(yb(0), cat(planes[j : j + 2], 1), NN)
            for i in range(2):
                work[column(first_k + j + i), :] = out[:, i * LANES : (i + 1) * LANES]

    span = base_sum.shape[0] // 2
    sum_copies = []
    for t in range(SIDE_QUADS):
        each_side(base_copies[t], lambda copy: copy.wait_recv())
        mine = slice(QUAD_ROWS * t, QUAD_ROWS * (t + 1))
        total = base_send[mine, :] + base_recv[mine, :]
        if t == SIDE_QUADS - 1:
            place = lax.broadcasted_iota(jnp.int32, total.shape, 0)
            total = jnp.where((side == 0) | (place < PAIR_ROWS), total, 0.0)
        rows = pl.ds(pl.multiple_of(span * side + QUAD_ROWS * t, 8), QUAD_ROWS)
        base_sum[rows, :] = total
        copy = remote(
            base_sum.at[rows], base_sum.at[rows], sum_send.at[t], sum_recv.at[t], twin
        )
        copy.start()
        sum_copies.append(copy)

    def base_back(place, t):
        rows = pl.ds(pl.multiple_of(span * place + QUAD_ROWS * t, 8), QUAD_ROWS)
        fold = place == 0 if t == 0 else None
        spectral(base_sum[rows, :], fold, 4 * (SIDE_QUADS * place + t), xb, w0)

    for t in range(SIDE_QUADS):
        base_back(side, t)
    for t in range(SIDE_QUADS):
        sum_copies[t].wait_recv()
        base_back(1 - side, t)

    def finish_base(p):
        rows = left3(zb(0), w0[pair_rows(p), :], NN).T
        out_base[:, :, lanes(p)] = rows[:48].reshape(3, half, LANES)

    loop(PAIRS, 8, finish_base)

    for q in range(STATE_QUADS):
        state_copies[q].wait_recv()
        rows = QUAD_ROWS if q < STATE_QUADS - 1 else PAIR_ROWS
        mine = slice(QUAD_ROWS * q, QUAD_ROWS * q + rows)
        total = state_send[mine, :] + state_recv[mine, :]
        spectral(total, True if q == 0 else None, 4 * q, xs, wc)

    def finish_state(p):
        rows = left3(zb(0), wc[pair_rows(p), :], NN).T
        near = near_state[:, :, lanes(p)]
        out_state[:, :, lanes(p)] = rows[:96].reshape(near.shape) - near

    near_copies[0].wait_recv()
    loop(PAIRS, 8, finish_state)

    def base_difference(i):
        span = pl.ds(pl.multiple_of(i * 512, 512), 512)
        out_base[:, :, span] -= near_base[:, :, span]

    near_copies[1].wait_recv()
    loop(N * N // 512, 4, base_difference)

    sent = near_copies + share_copies + pass_copies + sum_copies + state_copies
    for copy in sent:
        copy.wait_send()
    for copies in base_copies:
        each_side(copies, lambda copy: copy.wait_send())


def copy_out(base_v, state_v, base_hbm, state_hbm, sem):
    copies = [
        pltpu.make_async_copy(base_v, base_hbm, sem.at[0]),
        pltpu.make_async_copy(state_v, state_hbm, sem.at[1]),
    ]
    for copy in copies:
        copy.start()
    for copy in copies:
        copy.wait()


def write_out(*fields):
    return pl.pallas_call(
        copy_out,
        out_shape=[jax.ShapeDtypeStruct(field.shape, f32) for field in fields],
        in_specs=[pl.BlockSpec(memory_space=pltpu.VMEM)] * 2,
        out_specs=[pl.BlockSpec(memory_space=pltpu.HBM)] * 2,
        scratch_shapes=[pltpu.SemaphoreType.DMA((2,))],
        compiler_params=pltpu.CompilerParams(vmem_limit_bytes=2**20),
    )(*fields)


def fused_body(base, state, wavenumber, cutoff):
    base, state = base[0], state[0, 0]
    rows = base.shape[1]
    half = rows // lax.axis_size("comp")
    slabs = lax.axis_size("slab")
    tables = [jnp.asarray(np.concatenate(group)) for group in table_groups()]
    hbm = pl.BlockSpec(memory_space=pltpu.HBM)
    smem = pl.BlockSpec(memory_space=pltpu.SMEM)
    vmem = lambda *shape: pltpu.VMEM(shape, f32)
    dma = lambda count: pltpu.SemaphoreType.DMA((count,))
    wide, narrow = table_places()
    wz, wy, yb, zb, xt = (pltpu.VMEM((entry[1], 2 * MP, 3 * LANES), bf16) for entry in wide)
    pd, xs, xb = (pltpu.VMEM((entry[1], 3 * LANES, 2 * LANES), bf16) for entry in narrow)
    work = vmem(2 * N * KP, LANES)
    share = vmem(3 * SIDE_QUADS, 2 * BODY + 8, LANES)
    planes = vmem(QK, 2 * MP, LANES)
    base_tiles = vmem(SIDE_QUADS * QUAD_ROWS, LANES)
    state_tiles = vmem((STATE_QUADS - 1) * QUAD_ROWS + PAIR_ROWS, LANES)
    base_half = vmem(3, half, N * N)
    whole = vmem(3, rows, N * N)
    scratch = [
        whole, whole, base_half, whole, pltpu.SMEM((3,), jnp.int32), wz, wy, pd, xt, xs, xb, yb, zb,
        *[work] * 7, vmem(3 * rows, N * N), planes, share, share, share, planes, planes,
        base_tiles, base_tiles, vmem(2 * SIDE_QUADS * QUAD_ROWS, LANES), state_tiles, state_tiles,
        dma(14), dma(2), dma(2), *[dma(SIDE_QUADS)] * 8, *[dma(STATE_QUADS)] * 2,
    ]
    base_gap, state_gap = pl.pallas_call(
        fused,
        out_shape=[
            jax.ShapeDtypeStruct((3, half, N * N), f32),
            jax.ShapeDtypeStruct((3, rows, N * N), f32),
        ],
        in_specs=[hbm, hbm, hbm, smem, hbm, hbm],
        out_specs=[pl.BlockSpec(memory_space=pltpu.VMEM)] * 2,
        scratch_shapes=scratch,
        compiler_params=pltpu.CompilerParams(
            vmem_limit_bytes=51 * 2**20, collective_id=0, has_side_effects=True
        ),
        cost_estimate=pl.CostEstimate(flops=10**10, bytes_accessed=10**7, transcendentals=0),
    )(base, state, cutoff, wavenumber, *tables)
    base_gap, state_gap = write_out(base_gap, state_gap)
    return base_gap[None], state_gap[None, None]


def solution(mesh):
    sizes = dict(mesh.shape)
    one_kernel = sizes["slab"] == 2 and sizes["comp"] == 2 and sizes["seg"] > 1
    return jax.shard_map(
        fused_body if one_kernel else body,
        mesh=mesh,
        in_specs=(
            P(("groups", "seg"), None, "slab", None),
            P(("groups", "seg"), "comp", None, "slab", None),
            P("groups"),
            P("groups"),
        ),
        out_specs=(
            P(("groups", "seg"), None, ("slab", "comp"), None),
            P(("groups", "seg"), "comp", None, "slab", None),
        ),
        check_vma=False,
    )
```

```python
import functools

import jax
import jax.numpy as jnp
import ml_dtypes
import numpy as np
from jax import lax
from jax.experimental import pallas as pl
from jax.experimental.pallas import tpu as pltpu
from jax.sharding import PartitionSpec as P

N = 64
BACK, GRID, AHEAD, SPEC, Z1, Z2, Z3, Y1 = 4, 4, 4, 4, 8, 4, 8, 6
THIRD = N // 3
LOW = THIRD - 3
KZ = THIRD + 1
KP = 24
MP = 48
PAIRS = N // 2
FLUX = 14 * 10**9
HALF = KZ // 2
viscosity = 0.025
time_step = 0.02
forcing_amp = 10.0
f32 = jnp.float32
bf16 = jnp.bfloat16

NN = (((1,), (0,)), ((), ()))
NT = (((1,), (1,)), ((), ()))


def split(value):
    high = value.astype(bf16)
    return high, (value - high.astype(f32)).astype(bf16)


def dot3(left, right, dims):
    dot = functools.partial(lax.dot_general, dimension_numbers=dims, preferred_element_type=f32)
    return dot(left[0], right[0]) + (dot(left[0], right[1]) + dot(left[1], right[0]))


def table(values):
    values = np.asarray(values, np.float32)
    high = values.astype(ml_dtypes.bfloat16)
    low = (values - high.astype(np.float32)).astype(ml_dtypes.bfloat16)
    return np.stack([high, low], axis=-3)


def table3(values):
    high, low = np.moveaxis(table(values), -3, 0)
    return np.concatenate([high, high, low], axis=-1)


def left3(left, value, dims):
    high, low = split(value)
    deep = jnp.concatenate([high, low, high], axis=dims[0][1][0])
    return lax.dot_general(left, deep, dimension_numbers=dims, preferred_element_type=f32)


def signed():
    m = np.arange(2 * THIRD + 1)
    return np.where(m <= THIRD, m, m - (2 * THIRD + 1))


def angles(first, second):
    return np.mod(np.outer(first, second), N) * (2 * np.pi / N)


def cuts():
    return range(LOW, THIRD + 1)


def z_tables():
    plain, ik = [], []
    k = np.arange(KZ)
    a = angles(k, np.arange(N))
    for cut in cuts():
        keep = 1.0 * (k <= cut)[:, None]
        w = np.zeros((2, KP, N))
        v = np.zeros((2, KP, N))
        w[0, :KZ], w[1, :KZ] = keep * np.cos(a), -keep * np.sin(a)
        v[0, :KZ], v[1, :KZ] = keep * k[:, None] * np.sin(a), keep * k[:, None] * np.cos(a)
        plain.append(np.kron(np.eye(2), w.reshape(2 * KP, N)))
        ik.append(np.kron(np.eye(2), v.reshape(2 * KP, N)))
    return table3(np.stack([np.stack(plain), np.stack(ik)], axis=1))


def y_tables():
    out = []
    m = signed()
    count = len(m)
    a = angles(m, np.arange(N))
    for cut in cuts():
        keep = 1.0 * (np.abs(m) <= cut)[:, None]
        c, s = keep * np.cos(a), keep * np.sin(a)
        w = np.zeros((2, MP, N, 2))
        w[0, :count, :, 0], w[0, :count, :, 1] = c, s
        w[1, :count, :, 0], w[1, :count, :, 1] = -s, c
        v = np.zeros_like(w)
        v[0, :count] = -m[:, None, None] * w[1, :count]
        v[1, :count] = m[:, None, None] * w[0, :count]
        out.append(np.stack([w.reshape(2 * MP, 2 * N), v.reshape(2 * MP, 2 * N)]))
    return table3(np.stack(out))


def y_back():
    m = signed()
    count = len(m)
    a = angles(np.arange(N), m)
    c, s = np.cos(a) / N, np.sin(a) / N
    w = np.zeros((N, 2, 2, MP))
    w[:, 0, 0, :count], w[:, 0, 1, :count] = c, -s
    w[:, 1, 0, :count], w[:, 1, 1, :count] = s, c
    v = np.zeros_like(w)
    v[:, :, 0, :count] = m * w[:, :, 1, :count]
    v[:, :, 1, :count] = -m * w[:, :, 0, :count]
    return table3(np.stack([w.reshape(2 * N, 2 * MP), v.reshape(2 * N, 2 * MP)]))


def z_back():
    k = np.arange(KZ)
    a = angles(k, np.arange(N))
    weight = (np.where(k == 0, 1.0, 2.0) / N)[:, None]
    w = np.zeros((2, KP, N))
    w[0, :KZ], w[1, :KZ] = weight * np.cos(a), -weight * np.sin(a)
    v = np.zeros_like(w)
    v[0, :KZ] = k[:, None] * w[1, :KZ]
    v[1, :KZ] = -k[:, None] * w[0, :KZ]
    pair = lambda t: np.kron(np.eye(2), t.reshape(2 * KP, N))
    return table3(np.stack([pair(w).T, pair(v).T]))


def x_filters(slabs):
    rows = N // slabs
    out = []
    x = np.arange(N)
    for cut in cuts():
        n = np.arange(-cut, cut + 1)
        d = np.mod(x[:, None] - x[None, :], N)
        phase = 2 * np.pi / N * n[:, None, None] * -d
        plain = np.cos(phase).sum(0) / N
        deriv = (-n[:, None, None] * np.sin(phase)).sum(0) / N
        both = np.stack([plain, deriv]).reshape(2, slabs, rows, slabs, rows)
        wide = np.zeros((slabs, 2, slabs, 3, rows, 3, rows))
        for i in range(3):
            wide[:, :, :, i, :, i, :] = both.transpose(3, 0, 1, 2, 4)
        out.append(wide.reshape(slabs, 2, slabs, 3 * rows, 3 * rows))
    return table(np.stack(out))


def x_tables(slabs):
    rows = N // slabs
    n = signed()
    count = len(n)
    a = angles(np.arange(N), n).reshape(slabs, rows, count)
    out = []
    for cut in cuts():
        keep = 1.0 * (np.abs(n) <= cut)
        c, s = np.cos(a) * keep, np.sin(a) * keep
        w = np.zeros((slabs, 2, 2, 3, rows, 3, 2, 64))
        for i in range(3):
            w[:, 0, 0, i, :, i, 0, :count] = c
            w[:, 0, 0, i, :, i, 1, :count] = -s
            w[:, 0, 1, i, :, i, 0, :count] = s
            w[:, 0, 1, i, :, i, 1, :count] = c
        w[:, 1, :, :, :, :, 0, :count] = -n * w[:, 0, :, :, :, :, 1, :count]
        w[:, 1, :, :, :, :, 1, :count] = n * w[:, 0, :, :, :, :, 0, :count]
        out.append(w.reshape(slabs, 2, 2, 3 * rows, 384))
    return table(np.stack(out))


def x_back(slabs):
    rows = N // slabs
    n = signed()
    count = len(n)
    a = angles(n, np.arange(N)).reshape(count, slabs, rows).transpose(1, 0, 2)
    c, s = np.cos(a) / N, np.sin(a) / N
    w = np.zeros((slabs, 2, 3, 2, 64, 3, rows))
    for i in range(3):
        w[:, 0, i, 0, :count, i] = c
        w[:, 0, i, 1, :count, i] = -s
        w[:, 1, i, 0, :count, i] = s
        w[:, 1, i, 1, :count, i] = c
    return table(w.reshape(slabs, 2, 384, 3 * rows))


def both(ref, *index):
    return ref[(*index, 0)], ref[(*index, 1)]


def lanes(p):
    return pl.ds(pl.multiple_of(p * 128, 128), 128)


def pair_rows(p):
    return pl.ds(pl.multiple_of(p * 4 * KP, 8), 4 * KP)


def column(k):
    return pl.ds(k, 2 * N, stride=KP)


def flat(block):
    return block.reshape(block.shape[0] * block.shape[1], block.shape[2])


def loop(count, unroll, step):
    def go(i, carry):
        step(i)
        return carry

    lax.fori_loop(0, count, go, 0, unroll=unroll)


def clear_padding(*works):
    for k in range(KZ, KP):
        for work in works:
            work[column(k), :] = jnp.zeros((2 * N, work.shape[1]), f32)


def base_ahead(base_ref, wz_ref, wy_ref, out_ref, half_ref, work):
    def along_z(p):
        work[pair_rows(p), :] = left3(wz_ref[0], flat(base_ref[:, :, lanes(p)]), NT)

    loop(PAIRS, Z1, along_z)

    def along_y(k):
        out_ref[k] = left3(wy_ref[0], work[column(k), :], NN)

    loop(KZ, Y1, along_y)
    first = HALF * lax.axis_index("comp")

    def share(j):
        half_ref[j] = out_ref[first + j]

    loop(HALF, 1, share)


def sign_step():
    return jnp.where(lax.axis_index("comp") == 0, -time_step, time_step).astype(f32)


def flux_ahead(base_ref, state_ref, wz_ref, wy_ref, g_ref, work_a, work_b):
    scale = sign_step()

    def along_z(p):
        state = state_ref[:, :, lanes(p)]
        scaled = state * scale
        f1, f2 = (flat(scaled * base_ref[j, :, lanes(p)][None]) for j in (1, 2))
        plain = wz_ref[0]
        work_a[pair_rows(p), :] = left3(plain, flat(state), NT) + left3(wz_ref[1], f2, NT)
        work_b[pair_rows(p), :] = left3(plain, f1, NT)

    loop(PAIRS, Z2, along_z)

    def along_y(k):
        g_ref[k] = left3(wy_ref[0], work_a[column(k), :], NN) + left3(
            wy_ref[1], work_b[column(k), :], NN
        )

    loop(KZ, Y1, along_y)


def flux_x_ahead(base_ref, state_ref, wz_ref, wy_ref, f_ref, work):
    scale = sign_step()

    def along_z(p):
        f0 = flat(state_ref[:, :, lanes(p)] * scale * base_ref[0, :, lanes(p)][None])
        work[pair_rows(p), :] = left3(wz_ref[0], f0, NT)

    loop(PAIRS, Z2, along_z)

    def along_y(k):
        f_ref[k] = left3(wy_ref[0], work[column(k), :], NN)

    loop(KZ, Y1, along_y)


def gradients(
    slabs, count, *refs,
):
    got, rest = refs[:count], refs[count:]
    side = lax.axis_index("comp")
    if count == 1:
        visits = [(lambda j: (j, [got[0][s, j] for s in range(slabs)]), KZ)]
    else:
        own, mine, partner = got

        def visit(ref, first):
            return lambda j: (first + j, [own[first + j], ref[j]])

        visits = [
            (visit(mine, HALF * side), HALF),
            (visit(partner, HALF * (1 - side)), HALF),
        ]
    gradients_of(slabs, visits, *rest)


def gradients_of(
    slabs, visits, base_ref, state_ref, force_ref, pd_ref, yb_ref, zb_ref, wz_ref, wy_ref,
    xt_ref, base_out_ref, coupled_ref, work_0, work_1, work_2,
):
    tangent = lax.axis_index("comp") == 0

    def back_y(visit, j):
        k, sources = visit(j)
        sources = [split(source) for source in sources]

        def across(kind):
            total = dot3(sources[0], both(pd_ref, kind, 0), NN)
            for s in range(1, slabs):
                total = total + dot3(sources[s], both(pd_ref, kind, s), NN)
            return total

        plain, deriv = across(0), across(1)
        work_0[column(k), :] = left3(yb_ref[0], deriv, NN)
        work_1[column(k), :] = left3(yb_ref[1], plain, NN)
        work_2[column(k), :] = left3(yb_ref[0], plain, NN)

    clear_padding(work_0, work_1, work_2)
    for visit, count in visits:
        loop(count, BACK, functools.partial(back_y, visit))

    def grid_space(p):
        state = state_ref[:, :, lanes(p)]
        base = base_ref[:, :, lanes(p)]
        grad = []
        for work, kind in ((work_0, 0), (work_1, 0), (work_2, 1)):
            rows = left3(zb_ref[kind], work[pair_rows(p), :], NN).T
            grad.append(rows.reshape(base.shape))
        coupled, driven = [], []
        for i in range(3):
            total = 0.0
            drive = 0.0
            for j in range(3):
                total = total + jnp.where(tangent, grad[j][i], grad[i][j]) * state[j]
                drive = drive + grad[j][i] * base[j]
            if i == 0:
                drive = drive - force_ref[:, lanes(p)]
            coupled.append(-time_step * total)
            driven.append(base[i] - time_step * drive)
        plain = wz_ref[0]
        coupled_ref[pair_rows(p), :] = left3(plain, jnp.concatenate(coupled, axis=0), NT)
        work_1[pair_rows(p), :] = left3(plain, jnp.concatenate(driven, axis=0), NT)

    loop(PAIRS, GRID, grid_space)

    waves = plane_waves()
    first = HALF * lax.axis_index("comp")

    def base_ahead_x(step):
        j = HALF - 1 - step
        k = first + j
        driven = left3(wy_ref[0], work_1[column(k), :], NN)
        modes = 0.0
        for d in range(2):
            rows = slice(d * MP, (d + 1) * MP)
            modes = modes + dot3(split(driven[rows]), both(xt_ref, 0, d), NN)
        emit(waves, base_out_ref, j, HALF, modes, k)

    loop(HALF, AHEAD, base_ahead_x)


def emit(waves, ref, slot, last, modes, k):
    new = projected(waves, modes, k)
    ref[slot] = jnp.concatenate(new[:2], axis=1)
    ref[last] = jnp.concatenate([new[2], jnp.zeros_like(new[2])], axis=1)


def state_ahead_x(coupled_ref, wy_ref, xt_ref, g_ref, f_ref, out_ref):
    waves = plane_waves()

    def ahead_x(step):
        k = KZ - 1 - step
        total = g_ref[k] + left3(wy_ref[0], coupled_ref[column(k), :], NN)
        outer = f_ref[k]
        modes = 0.0
        for d in range(2):
            rows = slice(d * MP, (d + 1) * MP)
            modes = modes + dot3(split(total[rows]), both(xt_ref, 0, d), NN)
            modes = modes + dot3(split(outer[rows]), both(xt_ref, 1, d), NN)
        emit(waves, out_ref, k, KZ, modes, k)

    loop(KZ, AHEAD, ahead_x)


def plane_waves():
    column_n = lax.rem(lax.broadcasted_iota(jnp.int32, (MP, 128), 1), 64)
    row_m = lax.broadcasted_iota(jnp.int32, (MP, 128), 0)
    wrap = lambda v: jnp.where(v <= THIRD, v, v - (2 * THIRD + 1)).astype(f32)
    return wrap(column_n), wrap(row_m)


def projected(waves, modes, k):
    wave_x, wave_y = waves
    wave_z = jnp.asarray(k, jnp.int32).astype(f32)
    square = wave_x * wave_x + wave_y * wave_y + wave_z * wave_z
    safe = jnp.where(square > 0, square, 1.0)
    damping = 1.0 / (1.0 + viscosity * time_step * square)
    w = [modes[:, i * 128 : (i + 1) * 128] for i in range(3)]
    divergence = (wave_x * w[0] + wave_y * w[1] + wave_z * w[2]) / safe
    return [
        damping * (w[0] - wave_x * divergence),
        damping * (w[1] - wave_y * divergence),
        damping * (w[2] - wave_z * divergence),
    ]


def finish(count, halved, *refs):
    parts, (near_ref, xb_ref, yb_ref, zb_ref, out_ref, work) = refs[:count], refs[count:]
    wave_x, wave_y = plane_waves()
    clear_padding(work)

    def spectral(parts, first, last, j):
        k = first + j
        modes, third = 0.0, 0.0
        for part in parts:
            modes = modes + part[j]
            third = third + part[last, :, :128]
        w0, w1 = modes[:, :128], modes[:, 128:]
        whole = jnp.asarray(k, jnp.int32)
        inverse = 1.0 / jnp.maximum(whole, 1).astype(f32)
        w2 = jnp.where(whole == 0, third, -(wave_x * w0 + wave_y * w1) * inverse)
        new = split(jnp.concatenate([w0, w1, w2], axis=1))
        rows = [dot3(new, both(xb_ref, d), NN) for d in range(2)]
        work[column(k), :] = left3(yb_ref[0], jnp.concatenate(rows, axis=0), NN)

    if halved:
        side = lax.axis_index("comp")
        for part, place in zip(parts, (side, 1 - side)):
            loop(HALF, SPEC, functools.partial(spectral, [part], HALF * place, HALF))
    else:
        loop(KZ, SPEC, functools.partial(spectral, parts, 0, KZ))

    def along_z(p):
        rows = left3(zb_ref[0], work[pair_rows(p), :], NN).T
        near = near_ref[:, :, lanes(p)]
        out_ref[:, :, lanes(p)] = rows.reshape(near.shape) - near

    loop(PAIRS, Z3, along_z)


def call(kernel, out_shape, scratch, cost, *operands):
    return pl.pallas_call(
        kernel,
        out_shape=out_shape,
        in_specs=[pl.BlockSpec(memory_space=pltpu.VMEM)] * len(operands),
        out_specs=jax.tree.map(lambda _: pl.BlockSpec(memory_space=pltpu.VMEM), out_shape),
        scratch_shapes=scratch,
        compiler_params=pltpu.CompilerParams(vmem_limit_bytes=48 * 2**20),
        cost_estimate=pl.CostEstimate(flops=cost, bytes_accessed=2**10, transcendentals=0),
    )(*operands)


def body(base, state, wavenumber, cutoff):
    base, state = base[0], state[0, 0]
    slab_rows = base.shape[1]
    half = slab_rows // lax.axis_size("comp")
    slabs = lax.axis_size("slab")
    segs = lax.axis_size("seg")
    slab = lax.axis_index("slab")
    side = lax.axis_index("comp")
    width = 3 * slab_rows
    which = cutoff - LOW

    route = [((s, 0), ((s - 1) % segs, 0)) for s in range(segs)]
    route += [((s, 1), ((s + 1) % segs, 1)) for s in range(segs)]
    route = [(a * 2 + b, c * 2 + d) for (a, b), (c, d) in route]
    wz = lax.dynamic_index_in_dim(jnp.asarray(z_tables()), which[2], 0, False)
    wy = lax.dynamic_index_in_dim(jnp.asarray(y_tables()), which[1], 0, False)
    filters, ahead = jnp.asarray(x_filters(slabs)), jnp.asarray(x_tables(slabs))
    pick = lambda t: lax.dynamic_slice(
        t, (which[0], slab) + (0,) * (t.ndim - 2), (1, 1) + t.shape[2:]
    )[0, 0]
    pd, xt = pick(filters), pick(ahead)
    xb = lax.dynamic_index_in_dim(jnp.asarray(x_back(slabs)), slab, 0, False)
    yb, zb = jnp.asarray(y_back()), jnp.asarray(z_back())

    modes = jax.ShapeDtypeStruct((KZ, 2 * MP, width), f32)
    half_modes = jax.ShapeDtypeStruct((HALF, 2 * MP, width), f32)
    spectrum = jax.ShapeDtypeStruct((KZ + 1, MP, 256), f32)
    half_spectrum = jax.ShapeDtypeStruct((HALF + 1, MP, 256), f32)
    work = pltpu.VMEM((2 * N * KP, width), f32)
    own, share = call(base_ahead, (modes, half_modes), [work], 4 * 10**9, base, wz, wy)
    later, later_base, share = lax.optimization_barrier((state, base, share))
    near_state = lax.ppermute(later, ("seg", "comp"), route)
    base_half = lax.dynamic_slice_in_dim(later_base, side * half, half, 1)
    near_base = lax.ppermute(base_half, "seg", [((s + 1) % segs, s) for s in range(segs)])
    if slabs == 2:
        other = lax.ppermute(share, "slab", [(0, 1), (1, 0)])
        partner = lax.ppermute(other, "comp", [(0, 1), (1, 0)])
        first = slab == 0
        got = (own, other, partner)
        pd = jnp.where(first, pd, pd[:, ::-1])
    else:
        got = (lax.all_gather(own, "slab"),)
    g = call(flux_ahead, modes, [work] * 2, FLUX, base, state, wz, wy)
    f = call(flux_x_ahead, modes, [work], 10**9, base, state, wz, wy)

    *got, g, f = lax.optimization_barrier((*got, g, f))

    y = jnp.arange(N, dtype=jnp.int32)
    phase = jnp.mod(wavenumber[0] * y, N).astype(f32) * (2.0 * jnp.pi / N)
    force = jnp.repeat(forcing_amp * jnp.sin(phase), N)[None]
    lined = jax.ShapeDtypeStruct((2 * N * KP, width), f32)
    base_modes, coupled = call(
        functools.partial(gradients, slabs, len(got)), (half_spectrum, lined), [work] * 3,
        25 * 10**9, *got, base, state, force, pd, yb, zb, wz, wy, xt,
    )
    state_modes = call(state_ahead_x, spectrum, [], 3 * 10**9, coupled, wy, xt, g, f)
    near_state, near_base, state_modes = lax.optimization_barrier(
        (near_state, near_base, state_modes)
    )
    if slabs == 2:
        swap = lambda v: lax.ppermute(v, "slab", [(0, 1), (1, 0)])
        state_other = swap(state_modes)
        base_other, state_modes = lax.optimization_barrier((swap(base_modes), state_modes))
        base_sum = base_modes + base_other
        state_parts = (state_modes, state_other)
    else:
        base_sum = lax.psum(base_modes, "slab")
        state_parts = (lax.psum(state_modes, "slab"),)
    base_parts = (base_sum, lax.ppermute(base_sum, "comp", [(0, 1), (1, 0)]))

    shape = jax.ShapeDtypeStruct(base.shape, f32)
    last = functools.partial(finish, len(state_parts), False)
    last_base = functools.partial(finish, 2, True)
    near_wide = jnp.concatenate([near_base, near_base], axis=1)
    base_gap = call(last_base, shape, [work], 10**8, *base_parts, near_wide, xb, yb, zb)
    base_gap = lax.dynamic_slice_in_dim(base_gap, side * half, half, 1)
    state_gap = call(last, shape, [work], 10**10, *state_parts, near_state, xb, yb, zb)
    return base_gap[None], state_gap[None, None]


LANES = 128
QK = 24
SIDE_QUADS = 3
STATE_QUADS = 6
FLUX_FIRST = 12


def lane_pad(values, axis, size=LANES):
    pad = [(0, 0)] * values.ndim
    pad[axis] = (0, size - values.shape[axis])
    return np.pad(values, pad)


def halves(values):
    values = np.asarray(values, np.float32)
    high = values.astype(ml_dtypes.bfloat16)
    return high, (values - high.astype(np.float32)).astype(ml_dtypes.bfloat16)


def filter_tables(slabs):
    rows = N // slabs
    x = np.arange(N)
    out = []
    for cut in cuts():
        n = np.arange(-cut, cut + 1)
        d = np.mod(x[:, None] - x[None, :], N)
        phase = 2 * np.pi / N * n[:, None, None] * -d
        plain = np.cos(phase).sum(0) / N
        deriv = (-n[:, None, None] * np.sin(phase)).sum(0) / N
        both_kinds = np.stack([plain, deriv]).reshape(2, slabs, rows, slabs, rows)
        per_slab = []
        for slab in range(slabs):
            blocks = []
            for source in (slab, 1 - slab):
                wide = np.zeros((3, rows, 2, LANES))
                for i in range(3):
                    wide[i, :, :, i * rows : (i + 1) * rows] = both_kinds[
                        :, source, :, slab
                    ].transpose(1, 0, 2)
                blocks.append(halves(lane_pad(wide.reshape(3 * rows, 2 * LANES), 0)))
            (own_high, own_low), (far_high, far_low) = blocks
            per_slab.append(
                np.concatenate([own_high, own_high, far_high, far_high, own_low, far_low])
            )
        out.append(np.stack(per_slab))
    return np.stack(out, axis=1)


def ahead_tables(slabs):
    rows = N // slabs
    n = signed()
    count = len(n)
    a = angles(np.arange(N), n).reshape(slabs, rows, count)
    c, s = np.cos(a), np.sin(a)
    w = np.zeros((slabs, 2, 2, 3, rows, 3, 2, 64))
    for i in range(3):
        w[:, 0, 0, i, :, i, 0, :count] = c
        w[:, 0, 0, i, :, i, 1, :count] = -s
        w[:, 0, 1, i, :, i, 0, :count] = s
        w[:, 0, 1, i, :, i, 1, :count] = c
    w[:, 1, :, :, :, :, 0, :count] = -n * w[:, 0, :, :, :, :, 1, :count]
    w[:, 1, :, :, :, :, 1, :count] = n * w[:, 0, :, :, :, :, 0, :count]
    high, low = halves(lane_pad(w.reshape(slabs, 2, 2, 3 * rows, 3 * LANES), 3))
    blocks = []
    for kind in range(2):
        h, l = high[:, kind], low[:, kind]
        blocks += [h[:, 0], h[:, 0], h[:, 1], h[:, 1], l[:, 0], l[:, 1]]
    return np.concatenate(blocks, axis=1)


def behind_tables(parts):
    rows = N // parts
    n = signed()
    count = len(n)
    a = angles(n, np.arange(N)).reshape(count, parts, rows).transpose(1, 0, 2)
    c, s = np.cos(a) / N, np.sin(a) / N
    w = np.zeros((parts, 3, 2, 64, 2, LANES))
    for i in range(3):
        place = slice(i * rows, (i + 1) * rows)
        w[:, i, 0, :count, 0, place] = c
        w[:, i, 1, :count, 0, place] = -s
        w[:, i, 0, :count, 1, place] = s
        w[:, i, 1, :count, 1, place] = c
    high, low = halves(w.reshape(parts, 3 * LANES, 2 * LANES))
    return np.concatenate([high, high, low], axis=1)


def table_groups():
    blocks = lambda t, height: t.reshape(-1, height, t.shape[-1])
    wide = [z_tables(), y_tables()]
    wide += [lane_pad(lane_pad(t, 1, 4 * MP), 2, 3 * LANES) for t in (y_back(), z_back())]
    wide.append(ahead_tables(2))
    narrow = [filter_tables(2), behind_tables(2), behind_tables(4)]
    return [blocks(t, 2 * MP) for t in wide], [blocks(t, 3 * LANES) for t in narrow]


def table_places():
    counts = (1, 1, 1, 1, 2), (2, 2, 4)
    places = []
    for group, shares in zip(table_groups(), counts):
        start, entries = 0, []
        for t, share in zip(group, shares):
            entries.append((start, len(t) // share))
            start += len(t)
        places.append(entries)
    return places


def quarter_sine(position):
    folded = lax.rem(position, N // 2)
    folded = jnp.minimum(folded, N // 2 - folded)
    angle = folded.astype(f32) * (2.0 * np.pi / N)
    square = angle * angle
    series = 1.0
    for order in (12, 10, 8, 6, 4, 2):
        series = 1.0 - series * square * (1.0 / (order * (order + 1)))
    return jnp.where(position < N // 2, 1.0, -1.0) * angle * series


def cat(values, axis):
    return jnp.concatenate(values, axis=axis)


def wide_rows(*fields):
    blank = jnp.zeros((LANES - fields[0].shape[0], LANES), f32)
    return cat([part for field in fields for part in (field, blank)], 0)


def matmul(left, right):
    return lax.dot_general(left, right, NN, preferred_element_type=f32)


def half_lane(shape):
    return lax.rem(lax.broadcasted_iota(jnp.int32, shape, 1), 64)


def turn(value, shift):
    return pltpu.roll(value, shift % LANES, 1)


GAP = 2 * THIRD + 1
STEP = 64 - GAP
PIECES = (GAP, GAP - STEP, GAP - 2 * STEP)
BODY = 40
PAIR_ROWS = 3 * BODY + 16
QUAD_ROWS = PAIR_ROWS + 3 * BODY + 8


def pack_pair(first, second):
    gap = half_lane(first[0].shape) >= GAP
    carried = (first[0], second[0], first[1])
    return [jnp.where(gap, turn(second[1], by), held) for by, held in zip(PIECES, carried)]


def unpack_pair(tiles):
    lane = half_lane(tiles[0].shape)
    last = turn(tiles[2], -PIECES[2])
    last = jnp.where(lane < 2 * STEP, turn(tiles[1], -PIECES[1]), last)
    last = jnp.where(lane < STEP, turn(tiles[0], -PIECES[0]), last)
    return (tiles[0], tiles[2]), (tiles[1], last)


def tails(first, second):
    low = lax.broadcasted_iota(jnp.int32, first.shape, 0) < 4
    return jnp.where(low, first, pltpu.roll(second, 4, 0))


def squeeze(tile):
    return cat([tile[:BODY], tile[MP : MP + BODY], tails(tile[BODY:MP], tile[MP + BODY :])], 0)


def unsqueeze(held):
    tail = held[2 * BODY :]
    return cat([held[:BODY], tail, held[BODY : 2 * BODY], pltpu.roll(tail, 4, 0)], 0)


def pack_quad(tiles):
    body = [tile[:BODY] for tile in tiles]
    tail = [tile[BODY:] for tile in tiles]
    if len(tiles) == 3:
        return cat([*body, tails(tail[0], tail[1]), tail[2]], 0)
    return cat(
        [
            *body[:3], tails(tail[0], tail[1]), tails(tail[2], tail[5]),
            *body[3:], tails(tail[3], tail[4]),
        ],
        0,
    )


def unpack_quad(held):
    part = lambda start, size: held[start : start + size]
    body = [part(BODY * i, BODY) for i in range(3)]
    first, second = part(3 * BODY, 8), part(3 * BODY + 8, 8)
    tail = [first, pltpu.roll(first, 4, 0), second]
    if held.shape[0] > PAIR_ROWS:
        body += [part(PAIR_ROWS + BODY * i, BODY) for i in range(3)]
        last = part(PAIR_ROWS + 3 * BODY, 8)
        tail += [last, pltpu.roll(last, 4, 0), pltpu.roll(second, 4, 0)]
    return [cat([b, t], 0) for b, t in zip(body, tail)]


def pack_share(planes):
    lane = lax.broadcasted_iota(jnp.int32, planes[0].shape, 1)
    tiles = [jnp.where(lane < 96, planes[i], turn(planes[3], 96 - 32 * i)) for i in range(3)]
    return [squeeze(tile) for tile in tiles]


def unpack_share(held):
    tiles = [unsqueeze(part) for part in held]
    lane = lax.broadcasted_iota(jnp.int32, tiles[0].shape, 1)
    last = jnp.where(lane < 64, turn(tiles[1], 64), turn(tiles[2], 96))
    return [*tiles, jnp.where(lane < 32, turn(tiles[0], 32), last)]


def two_columns(work, k):
    return cat([work[column(k), :], work[column(k + 1), :]], 1)


def fused(
    base_hbm, state_hbm, cutoff_hbm, wave_ref, wide_hbm, narrow_hbm, out_base, out_state,
    base_v, state_v, near_base, near_state, cutoff_ref, wz_v, wy_v, pd_v, xt, xs, xb, yb_v, zb_v,
    w0, w1, w2, wa, wb, wc, wd, held_coupled, own, share, other, partner, g, f,
    base_send, base_recv, base_sum, state_send, state_recv, local_sem, near_send, near_recv, share_send, share_recv, pass_send, pass_recv,
    base_send_sem, base_recv_sem, sum_send, sum_recv, state_send_sem, state_recv_sem,
):
    side = lax.axis_index("comp")
    slab = lax.axis_index("slab")
    seg = lax.axis_index("seg")
    segs = lax.axis_size("seg")
    far = {"slab": 1 - slab}
    twin = {"comp": 1 - side}
    after, before = lax.rem(seg + 1, segs), lax.rem(seg + segs - 1, segs)
    half = near_base.shape[1]
    quarter = N * N // 4

    def local(index, src, dst):
        return pltpu.make_async_copy(src, dst, local_sem.at[index])

    def remote(src, dst, send, recv, device):
        return pltpu.make_async_remote_copy(
            src_ref=src, dst_ref=dst, send_sem=send, recv_sem=recv, device_id=device,
            device_id_type=pl.DeviceIdType.MESH,
        )

    barrier = pltpu.get_barrier_semaphore()
    for device in (far, twin, {"seg": after}, {"seg": before}):
        pl.semaphore_signal(
            barrier, inc=1, device_id=device, device_id_type=pl.DeviceIdType.MESH
        )

    def quarter_of(ref, i):
        return ref.at[:, :, pl.ds(i * quarter, quarter)]

    wide_places, narrow_places = table_places()

    def table_part(hbm, entry, index, dst):
        start, rows = entry
        return hbm.at[pl.ds(start + rows * index, rows)], dst

    cut_copy = local(13, cutoff_hbm, cutoff_ref)
    cut_copy.start()
    wz_copy = local(0, *table_part(wide_hbm, wide_places[0], 0, wz_v))
    base_copies = [
        local(1 + i, quarter_of(base_hbm, i), quarter_of(base_v, i)) for i in range(4)
    ]
    wy_copy = local(5, *table_part(wide_hbm, wide_places[1], 0, wy_v))
    state_copy = local(6, state_hbm, state_v)
    late_copies = [
        local(7, *table_part(narrow_hbm, narrow_places[0], slab, pd_v)),
        local(8, *table_part(wide_hbm, wide_places[2], 0, yb_v)),
        local(9, *table_part(wide_hbm, wide_places[3], 0, zb_v)),
        local(10, *table_part(wide_hbm, wide_places[4], slab, xt)),
        local(11, *table_part(narrow_hbm, narrow_places[1], slab, xs)),
        local(12, *table_part(narrow_hbm, narrow_places[2], 2 * slab + side, xb)),
    ]
    for copy in (wz_copy, *base_copies, wy_copy, state_copy):
        copy.start()

    near_copies = [
        *[
            remote(
                quarter_of(state_hbm, i), quarter_of(near_state, i), near_send.at[1 + i],
                near_recv.at[1 + i], {"seg": jnp.where(side == 0, before, after)},
            )
            for i in range(4)
        ],
        remote(
            base_hbm.at[:, pl.ds(half * side, half), :], near_base, near_send.at[0],
            near_recv.at[0], {"seg": before},
        ),
    ]
    cut_copy.wait()
    cut_x, cut_y, cut_z = (cutoff_ref[i] for i in range(3))
    at_x, at_y, at_z = (jnp.clip(cut - LOW, 0, THIRD - LOW) for cut in (cut_x, cut_y, cut_z))

    def back_table(ref, kind, depth):
        return ref[2 * kind : 2 * kind + 2].reshape(4 * MP, 3 * LANES)[: 2 * N, :depth]

    wz = lambda kind: wz_v[2 * at_z + kind]
    wy = lambda kind: wy_v[2 * at_y + kind]
    yb = lambda kind: back_table(yb_v, kind, 6 * MP)
    zb = lambda kind: back_table(zb_v, kind, 12 * KP)

    def base_ahead_z(p):
        w0[pair_rows(p), :] = left3(wz(0), wide_rows(flat(base_v[:, :, lanes(p)])), NT)

    pl.semaphore_wait(barrier, 4)
    for near_copy in near_copies:
        near_copy.start()
    wz_copy.wait()
    for i, copy in enumerate(base_copies):
        copy.wait()
        loop(PAIRS // 4, Z1, lambda p, i=i: base_ahead_z(p + i * (PAIRS // 4)))
    for copy in late_copies:
        copy.start()
    wy_copy.wait()

    def base_planes(q):
        planes = []
        for j in (0, 2):
            both_planes = left3(wy(0), two_columns(w0, 4 * q + j), NN)
            planes += [both_planes[:, :LANES], both_planes[:, LANES:]]
        for i in range(4):
            own[4 * q + i] = planes[i]
        return planes

    share_copies = []
    for t in range(SIDE_QUADS):
        for i, tile in enumerate(pack_share(base_planes(SIDE_QUADS * side + t))):
            share[3 * t + i] = tile
        rows = pl.ds(3 * t, 3)
        copy = remote(
            share.at[rows], other.at[rows], share_send.at[t], share_recv.at[t], far
        )
        copy.start()
        share_copies.append(copy)
    for t in range(SIDE_QUADS):
        base_planes(SIDE_QUADS * (1 - side) + t)

    pass_copies = []

    def pass_on(t):
        share_copies[t].wait_recv()
        rows = pl.ds(3 * t, 3)
        copy = remote(
            other.at[rows], partner.at[rows], pass_send.at[t], pass_recv.at[t], twin
        )
        copy.start()
        pass_copies.append(copy)

    state_copy.wait()
    scale = sign_step()

    def flux_z(t):
        first, second = [], []
        for i in range(2):
            p = 2 * t + i
            state = state_v[:, :, lanes(p)]
            scaled = state * scale
            f0, f1, f2 = (flat(scaled * base_v[j, :, lanes(p)][None]) for j in range(3))
            plain = left3(wz(0), wide_rows(flat(state), f0), NT)
            wa[pair_rows(p), :] = plain[:, :LANES]
            wc[pair_rows(p), :] = plain[:, LANES:]
            first.append(f1)
            second.append(f2)
        along_y = left3(wz(0), wide_rows(*first), NT)
        along_z = left3(wz(1), wide_rows(*second), NT)
        for i in range(2):
            p = 2 * t + i
            mine = slice(i * LANES, (i + 1) * LANES)
            wb[pair_rows(p), :] = along_y[:, mine]
            wa[pair_rows(p), :] += along_z[:, mine]

    for copy in late_copies:
        copy.wait()

    def back_y(ref, place, t):
        q = SIDE_QUADS * place + t
        planes = unpack_share([ref[3 * t + i] for i in range(3)])
        deep = []
        for i in range(4):
            own_high, own_low = split(own[4 * q + i])
            far_high, far_low = split(planes[i])
            deep.append(cat([own_high, own_low, far_high, far_low, own_high, far_high], 1))
        filtered = matmul(cat(deep, 0), cat([pd_v[2 * at_x], pd_v[2 * at_x + 1]], 0))
        kinds = [filtered[96 * i : 96 * (i + 1)] for i in range(4)]
        for j in (0, 2):
            along = left3(yb(1), cat([kinds[j][:, :LANES], kinds[j + 1][:, :LANES]], 1), NN)
            for i in range(2):
                k = 4 * q + j + i
                whole = left3(yb(0), kinds[j + i], NN)
                w2[column(k), :] = whole[:, :LANES]
                w0[column(k), :] = whole[:, LANES:]
                w1[column(k), :] = along[:, i * LANES : (i + 1) * LANES]

    loop(FLUX_FIRST, 6, flux_z)
    pass_on(0)
    back_y(other, side, 0)
    loop(PAIRS // 2 - FLUX_FIRST, 4, lambda t: flux_z(t + FLUX_FIRST))
    pass_on(1)
    back_y(other, side, 1)
    pass_copies[0].wait_recv()
    back_y(partner, 1 - side, 0)
    pass_on(2)
    back_y(other, side, 2)
    for t in (1, 2):
        pass_copies[t].wait_recv()
        back_y(partner, 1 - side, t)

    tangent = side == 0
    wave = wave_ref[0]

    def force(p):
        lane = lax.broadcasted_iota(jnp.int32, (1, LANES), 1)
        y = 2 * p + jnp.where(lane < 64, 0, 1)
        return forcing_amp * quarter_sine(lax.rem(wave * y, N))

    def grid_space(t):
        third = left3(
            zb(1), cat([w2[pair_rows(2 * t + i), :] for i in range(2)], 1), NN
        ).T
        driven_pair = []
        for i in range(2):
            p = 2 * t + i
            state = state_v[:, :, lanes(p)]
            base = base_v[:, :, lanes(p)]
            pair = left3(zb(0), cat([w0[pair_rows(p), :], w1[pair_rows(p), :]], 1), NN).T
            grad = [
                pair[:96].reshape(base.shape),
                pair[LANES : LANES + 96].reshape(base.shape),
                third[i * LANES : i * LANES + 96].reshape(base.shape),
            ]
            coupled, driven = [], []
            for a in range(3):
                total = 0.0
                drive = 0.0
                for b in range(3):
                    total = total + jnp.where(tangent, grad[b][a], grad[a][b]) * state[b]
                    drive = drive + grad[b][a] * base[b]
                if a == 0:
                    drive = drive - force(p)
                coupled.append(-time_step * total)
                driven.append(base[a] - time_step * drive)
            held_coupled[:, lanes(p)] = cat(coupled, 0)
            driven_pair.append(cat(driven, 0))
        out = left3(wz(0), wide_rows(*driven_pair), NT)
        for i in range(2):
            wd[pair_rows(2 * t + i), :] = out[:, i * LANES : (i + 1) * LANES]

    loop(PAIRS // 2, 8, grid_space)

    waves = plane_waves()
    keep = jnp.where(jnp.abs(waves[0]) <= cut_x.astype(f32), 1.0, 0.0)

    def ahead_deep(plane):
        high, low = split(plane)
        return [high[:MP], low[:MP], high[MP:], low[MP:], high[:MP], high[MP:]]

    row = lax.broadcasted_iota(jnp.int32, (MP, LANES), 0)
    upper = row > THIRD
    folded = jnp.where(upper, 0.0, jnp.where(row == 0, 1.0, 2.0))

    def emit_planes(ref, start, first_k, modes, count, fold):
        new = []
        for i in range(count):
            w = projected(waves, modes[MP * i : MP * (i + 1)], first_k + i)
            new.append([keep * part for part in w])
        if fold is not None:
            held = jnp.where(upper, pltpu.roll(new[0][2], THIRD + 1, 0), new[0][0])
            new[0][0] = jnp.where(fold, held, new[0][0])
        tiles = []
        for j in range(0, count, 2):
            tiles += pack_pair(new[j], new[j + 1])
        rows = QUAD_ROWS if count == 4 else PAIR_ROWS
        ref[start : start + rows, :] = pack_quad(tiles)

    def base_copy(t, rows):
        rows = pl.ds(QUAD_ROWS * t, rows)
        return remote(
            base_send.at[rows], base_recv.at[rows], base_send_sem.at[t], base_recv_sem.at[t],
            far,
        )

    def each_side(copies, act):
        if len(copies) == 1:
            act(copies[0])
        else:
            pl.when(side == 0)(lambda: act(copies[0]))
            pl.when(side == 1)(lambda: act(copies[1]))

    base_copies = []
    for t in range(SIDE_QUADS):
        q = SIDE_QUADS * side + t
        deep = []
        for j in (0, 2):
            both_planes = left3(wy(0), two_columns(wd, 4 * q + j), NN)
            for i in range(2):
                deep.append(cat(ahead_deep(both_planes[:, i * LANES : (i + 1) * LANES]), 1))
        modes = matmul(cat(deep, 0), flat(xt[:8]))
        emit_planes(base_send, QUAD_ROWS * t, 4 * q, modes, 4, side == 0 if t == 0 else None)
        copies = [base_copy(t, QUAD_ROWS)]
        if t == SIDE_QUADS - 1:
            copies.append(base_copy(t, PAIR_ROWS))
        base_copies.append(copies)
        each_side(copies, lambda copy: copy.start())

    def flux_y(t):
        k = 2 * t
        extra = left3(wy(1), two_columns(wb, k), NN)
        for i in range(2):
            whole = left3(
                wy(0), cat([wa[column(k + i), :], wc[column(k + i), :]], 1), NN
            )
            g[k + i] = whole[:, :LANES] + extra[:, i * LANES : (i + 1) * LANES]
            f[k + i] = whole[:, LANES:]

    loop(QK // 2, 4, flux_y)

    def coupled_z(t):
        rows = [held_coupled[:, lanes(2 * t + i)] for i in range(2)]
        out = left3(wz(0), wide_rows(*rows), NT)
        for i in range(2):
            wa[pair_rows(2 * t + i), :] = out[:, i * LANES : (i + 1) * LANES]

    loop(PAIRS // 2, 4, coupled_z)

    state_copies = []
    for q in range(STATE_QUADS):
        pairs = 2 if q < STATE_QUADS - 1 else 1
        deep = []
        for j in range(0, 2 * pairs, 2):
            both_planes = left3(wy(0), two_columns(wa, 4 * q + j), NN)
            for i in range(2):
                k = 4 * q + j + i
                total = g[k] + both_planes[:, i * LANES : (i + 1) * LANES]
                deep.append(cat(ahead_deep(total) + ahead_deep(f[k]), 1))
        modes = matmul(cat(deep, 0), flat(xt[...]))
        fold = True if q == 0 else None
        emit_planes(state_send, QUAD_ROWS * q, 4 * q, modes, 2 * pairs, fold)
        rows = pl.ds(QUAD_ROWS * q, QUAD_ROWS if pairs == 2 else PAIR_ROWS)
        copy = remote(
            state_send.at[rows], state_recv.at[rows], state_send_sem.at[q],
            state_recv_sem.at[q], far,
        )
        copy.start()
        state_copies.append(copy)

    def spectral(held, fold, first_k, table_ref, work):
        tiles = unpack_quad(held)
        deep = []
        wave_x, wave_y = waves
        for j in range(len(tiles) // 3):
            for i, (m0, m1) in enumerate(unpack_pair(tiles[3 * j : 3 * j + 3])):
                k = jnp.asarray(first_k + 2 * j + i, jnp.int32)
                inverse = 1.0 / jnp.maximum(k, 1).astype(f32)
                m2 = -(wave_x * m0 + wave_y * m1) * inverse
                if fold is not None and i == 0 and j == 0:
                    third = pltpu.roll(m0, MP - THIRD - 1, 0)
                    m2 = jnp.where(fold, folded * third, m2)
                    m0 = jnp.where(fold, folded * m0, m0)
                    m1 = jnp.where(fold, folded * m1, m1)
                high, low = split(cat([m0, m1, m2], 1))
                deep.append(cat([high, low, high], 1))
        rows = matmul(cat(deep, 0), flat(table_ref[...]))
        planes = []
        for i in range(len(deep)):
            mine = rows[MP * i : MP * (i + 1)]
            planes.append(cat([mine[:, :LANES], mine[:, LANES:]], 0))
        for j in range(0, len(deep), 2):
            out = left3(yb(0), cat(planes[j : j + 2], 1), NN)
            for i in range(2):
                work[column(first_k + j + i), :] = out[:, i * LANES : (i + 1) * LANES]

    span = base_sum.shape[0] // 2
    sum_copies = []
    for t in range(SIDE_QUADS):
        each_side(base_copies[t], lambda copy: copy.wait_recv())
        mine = slice(QUAD_ROWS * t, QUAD_ROWS * (t + 1))
        total = base_send[mine, :] + base_recv[mine, :]
        if t == SIDE_QUADS - 1:
            place = lax.broadcasted_iota(jnp.int32, total.shape, 0)
            total = jnp.where((side == 0) | (place < PAIR_ROWS), total, 0.0)
        rows = pl.ds(pl.multiple_of(span * side + QUAD_ROWS * t, 8), QUAD_ROWS)
        base_sum[rows, :] = total
        copy = remote(
            base_sum.at[rows], base_sum.at[rows], sum_send.at[t], sum_recv.at[t], twin
        )
        copy.start()
        sum_copies.append(copy)

    def base_back(place, t):
        rows = pl.ds(pl.multiple_of(span * place + QUAD_ROWS * t, 8), QUAD_ROWS)
        fold = place == 0 if t == 0 else None
        spectral(base_sum[rows, :], fold, 4 * (SIDE_QUADS * place + t), xb, w0)

    for t in range(SIDE_QUADS):
        base_back(side, t)
    for t in range(SIDE_QUADS):
        sum_copies[t].wait_recv()
        base_back(1 - side, t)

    def finish_base(p):
        rows = left3(zb(0), w0[pair_rows(p), :], NN).T
        out_base[:, :, lanes(p)] = rows[:48].reshape(3, half, LANES)

    loop(PAIRS, 8, finish_base)

    for q in range(STATE_QUADS):
        state_copies[q].wait_recv()
        rows = QUAD_ROWS if q < STATE_QUADS - 1 else PAIR_ROWS
        mine = slice(QUAD_ROWS * q, QUAD_ROWS * q + rows)
        total = state_send[mine, :] + state_recv[mine, :]
        spectral(total, True if q == 0 else None, 4 * q, xs, wc)

    def finish_state(p):
        rows = left3(zb(0), wc[pair_rows(p), :], NN).T
        out_state[:, :, lanes(p)] = rows[:96].reshape(3, 2 * half, LANES)

    loop(PAIRS, 16, finish_state)

    def state_difference(i):
        span = pl.ds(pl.multiple_of(i * 512, 512), 512)
        out_state[:, :, span] -= near_state[:, :, span]

    for i in range(4):
        near_copies[i].wait_recv()
        loop(2, 2, lambda j, i=i: state_difference(2 * i + j))

    def base_difference(i):
        span = pl.ds(pl.multiple_of(i * 512, 512), 512)
        out_base[:, :, span] -= near_base[:, :, span]

    near_copies[4].wait_recv()
    loop(N * N // 512, 4, base_difference)

    sent = near_copies + share_copies + pass_copies + sum_copies + state_copies
    for copy in sent:
        copy.wait_send()
    for copies in base_copies:
        each_side(copies, lambda copy: copy.wait_send())


def copy_out(base_v, state_v, base_hbm, state_hbm, sem):
    copies = [
        pltpu.make_async_copy(base_v, base_hbm, sem.at[0]),
        pltpu.make_async_copy(state_v, state_hbm, sem.at[1]),
    ]
    for copy in copies:
        copy.start()
    for copy in copies:
        copy.wait()


def write_out(*fields):
    return pl.pallas_call(
        copy_out,
        out_shape=[jax.ShapeDtypeStruct(field.shape, f32) for field in fields],
        in_specs=[pl.BlockSpec(memory_space=pltpu.VMEM)] * 2,
        out_specs=[pl.BlockSpec(memory_space=pltpu.HBM)] * 2,
        scratch_shapes=[pltpu.SemaphoreType.DMA((2,))],
        compiler_params=pltpu.CompilerParams(vmem_limit_bytes=2**20),
    )(*fields)


def fused_body(base, state, wavenumber, cutoff):
    base, state = base[0], state[0, 0]
    rows = base.shape[1]
    half = rows // lax.axis_size("comp")
    slabs = lax.axis_size("slab")
    tables = [jnp.asarray(np.concatenate(group)) for group in table_groups()]
    hbm = pl.BlockSpec(memory_space=pltpu.HBM)
    smem = pl.BlockSpec(memory_space=pltpu.SMEM)
    vmem = lambda *shape: pltpu.VMEM(shape, f32)
    dma = lambda count: pltpu.SemaphoreType.DMA((count,))
    wide, narrow = table_places()
    wz, wy, yb, zb, xt = (pltpu.VMEM((entry[1], 2 * MP, 3 * LANES), bf16) for entry in wide)
    pd, xs, xb = (pltpu.VMEM((entry[1], 3 * LANES, 2 * LANES), bf16) for entry in narrow)
    work = vmem(2 * N * KP, LANES)
    share = vmem(3 * SIDE_QUADS, 2 * BODY + 8, LANES)
    planes = vmem(QK, 2 * MP, LANES)
    base_tiles = vmem(SIDE_QUADS * QUAD_ROWS, LANES)
    state_tiles = vmem((STATE_QUADS - 1) * QUAD_ROWS + PAIR_ROWS, LANES)
    base_half = vmem(3, half, N * N)
    whole = vmem(3, rows, N * N)
    scratch = [
        whole, whole, base_half, whole, pltpu.SMEM((3,), jnp.int32), wz, wy, pd, xt, xs, xb, yb, zb,
        *[work] * 7, vmem(3 * rows, N * N), planes, share, share, share, planes, planes,
        base_tiles, base_tiles, vmem(2 * SIDE_QUADS * QUAD_ROWS, LANES), state_tiles, state_tiles,
        dma(14), dma(5), dma(5), *[dma(SIDE_QUADS)] * 8, *[dma(STATE_QUADS)] * 2,
    ]
    base_gap, state_gap = pl.pallas_call(
        fused,
        out_shape=[
            jax.ShapeDtypeStruct((3, half, N * N), f32),
            jax.ShapeDtypeStruct((3, rows, N * N), f32),
        ],
        in_specs=[hbm, hbm, hbm, smem, hbm, hbm],
        out_specs=[pl.BlockSpec(memory_space=pltpu.VMEM)] * 2,
        scratch_shapes=scratch,
        compiler_params=pltpu.CompilerParams(
            vmem_limit_bytes=51 * 2**20, collective_id=0, has_side_effects=True
        ),
        cost_estimate=pl.CostEstimate(flops=10**10, bytes_accessed=10**7, transcendentals=0),
    )(base, state, cutoff, wavenumber, *tables)
    base_gap, state_gap = write_out(base_gap, state_gap)
    return base_gap[None], state_gap[None, None]


def solution(mesh):
    sizes = dict(mesh.shape)
    one_kernel = sizes["slab"] == 2 and sizes["comp"] == 2 and sizes["seg"] > 1
    return jax.shard_map(
        fused_body if one_kernel else body,
        mesh=mesh,
        in_specs=(
            P(("groups", "seg"), None, "slab", None),
            P(("groups", "seg"), "comp", None, "slab", None),
            P("groups"),
            P("groups"),
        ),
        out_specs=(
            P(("groups", "seg"), None, ("slab", "comp"), None),
            P(("groups", "seg"), "comp", None, "slab", None),
        ),
        check_vma=False,
    )
```

```python
import functools

import jax
import jax.numpy as jnp
import ml_dtypes
import numpy as np
from jax import lax
from jax.experimental import pallas as pl
from jax.experimental.pallas import tpu as pltpu
from jax.sharding import PartitionSpec as P

N = 64
BACK, GRID, AHEAD, SPEC, Z1, Z2, Z3, Y1 = 4, 4, 4, 4, 8, 4, 8, 6
THIRD = N // 3
LOW = THIRD - 3
KZ = THIRD + 1
KP = 24
MP = 48
PAIRS = N // 2
FLUX = 14 * 10**9
HALF = KZ // 2
viscosity = 0.025
time_step = 0.02
forcing_amp = 10.0
f32 = jnp.float32
bf16 = jnp.bfloat16

NN = (((1,), (0,)), ((), ()))
NT = (((1,), (1,)), ((), ()))


def split(value):
    high = value.astype(bf16)
    return high, (value - high.astype(f32)).astype(bf16)


def dot3(left, right, dims):
    dot = functools.partial(lax.dot_general, dimension_numbers=dims, preferred_element_type=f32)
    return dot(left[0], right[0]) + (dot(left[0], right[1]) + dot(left[1], right[0]))


def table(values):
    values = np.asarray(values, np.float32)
    high = values.astype(ml_dtypes.bfloat16)
    low = (values - high.astype(np.float32)).astype(ml_dtypes.bfloat16)
    return np.stack([high, low], axis=-3)


def table3(values):
    high, low = np.moveaxis(table(values), -3, 0)
    return np.concatenate([high, high, low], axis=-1)


def left3(left, value, dims):
    high, low = split(value)
    deep = jnp.concatenate([high, low, high], axis=dims[0][1][0])
    return lax.dot_general(left, deep, dimension_numbers=dims, preferred_element_type=f32)


def signed():
    m = np.arange(2 * THIRD + 1)
    return np.where(m <= THIRD, m, m - (2 * THIRD + 1))


def angles(first, second):
    return np.mod(np.outer(first, second), N) * (2 * np.pi / N)


def cuts():
    return range(LOW, THIRD + 1)


def z_tables():
    plain, ik = [], []
    k = np.arange(KZ)
    a = angles(k, np.arange(N))
    for cut in cuts():
        keep = 1.0 * (k <= cut)[:, None]
        w = np.zeros((2, KP, N))
        v = np.zeros((2, KP, N))
        w[0, :KZ], w[1, :KZ] = keep * np.cos(a), -keep * np.sin(a)
        v[0, :KZ], v[1, :KZ] = keep * k[:, None] * np.sin(a), keep * k[:, None] * np.cos(a)
        plain.append(np.kron(np.eye(2), w.reshape(2 * KP, N)))
        ik.append(np.kron(np.eye(2), v.reshape(2 * KP, N)))
    return table3(np.stack([np.stack(plain), np.stack(ik)], axis=1))


def y_tables():
    out = []
    m = signed()
    count = len(m)
    a = angles(m, np.arange(N))
    for cut in cuts():
        keep = 1.0 * (np.abs(m) <= cut)[:, None]
        c, s = keep * np.cos(a), keep * np.sin(a)
        w = np.zeros((2, MP, N, 2))
        w[0, :count, :, 0], w[0, :count, :, 1] = c, s
        w[1, :count, :, 0], w[1, :count, :, 1] = -s, c
        v = np.zeros_like(w)
        v[0, :count] = -m[:, None, None] * w[1, :count]
        v[1, :count] = m[:, None, None] * w[0, :count]
        out.append(np.stack([w.reshape(2 * MP, 2 * N), v.reshape(2 * MP, 2 * N)]))
    return table3(np.stack(out))


def y_back():
    m = signed()
    count = len(m)
    a = angles(np.arange(N), m)
    c, s = np.cos(a) / N, np.sin(a) / N
    w = np.zeros((N, 2, 2, MP))
    w[:, 0, 0, :count], w[:, 0, 1, :count] = c, -s
    w[:, 1, 0, :count], w[:, 1, 1, :count] = s, c
    v = np.zeros_like(w)
    v[:, :, 0, :count] = m * w[:, :, 1, :count]
    v[:, :, 1, :count] = -m * w[:, :, 0, :count]
    return table3(np.stack([w.reshape(2 * N, 2 * MP), v.reshape(2 * N, 2 * MP)]))


def z_back():
    k = np.arange(KZ)
    a = angles(k, np.arange(N))
    weight = (np.where(k == 0, 1.0, 2.0) / N)[:, None]
    w = np.zeros((2, KP, N))
    w[0, :KZ], w[1, :KZ] = weight * np.cos(a), -weight * np.sin(a)
    v = np.zeros_like(w)
    v[0, :KZ] = k[:, None] * w[1, :KZ]
    v[1, :KZ] = -k[:, None] * w[0, :KZ]
    pair = lambda t: np.kron(np.eye(2), t.reshape(2 * KP, N))
    return table3(np.stack([pair(w).T, pair(v).T]))


def x_filters(slabs):
    rows = N // slabs
    out = []
    x = np.arange(N)
    for cut in cuts():
        n = np.arange(-cut, cut + 1)
        d = np.mod(x[:, None] - x[None, :], N)
        phase = 2 * np.pi / N * n[:, None, None] * -d
        plain = np.cos(phase).sum(0) / N
        deriv = (-n[:, None, None] * np.sin(phase)).sum(0) / N
        both = np.stack([plain, deriv]).reshape(2, slabs, rows, slabs, rows)
        wide = np.zeros((slabs, 2, slabs, 3, rows, 3, rows))
        for i in range(3):
            wide[:, :, :, i, :, i, :] = both.transpose(3, 0, 1, 2, 4)
        out.append(wide.reshape(slabs, 2, slabs, 3 * rows, 3 * rows))
    return table(np.stack(out))


def x_tables(slabs):
    rows = N // slabs
    n = signed()
    count = len(n)
    a = angles(np.arange(N), n).reshape(slabs, rows, count)
    out = []
    for cut in cuts():
        keep = 1.0 * (np.abs(n) <= cut)
        c, s = np.cos(a) * keep, np.sin(a) * keep
        w = np.zeros((slabs, 2, 2, 3, rows, 3, 2, 64))
        for i in range(3):
            w[:, 0, 0, i, :, i, 0, :count] = c
            w[:, 0, 0, i, :, i, 1, :count] = -s
            w[:, 0, 1, i, :, i, 0, :count] = s
            w[:, 0, 1, i, :, i, 1, :count] = c
        w[:, 1, :, :, :, :, 0, :count] = -n * w[:, 0, :, :, :, :, 1, :count]
        w[:, 1, :, :, :, :, 1, :count] = n * w[:, 0, :, :, :, :, 0, :count]
        out.append(w.reshape(slabs, 2, 2, 3 * rows, 384))
    return table(np.stack(out))


def x_back(slabs):
    rows = N // slabs
    n = signed()
    count = len(n)
    a = angles(n, np.arange(N)).reshape(count, slabs, rows).transpose(1, 0, 2)
    c, s = np.cos(a) / N, np.sin(a) / N
    w = np.zeros((slabs, 2, 3, 2, 64, 3, rows))
    for i in range(3):
        w[:, 0, i, 0, :count, i] = c
        w[:, 0, i, 1, :count, i] = -s
        w[:, 1, i, 0, :count, i] = s
        w[:, 1, i, 1, :count, i] = c
    return table(w.reshape(slabs, 2, 384, 3 * rows))


def both(ref, *index):
    return ref[(*index, 0)], ref[(*index, 1)]


def lanes(p):
    return pl.ds(pl.multiple_of(p * 128, 128), 128)


def pair_rows(p):
    return pl.ds(pl.multiple_of(p * 4 * KP, 8), 4 * KP)


def column(k):
    return pl.ds(k, 2 * N, stride=KP)


def flat(block):
    return block.reshape(block.shape[0] * block.shape[1], block.shape[2])


def loop(count, unroll, step):
    def go(i, carry):
        step(i)
        return carry

    lax.fori_loop(0, count, go, 0, unroll=unroll)


def clear_padding(*works):
    for k in range(KZ, KP):
        for work in works:
            work[column(k), :] = jnp.zeros((2 * N, work.shape[1]), f32)


def base_ahead(base_ref, wz_ref, wy_ref, out_ref, half_ref, work):
    def along_z(p):
        work[pair_rows(p), :] = left3(wz_ref[0], flat(base_ref[:, :, lanes(p)]), NT)

    loop(PAIRS, Z1, along_z)

    def along_y(k):
        out_ref[k] = left3(wy_ref[0], work[column(k), :], NN)

    loop(KZ, Y1, along_y)
    first = HALF * lax.axis_index("comp")

    def share(j):
        half_ref[j] = out_ref[first + j]

    loop(HALF, 1, share)


def sign_step():
    return jnp.where(lax.axis_index("comp") == 0, -time_step, time_step).astype(f32)


def flux_ahead(base_ref, state_ref, wz_ref, wy_ref, g_ref, work_a, work_b):
    scale = sign_step()

    def along_z(p):
        state = state_ref[:, :, lanes(p)]
        scaled = state * scale
        f1, f2 = (flat(scaled * base_ref[j, :, lanes(p)][None]) for j in (1, 2))
        plain = wz_ref[0]
        work_a[pair_rows(p), :] = left3(plain, flat(state), NT) + left3(wz_ref[1], f2, NT)
        work_b[pair_rows(p), :] = left3(plain, f1, NT)

    loop(PAIRS, Z2, along_z)

    def along_y(k):
        g_ref[k] = left3(wy_ref[0], work_a[column(k), :], NN) + left3(
            wy_ref[1], work_b[column(k), :], NN
        )

    loop(KZ, Y1, along_y)


def flux_x_ahead(base_ref, state_ref, wz_ref, wy_ref, f_ref, work):
    scale = sign_step()

    def along_z(p):
        f0 = flat(state_ref[:, :, lanes(p)] * scale * base_ref[0, :, lanes(p)][None])
        work[pair_rows(p), :] = left3(wz_ref[0], f0, NT)

    loop(PAIRS, Z2, along_z)

    def along_y(k):
        f_ref[k] = left3(wy_ref[0], work[column(k), :], NN)

    loop(KZ, Y1, along_y)


def gradients(
    slabs, count, *refs,
):
    got, rest = refs[:count], refs[count:]
    side = lax.axis_index("comp")
    if count == 1:
        visits = [(lambda j: (j, [got[0][s, j] for s in range(slabs)]), KZ)]
    else:
        own, mine, partner = got

        def visit(ref, first):
            return lambda j: (first + j, [own[first + j], ref[j]])

        visits = [
            (visit(mine, HALF * side), HALF),
            (visit(partner, HALF * (1 - side)), HALF),
        ]
    gradients_of(slabs, visits, *rest)


def gradients_of(
    slabs, visits, base_ref, state_ref, force_ref, pd_ref, yb_ref, zb_ref, wz_ref, wy_ref,
    xt_ref, base_out_ref, coupled_ref, work_0, work_1, work_2,
):
    tangent = lax.axis_index("comp") == 0

    def back_y(visit, j):
        k, sources = visit(j)
        sources = [split(source) for source in sources]

        def across(kind):
            total = dot3(sources[0], both(pd_ref, kind, 0), NN)
            for s in range(1, slabs):
                total = total + dot3(sources[s], both(pd_ref, kind, s), NN)
            return total

        plain, deriv = across(0), across(1)
        work_0[column(k), :] = left3(yb_ref[0], deriv, NN)
        work_1[column(k), :] = left3(yb_ref[1], plain, NN)
        work_2[column(k), :] = left3(yb_ref[0], plain, NN)

    clear_padding(work_0, work_1, work_2)
    for visit, count in visits:
        loop(count, BACK, functools.partial(back_y, visit))

    def grid_space(p):
        state = state_ref[:, :, lanes(p)]
        base = base_ref[:, :, lanes(p)]
        grad = []
        for work, kind in ((work_0, 0), (work_1, 0), (work_2, 1)):
            rows = left3(zb_ref[kind], work[pair_rows(p), :], NN).T
            grad.append(rows.reshape(base.shape))
        coupled, driven = [], []
        for i in range(3):
            total = 0.0
            drive = 0.0
            for j in range(3):
                total = total + jnp.where(tangent, grad[j][i], grad[i][j]) * state[j]
                drive = drive + grad[j][i] * base[j]
            if i == 0:
                drive = drive - force_ref[:, lanes(p)]
            coupled.append(-time_step * total)
            driven.append(base[i] - time_step * drive)
        plain = wz_ref[0]
        coupled_ref[pair_rows(p), :] = left3(plain, jnp.concatenate(coupled, axis=0), NT)
        work_1[pair_rows(p), :] = left3(plain, jnp.concatenate(driven, axis=0), NT)

    loop(PAIRS, GRID, grid_space)

    waves = plane_waves()
    first = HALF * lax.axis_index("comp")

    def base_ahead_x(step):
        j = HALF - 1 - step
        k = first + j
        driven = left3(wy_ref[0], work_1[column(k), :], NN)
        modes = 0.0
        for d in range(2):
            rows = slice(d * MP, (d + 1) * MP)
            modes = modes + dot3(split(driven[rows]), both(xt_ref, 0, d), NN)
        emit(waves, base_out_ref, j, HALF, modes, k)

    loop(HALF, AHEAD, base_ahead_x)


def emit(waves, ref, slot, last, modes, k):
    new = projected(waves, modes, k)
    ref[slot] = jnp.concatenate(new[:2], axis=1)
    ref[last] = jnp.concatenate([new[2], jnp.zeros_like(new[2])], axis=1)


def state_ahead_x(coupled_ref, wy_ref, xt_ref, g_ref, f_ref, out_ref):
    waves = plane_waves()

    def ahead_x(step):
        k = KZ - 1 - step
        total = g_ref[k] + left3(wy_ref[0], coupled_ref[column(k), :], NN)
        outer = f_ref[k]
        modes = 0.0
        for d in range(2):
            rows = slice(d * MP, (d + 1) * MP)
            modes = modes + dot3(split(total[rows]), both(xt_ref, 0, d), NN)
            modes = modes + dot3(split(outer[rows]), both(xt_ref, 1, d), NN)
        emit(waves, out_ref, k, KZ, modes, k)

    loop(KZ, AHEAD, ahead_x)


def plane_waves():
    column_n = lax.rem(lax.broadcasted_iota(jnp.int32, (MP, 128), 1), 64)
    row_m = lax.broadcasted_iota(jnp.int32, (MP, 128), 0)
    wrap = lambda v: jnp.where(v <= THIRD, v, v - (2 * THIRD + 1)).astype(f32)
    return wrap(column_n), wrap(row_m)


def projected(waves, modes, k):
    wave_x, wave_y = waves
    wave_z = jnp.asarray(k, jnp.int32).astype(f32)
    square = wave_x * wave_x + wave_y * wave_y + wave_z * wave_z
    safe = jnp.where(square > 0, square, 1.0)
    damping = 1.0 / (1.0 + viscosity * time_step * square)
    w = [modes[:, i * 128 : (i + 1) * 128] for i in range(3)]
    divergence = (wave_x * w[0] + wave_y * w[1] + wave_z * w[2]) / safe
    return [
        damping * (w[0] - wave_x * divergence),
        damping * (w[1] - wave_y * divergence),
        damping * (w[2] - wave_z * divergence),
    ]


def finish(count, halved, *refs):
    parts, (near_ref, xb_ref, yb_ref, zb_ref, out_ref, work) = refs[:count], refs[count:]
    wave_x, wave_y = plane_waves()
    clear_padding(work)

    def spectral(parts, first, last, j):
        k = first + j
        modes, third = 0.0, 0.0
        for part in parts:
            modes = modes + part[j]
            third = third + part[last, :, :128]
        w0, w1 = modes[:, :128], modes[:, 128:]
        whole = jnp.asarray(k, jnp.int32)
        inverse = 1.0 / jnp.maximum(whole, 1).astype(f32)
        w2 = jnp.where(whole == 0, third, -(wave_x * w0 + wave_y * w1) * inverse)
        new = split(jnp.concatenate([w0, w1, w2], axis=1))
        rows = [dot3(new, both(xb_ref, d), NN) for d in range(2)]
        work[column(k), :] = left3(yb_ref[0], jnp.concatenate(rows, axis=0), NN)

    if halved:
        side = lax.axis_index("comp")
        for part, place in zip(parts, (side, 1 - side)):
            loop(HALF, SPEC, functools.partial(spectral, [part], HALF * place, HALF))
    else:
        loop(KZ, SPEC, functools.partial(spectral, parts, 0, KZ))

    def along_z(p):
        rows = left3(zb_ref[0], work[pair_rows(p), :], NN).T
        near = near_ref[:, :, lanes(p)]
        out_ref[:, :, lanes(p)] = rows.reshape(near.shape) - near

    loop(PAIRS, Z3, along_z)


def call(kernel, out_shape, scratch, cost, *operands):
    return pl.pallas_call(
        kernel,
        out_shape=out_shape,
        in_specs=[pl.BlockSpec(memory_space=pltpu.VMEM)] * len(operands),
        out_specs=jax.tree.map(lambda _: pl.BlockSpec(memory_space=pltpu.VMEM), out_shape),
        scratch_shapes=scratch,
        compiler_params=pltpu.CompilerParams(vmem_limit_bytes=48 * 2**20),
        cost_estimate=pl.CostEstimate(flops=cost, bytes_accessed=2**10, transcendentals=0),
    )(*operands)


def body(base, state, wavenumber, cutoff):
    base, state = base[0], state[0, 0]
    slab_rows = base.shape[1]
    half = slab_rows // lax.axis_size("comp")
    slabs = lax.axis_size("slab")
    segs = lax.axis_size("seg")
    slab = lax.axis_index("slab")
    side = lax.axis_index("comp")
    width = 3 * slab_rows
    which = cutoff - LOW

    route = [((s, 0), ((s - 1) % segs, 0)) for s in range(segs)]
    route += [((s, 1), ((s + 1) % segs, 1)) for s in range(segs)]
    route = [(a * 2 + b, c * 2 + d) for (a, b), (c, d) in route]
    wz = lax.dynamic_index_in_dim(jnp.asarray(z_tables()), which[2], 0, False)
    wy = lax.dynamic_index_in_dim(jnp.asarray(y_tables()), which[1], 0, False)
    filters, ahead = jnp.asarray(x_filters(slabs)), jnp.asarray(x_tables(slabs))
    pick = lambda t: lax.dynamic_slice(
        t, (which[0], slab) + (0,) * (t.ndim - 2), (1, 1) + t.shape[2:]
    )[0, 0]
    pd, xt = pick(filters), pick(ahead)
    xb = lax.dynamic_index_in_dim(jnp.asarray(x_back(slabs)), slab, 0, False)
    yb, zb = jnp.asarray(y_back()), jnp.asarray(z_back())

    modes = jax.ShapeDtypeStruct((KZ, 2 * MP, width), f32)
    half_modes = jax.ShapeDtypeStruct((HALF, 2 * MP, width), f32)
    spectrum = jax.ShapeDtypeStruct((KZ + 1, MP, 256), f32)
    half_spectrum = jax.ShapeDtypeStruct((HALF + 1, MP, 256), f32)
    work = pltpu.VMEM((2 * N * KP, width), f32)
    own, share = call(base_ahead, (modes, half_modes), [work], 4 * 10**9, base, wz, wy)
    later, later_base, share = lax.optimization_barrier((state, base, share))
    near_state = lax.ppermute(later, ("seg", "comp"), route)
    base_half = lax.dynamic_slice_in_dim(later_base, side * half, half, 1)
    near_base = lax.ppermute(base_half, "seg", [((s + 1) % segs, s) for s in range(segs)])
    if slabs == 2:
        other = lax.ppermute(share, "slab", [(0, 1), (1, 0)])
        partner = lax.ppermute(other, "comp", [(0, 1), (1, 0)])
        first = slab == 0
        got = (own, other, partner)
        pd = jnp.where(first, pd, pd[:, ::-1])
    else:
        got = (lax.all_gather(own, "slab"),)
    g = call(flux_ahead, modes, [work] * 2, FLUX, base, state, wz, wy)
    f = call(flux_x_ahead, modes, [work], 10**9, base, state, wz, wy)

    *got, g, f = lax.optimization_barrier((*got, g, f))

    y = jnp.arange(N, dtype=jnp.int32)
    phase = jnp.mod(wavenumber[0] * y, N).astype(f32) * (2.0 * jnp.pi / N)
    force = jnp.repeat(forcing_amp * jnp.sin(phase), N)[None]
    lined = jax.ShapeDtypeStruct((2 * N * KP, width), f32)
    base_modes, coupled = call(
        functools.partial(gradients, slabs, len(got)), (half_spectrum, lined), [work] * 3,
        25 * 10**9, *got, base, state, force, pd, yb, zb, wz, wy, xt,
    )
    state_modes = call(state_ahead_x, spectrum, [], 3 * 10**9, coupled, wy, xt, g, f)
    near_state, near_base, state_modes = lax.optimization_barrier(
        (near_state, near_base, state_modes)
    )
    if slabs == 2:
        swap = lambda v: lax.ppermute(v, "slab", [(0, 1), (1, 0)])
        state_other = swap(state_modes)
        base_other, state_modes = lax.optimization_barrier((swap(base_modes), state_modes))
        base_sum = base_modes + base_other
        state_parts = (state_modes, state_other)
    else:
        base_sum = lax.psum(base_modes, "slab")
        state_parts = (lax.psum(state_modes, "slab"),)
    base_parts = (base_sum, lax.ppermute(base_sum, "comp", [(0, 1), (1, 0)]))

    shape = jax.ShapeDtypeStruct(base.shape, f32)
    last = functools.partial(finish, len(state_parts), False)
    last_base = functools.partial(finish, 2, True)
    near_wide = jnp.concatenate([near_base, near_base], axis=1)
    base_gap = call(last_base, shape, [work], 10**8, *base_parts, near_wide, xb, yb, zb)
    base_gap = lax.dynamic_slice_in_dim(base_gap, side * half, half, 1)
    state_gap = call(last, shape, [work], 10**10, *state_parts, near_state, xb, yb, zb)
    return base_gap[None], state_gap[None, None]


LANES = 128
QK = 24
SIDE_QUADS = 3
STATE_QUADS = 6
FLUX_FIRST = 12


def lane_pad(values, axis, size=LANES):
    pad = [(0, 0)] * values.ndim
    pad[axis] = (0, size - values.shape[axis])
    return np.pad(values, pad)


def halves(values):
    values = np.asarray(values, np.float32)
    high = values.astype(ml_dtypes.bfloat16)
    return high, (values - high.astype(np.float32)).astype(ml_dtypes.bfloat16)


def filter_tables(slabs):
    rows = N // slabs
    x = np.arange(N)
    out = []
    for cut in cuts():
        n = np.arange(-cut, cut + 1)
        d = np.mod(x[:, None] - x[None, :], N)
        phase = 2 * np.pi / N * n[:, None, None] * -d
        plain = np.cos(phase).sum(0) / N
        deriv = (-n[:, None, None] * np.sin(phase)).sum(0) / N
        both_kinds = np.stack([plain, deriv]).reshape(2, slabs, rows, slabs, rows)
        per_slab = []
        for slab in range(slabs):
            blocks = []
            for source in (slab, 1 - slab):
                wide = np.zeros((3, rows, 2, LANES))
                for i in range(3):
                    wide[i, :, :, i * rows : (i + 1) * rows] = both_kinds[
                        :, source, :, slab
                    ].transpose(1, 0, 2)
                blocks.append(halves(lane_pad(wide.reshape(3 * rows, 2 * LANES), 0)))
            (own_high, own_low), (far_high, far_low) = blocks
            per_slab.append(
                np.concatenate([own_high, own_high, far_high, far_high, own_low, far_low])
            )
        out.append(np.stack(per_slab))
    return np.stack(out, axis=1)


def ahead_tables(slabs):
    rows = N // slabs
    n = signed()
    count = len(n)
    a = angles(np.arange(N), n).reshape(slabs, rows, count)
    c, s = np.cos(a), np.sin(a)
    w = np.zeros((slabs, 2, 2, 3, rows, 3, 2, 64))
    for i in range(3):
        w[:, 0, 0, i, :, i, 0, :count] = c
        w[:, 0, 0, i, :, i, 1, :count] = -s
        w[:, 0, 1, i, :, i, 0, :count] = s
        w[:, 0, 1, i, :, i, 1, :count] = c
    w[:, 1, :, :, :, :, 0, :count] = -n * w[:, 0, :, :, :, :, 1, :count]
    w[:, 1, :, :, :, :, 1, :count] = n * w[:, 0, :, :, :, :, 0, :count]
    high, low = halves(lane_pad(w.reshape(slabs, 2, 2, 3 * rows, 3 * LANES), 3))
    blocks = []
    for kind in range(2):
        h, l = high[:, kind], low[:, kind]
        blocks += [h[:, 0], h[:, 0], h[:, 1], h[:, 1], l[:, 0], l[:, 1]]
    return np.concatenate(blocks, axis=1)


def behind_tables(parts):
    rows = N // parts
    n = signed()
    count = len(n)
    a = angles(n, np.arange(N)).reshape(count, parts, rows).transpose(1, 0, 2)
    c, s = np.cos(a) / N, np.sin(a) / N
    w = np.zeros((parts, 3, 2, 64, 2, LANES))
    for i in range(3):
        place = slice(i * rows, (i + 1) * rows)
        w[:, i, 0, :count, 0, place] = c
        w[:, i, 1, :count, 0, place] = -s
        w[:, i, 0, :count, 1, place] = s
        w[:, i, 1, :count, 1, place] = c
    high, low = halves(w.reshape(parts, 3 * LANES, 2 * LANES))
    return np.concatenate([high, high, low], axis=1)


def table_groups():
    blocks = lambda t, height: t.reshape(-1, height, t.shape[-1])
    wide = [z_tables(), y_tables()]
    wide += [lane_pad(lane_pad(t, 1, 4 * MP), 2, 3 * LANES) for t in (y_back(), z_back())]
    wide.append(ahead_tables(2))
    narrow = [filter_tables(2), behind_tables(2), behind_tables(4)]
    return [blocks(t, 2 * MP) for t in wide], [blocks(t, 3 * LANES) for t in narrow]


def table_places():
    counts = (1, 1, 1, 1, 2), (2, 2, 4)
    places = []
    for group, shares in zip(table_groups(), counts):
        start, entries = 0, []
        for t, share in zip(group, shares):
            entries.append((start, len(t) // share))
            start += len(t)
        places.append(entries)
    return places


def quarter_sine(position):
    folded = lax.rem(position, N // 2)
    folded = jnp.minimum(folded, N // 2 - folded)
    angle = folded.astype(f32) * (2.0 * np.pi / N)
    square = angle * angle
    series = 1.0
    for order in (12, 10, 8, 6, 4, 2):
        series = 1.0 - series * square * (1.0 / (order * (order + 1)))
    return jnp.where(position < N // 2, 1.0, -1.0) * angle * series


def cat(values, axis):
    return jnp.concatenate(values, axis=axis)


def wide_rows(*fields):
    blank = jnp.zeros((LANES - fields[0].shape[0], LANES), f32)
    return cat([part for field in fields for part in (field, blank)], 0)


def matmul(left, right):
    return lax.dot_general(left, right, NN, preferred_element_type=f32)


def half_lane(shape):
    return lax.rem(lax.broadcasted_iota(jnp.int32, shape, 1), 64)


def turn(value, shift):
    return pltpu.roll(value, shift % LANES, 1)


GAP = 2 * THIRD + 1
STEP = 64 - GAP
PIECES = (GAP, GAP - STEP, GAP - 2 * STEP)
BODY = 40
PAIR_ROWS = 3 * BODY + 16
QUAD_ROWS = PAIR_ROWS + 3 * BODY + 8


def pack_pair(first, second):
    gap = half_lane(first[0].shape) >= GAP
    carried = (first[0], second[0], first[1])
    return [jnp.where(gap, turn(second[1], by), held) for by, held in zip(PIECES, carried)]


def unpack_pair(tiles):
    lane = half_lane(tiles[0].shape)
    last = turn(tiles[2], -PIECES[2])
    last = jnp.where(lane < 2 * STEP, turn(tiles[1], -PIECES[1]), last)
    last = jnp.where(lane < STEP, turn(tiles[0], -PIECES[0]), last)
    return (tiles[0], tiles[2]), (tiles[1], last)


def tails(first, second):
    low = lax.broadcasted_iota(jnp.int32, first.shape, 0) < 4
    return jnp.where(low, first, pltpu.roll(second, 4, 0))


def squeeze(tile):
    return cat([tile[:BODY], tile[MP : MP + BODY], tails(tile[BODY:MP], tile[MP + BODY :])], 0)


def unsqueeze(held):
    tail = held[2 * BODY :]
    return cat([held[:BODY], tail, held[BODY : 2 * BODY], pltpu.roll(tail, 4, 0)], 0)


def pack_quad(tiles):
    body = [tile[:BODY] for tile in tiles]
    tail = [tile[BODY:] for tile in tiles]
    if len(tiles) == 3:
        return cat([*body, tails(tail[0], tail[1]), tail[2]], 0)
    return cat(
        [
            *body[:3], tails(tail[0], tail[1]), tails(tail[2], tail[5]),
            *body[3:], tails(tail[3], tail[4]),
        ],
        0,
    )


def unpack_quad(held):
    part = lambda start, size: held[start : start + size]
    body = [part(BODY * i, BODY) for i in range(3)]
    first, second = part(3 * BODY, 8), part(3 * BODY + 8, 8)
    tail = [first, pltpu.roll(first, 4, 0), second]
    if held.shape[0] > PAIR_ROWS:
        body += [part(PAIR_ROWS + BODY * i, BODY) for i in range(3)]
        last = part(PAIR_ROWS + 3 * BODY, 8)
        tail += [last, pltpu.roll(last, 4, 0), pltpu.roll(second, 4, 0)]
    return [cat([b, t], 0) for b, t in zip(body, tail)]


def pack_share(planes):
    lane = lax.broadcasted_iota(jnp.int32, planes[0].shape, 1)
    tiles = [jnp.where(lane < 96, planes[i], turn(planes[3], 96 - 32 * i)) for i in range(3)]
    return [squeeze(tile) for tile in tiles]


def unpack_share(held):
    tiles = [unsqueeze(part) for part in held]
    lane = lax.broadcasted_iota(jnp.int32, tiles[0].shape, 1)
    last = jnp.where(lane < 64, turn(tiles[1], 64), turn(tiles[2], 96))
    return [*tiles, jnp.where(lane < 32, turn(tiles[0], 32), last)]


def two_columns(work, k):
    return cat([work[column(k), :], work[column(k + 1), :]], 1)


def fused(
    base_hbm, state_hbm, cutoff_hbm, wave_ref, wide_hbm, narrow_hbm, out_base, out_state,
    base_v, state_v, near_base, near_state, cutoff_ref, wz_v, wy_v, pd_v, xt, xs, xb, yb_v, zb_v,
    w0, w1, w2, wa, wb, wc, wd, held_coupled, own, share, other, partner, g, f,
    base_send, base_recv, base_sum, state_send, state_recv, local_sem, near_send, near_recv, share_send, share_recv, pass_send, pass_recv,
    base_send_sem, base_recv_sem, sum_send, sum_recv, state_send_sem, state_recv_sem,
):
    side = lax.axis_index("comp")
    slab = lax.axis_index("slab")
    seg = lax.axis_index("seg")
    segs = lax.axis_size("seg")
    far = {"slab": 1 - slab}
    twin = {"comp": 1 - side}
    after, before = lax.rem(seg + 1, segs), lax.rem(seg + segs - 1, segs)
    half = near_base.shape[1]
    quarter = N * N // 4

    def local(index, src, dst):
        return pltpu.make_async_copy(src, dst, local_sem.at[index])

    def remote(src, dst, send, recv, device):
        return pltpu.make_async_remote_copy(
            src_ref=src, dst_ref=dst, send_sem=send, recv_sem=recv, device_id=device,
            device_id_type=pl.DeviceIdType.MESH,
        )

    barrier = pltpu.get_barrier_semaphore()
    for device in (far, twin, {"seg": after}, {"seg": before}):
        pl.semaphore_signal(
            barrier, inc=1, device_id=device, device_id_type=pl.DeviceIdType.MESH
        )

    def quarter_of(ref, i):
        return ref.at[:, :, pl.ds(i * quarter, quarter)]

    wide_places, narrow_places = table_places()

    def table_part(hbm, entry, index, dst):
        start, rows = entry
        return hbm.at[pl.ds(start + rows * index, rows)], dst

    cut_copy = local(13, cutoff_hbm, cutoff_ref)
    cut_copy.start()
    wz_copy = local(0, *table_part(wide_hbm, wide_places[0], 0, wz_v))
    base_copies = [
        local(1 + i, quarter_of(base_hbm, i), quarter_of(base_v, i)) for i in range(4)
    ]
    wy_copy = local(5, *table_part(wide_hbm, wide_places[1], 0, wy_v))
    state_copy = local(6, state_hbm, state_v)
    late_copies = [
        local(7, *table_part(narrow_hbm, narrow_places[0], slab, pd_v)),
        local(8, *table_part(wide_hbm, wide_places[2], 0, yb_v)),
        local(9, *table_part(wide_hbm, wide_places[3], 0, zb_v)),
        local(10, *table_part(wide_hbm, wide_places[4], slab, xt)),
        local(11, *table_part(narrow_hbm, narrow_places[1], slab, xs)),
        local(12, *table_part(narrow_hbm, narrow_places[2], 2 * slab + side, xb)),
    ]
    for copy in (wz_copy, *base_copies, wy_copy, state_copy):
        copy.start()

    near_copies = [
        *[
            remote(
                quarter_of(state_hbm, i), quarter_of(near_state, i), near_send.at[1 + i],
                near_recv.at[1 + i], {"seg": jnp.where(side == 0, before, after)},
            )
            for i in range(4)
        ],
        remote(
            base_hbm.at[:, pl.ds(half * side, half), :], near_base, near_send.at[0],
            near_recv.at[0], {"seg": before},
        ),
    ]
    cut_copy.wait()
    cut_x, cut_y, cut_z = (cutoff_ref[i] for i in range(3))
    at_x, at_y, at_z = (jnp.clip(cut - LOW, 0, THIRD - LOW) for cut in (cut_x, cut_y, cut_z))

    def back_table(ref, kind, depth):
        return ref[2 * kind : 2 * kind + 2].reshape(4 * MP, 3 * LANES)[: 2 * N, :depth]

    wz = lambda kind: wz_v[2 * at_z + kind]
    wy = lambda kind: wy_v[2 * at_y + kind]
    yb = lambda kind: back_table(yb_v, kind, 6 * MP)
    zb = lambda kind: back_table(zb_v, kind, 12 * KP)

    def base_ahead_z(p):
        w0[pair_rows(p), :] = left3(wz(0), wide_rows(flat(base_v[:, :, lanes(p)])), NT)

    pl.semaphore_wait(barrier, 4)
    for near_copy in near_copies:
        near_copy.start()
    wz_copy.wait()
    for i, copy in enumerate(base_copies):
        copy.wait()
        loop(PAIRS // 4, Z1, lambda p, i=i: base_ahead_z(p + i * (PAIRS // 4)))
    for copy in late_copies:
        copy.start()
    wy_copy.wait()

    def base_planes(q):
        planes = []
        for j in (0, 2):
            both_planes = left3(wy(0), two_columns(w0, 4 * q + j), NN)
            planes += [both_planes[:, :LANES], both_planes[:, LANES:]]
        for i in range(4):
            own[4 * q + i] = planes[i]
        return planes

    share_copies = []
    for t in range(SIDE_QUADS):
        for i, tile in enumerate(pack_share(base_planes(SIDE_QUADS * side + t))):
            share[3 * t + i] = tile
        rows = pl.ds(3 * t, 3)
        copy = remote(
            share.at[rows], other.at[rows], share_send.at[t], share_recv.at[t], far
        )
        copy.start()
        share_copies.append(copy)
    for t in range(SIDE_QUADS):
        base_planes(SIDE_QUADS * (1 - side) + t)

    pass_copies = []

    def pass_on(t):
        share_copies[t].wait_recv()
        rows = pl.ds(3 * t, 3)
        copy = remote(
            other.at[rows], partner.at[rows], pass_send.at[t], pass_recv.at[t], twin
        )
        copy.start()
        pass_copies.append(copy)

    state_copy.wait()
    scale = sign_step()

    def flux_z(t):
        first, second = [], []
        for i in range(2):
            p = 2 * t + i
            state = state_v[:, :, lanes(p)]
            scaled = state * scale
            f0, f1, f2 = (flat(scaled * base_v[j, :, lanes(p)][None]) for j in range(3))
            plain = left3(wz(0), wide_rows(flat(state), f0), NT)
            wa[pair_rows(p), :] = plain[:, :LANES]
            wc[pair_rows(p), :] = plain[:, LANES:]
            first.append(f1)
            second.append(f2)
        along_y = left3(wz(0), wide_rows(*first), NT)
        along_z = left3(wz(1), wide_rows(*second), NT)
        for i in range(2):
            p = 2 * t + i
            mine = slice(i * LANES, (i + 1) * LANES)
            wb[pair_rows(p), :] = along_y[:, mine]
            wa[pair_rows(p), :] += along_z[:, mine]

    for copy in late_copies:
        copy.wait()

    def back_y(ref, place, t):
        q = SIDE_QUADS * place + t
        planes = unpack_share([ref[3 * t + i] for i in range(3)])
        deep = []
        for i in range(4):
            own_high, own_low = split(own[4 * q + i])
            far_high, far_low = split(planes[i])
            deep.append(cat([own_high, own_low, far_high, far_low, own_high, far_high], 1))
        filtered = matmul(cat(deep, 0), cat([pd_v[2 * at_x], pd_v[2 * at_x + 1]], 0))
        kinds = [filtered[96 * i : 96 * (i + 1)] for i in range(4)]
        for j in (0, 2):
            along = left3(yb(1), cat([kinds[j][:, :LANES], kinds[j + 1][:, :LANES]], 1), NN)
            for i in range(2):
                k = 4 * q + j + i
                whole = left3(yb(0), kinds[j + i], NN)
                w2[column(k), :] = whole[:, :LANES]
                w0[column(k), :] = whole[:, LANES:]
                w1[column(k), :] = along[:, i * LANES : (i + 1) * LANES]

    loop(FLUX_FIRST, 6, flux_z)
    pass_on(0)
    back_y(other, side, 0)
    loop(PAIRS // 2 - FLUX_FIRST, 4, lambda t: flux_z(t + FLUX_FIRST))
    pass_on(1)
    back_y(other, side, 1)
    pass_copies[0].wait_recv()
    back_y(partner, 1 - side, 0)
    pass_on(2)
    back_y(other, side, 2)
    for t in (1, 2):
        pass_copies[t].wait_recv()
        back_y(partner, 1 - side, t)

    tangent = side == 0
    wave = wave_ref[0]

    def force(p):
        lane = lax.broadcasted_iota(jnp.int32, (1, LANES), 1)
        y = 2 * p + jnp.where(lane < 64, 0, 1)
        return forcing_amp * quarter_sine(lax.rem(wave * y, N))

    def grid_space(t):
        third = left3(
            zb(1), cat([w2[pair_rows(2 * t + i), :] for i in range(2)], 1), NN
        ).T
        driven_pair = []
        for i in range(2):
            p = 2 * t + i
            state = state_v[:, :, lanes(p)]
            base = base_v[:, :, lanes(p)]
            pair = left3(zb(0), cat([w0[pair_rows(p), :], w1[pair_rows(p), :]], 1), NN).T
            grad = [
                pair[:96].reshape(base.shape),
                pair[LANES : LANES + 96].reshape(base.shape),
                third[i * LANES : i * LANES + 96].reshape(base.shape),
            ]
            coupled, driven = [], []
            for a in range(3):
                total = 0.0
                drive = 0.0
                for b in range(3):
                    total = total + jnp.where(tangent, grad[b][a], grad[a][b]) * state[b]
                    drive = drive + grad[b][a] * base[b]
                if a == 0:
                    drive = drive - force(p)
                coupled.append(-time_step * total)
                driven.append(base[a] - time_step * drive)
            held_coupled[:, lanes(p)] = cat(coupled, 0)
            driven_pair.append(cat(driven, 0))
        out = left3(wz(0), wide_rows(*driven_pair), NT)
        for i in range(2):
            wd[pair_rows(2 * t + i), :] = out[:, i * LANES : (i + 1) * LANES]

    loop(PAIRS // 2, 8, grid_space)

    waves = plane_waves()
    keep = jnp.where(jnp.abs(waves[0]) <= cut_x.astype(f32), 1.0, 0.0)

    def ahead_deep(plane):
        high, low = split(plane)
        return [high[:MP], low[:MP], high[MP:], low[MP:], high[:MP], high[MP:]]

    row = lax.broadcasted_iota(jnp.int32, (MP, LANES), 0)
    upper = row > THIRD
    folded = jnp.where(upper, 0.0, jnp.where(row == 0, 1.0, 2.0))

    def emit_planes(ref, start, first_k, modes, count, fold):
        new = []
        for i in range(count):
            w = projected(waves, modes[MP * i : MP * (i + 1)], first_k + i)
            new.append([keep * part for part in w])
        if fold is not None:
            held = jnp.where(upper, pltpu.roll(new[0][2], THIRD + 1, 0), new[0][0])
            new[0][0] = jnp.where(fold, held, new[0][0])
        tiles = []
        for j in range(0, count, 2):
            tiles += pack_pair(new[j], new[j + 1])
        rows = QUAD_ROWS if count == 4 else PAIR_ROWS
        ref[start : start + rows, :] = pack_quad(tiles)

    def base_copy(t, rows):
        rows = pl.ds(QUAD_ROWS * t, rows)
        return remote(
            base_send.at[rows], base_recv.at[rows], base_send_sem.at[t], base_recv_sem.at[t],
            far,
        )

    def each_side(copies, act):
        if len(copies) == 1:
            act(copies[0])
        else:
            pl.when(side == 0)(lambda: act(copies[0]))
            pl.when(side == 1)(lambda: act(copies[1]))

    base_copies = []
    for t in range(SIDE_QUADS):
        q = SIDE_QUADS * side + t
        deep = []
        for j in (0, 2):
            both_planes = left3(wy(0), two_columns(wd, 4 * q + j), NN)
            for i in range(2):
                deep.append(cat(ahead_deep(both_planes[:, i * LANES : (i + 1) * LANES]), 1))
        modes = matmul(cat(deep, 0), flat(xt[:8]))
        emit_planes(base_send, QUAD_ROWS * t, 4 * q, modes, 4, side == 0 if t == 0 else None)
        copies = [base_copy(t, QUAD_ROWS)]
        if t == SIDE_QUADS - 1:
            copies.append(base_copy(t, PAIR_ROWS))
        base_copies.append(copies)
        each_side(copies, lambda copy: copy.start())

    def flux_y(t):
        k = 2 * t
        extra = left3(wy(1), two_columns(wb, k), NN)
        for i in range(2):
            whole = left3(
                wy(0), cat([wa[column(k + i), :], wc[column(k + i), :]], 1), NN
            )
            g[k + i] = whole[:, :LANES] + extra[:, i * LANES : (i + 1) * LANES]
            f[k + i] = whole[:, LANES:]

    loop(QK // 2, 4, flux_y)

    def coupled_z(t):
        rows = [held_coupled[:, lanes(2 * t + i)] for i in range(2)]
        out = left3(wz(0), wide_rows(*rows), NT)
        for i in range(2):
            wa[pair_rows(2 * t + i), :] = out[:, i * LANES : (i + 1) * LANES]

    loop(PAIRS // 2, 4, coupled_z)

    state_copies = []
    for q in range(STATE_QUADS):
        pairs = 2 if q < STATE_QUADS - 1 else 1
        deep = []
        for j in range(0, 2 * pairs, 2):
            both_planes = left3(wy(0), two_columns(wa, 4 * q + j), NN)
            for i in range(2):
                k = 4 * q + j + i
                total = g[k] + both_planes[:, i * LANES : (i + 1) * LANES]
                deep.append(cat(ahead_deep(total) + ahead_deep(f[k]), 1))
        modes = matmul(cat(deep, 0), flat(xt[...]))
        fold = True if q == 0 else None
        emit_planes(state_send, QUAD_ROWS * q, 4 * q, modes, 2 * pairs, fold)
        rows = pl.ds(QUAD_ROWS * q, QUAD_ROWS if pairs == 2 else PAIR_ROWS)
        copy = remote(
            state_send.at[rows], state_recv.at[rows], state_send_sem.at[q],
            state_recv_sem.at[q], far,
        )
        copy.start()
        state_copies.append(copy)

    def spectral(held, fold, first_k, table_ref, work):
        tiles = unpack_quad(held)
        deep = []
        wave_x, wave_y = waves
        for j in range(len(tiles) // 3):
            for i, (m0, m1) in enumerate(unpack_pair(tiles[3 * j : 3 * j + 3])):
                k = jnp.asarray(first_k + 2 * j + i, jnp.int32)
                inverse = 1.0 / jnp.maximum(k, 1).astype(f32)
                m2 = -(wave_x * m0 + wave_y * m1) * inverse
                if fold is not None and i == 0 and j == 0:
                    third = pltpu.roll(m0, MP - THIRD - 1, 0)
                    m2 = jnp.where(fold, folded * third, m2)
                    m0 = jnp.where(fold, folded * m0, m0)
                    m1 = jnp.where(fold, folded * m1, m1)
                high, low = split(cat([m0, m1, m2], 1))
                deep.append(cat([high, low, high], 1))
        rows = matmul(cat(deep, 0), flat(table_ref[...]))
        planes = []
        for i in range(len(deep)):
            mine = rows[MP * i : MP * (i + 1)]
            planes.append(cat([mine[:, :LANES], mine[:, LANES:]], 0))
        for j in range(0, len(deep), 2):
            out = left3(yb(0), cat(planes[j : j + 2], 1), NN)
            for i in range(2):
                work[column(first_k + j + i), :] = out[:, i * LANES : (i + 1) * LANES]

    span = base_sum.shape[0] // 2
    sum_copies = []
    for t in range(SIDE_QUADS):
        each_side(base_copies[t], lambda copy: copy.wait_recv())
        mine = slice(QUAD_ROWS * t, QUAD_ROWS * (t + 1))
        total = base_send[mine, :] + base_recv[mine, :]
        if t == SIDE_QUADS - 1:
            place = lax.broadcasted_iota(jnp.int32, total.shape, 0)
            total = jnp.where((side == 0) | (place < PAIR_ROWS), total, 0.0)
        rows = pl.ds(pl.multiple_of(span * side + QUAD_ROWS * t, 8), QUAD_ROWS)
        base_sum[rows, :] = total
        copy = remote(
            base_sum.at[rows], base_sum.at[rows], sum_send.at[t], sum_recv.at[t], twin
        )
        copy.start()
        sum_copies.append(copy)

    def base_back(place, t):
        rows = pl.ds(pl.multiple_of(span * place + QUAD_ROWS * t, 8), QUAD_ROWS)
        fold = place == 0 if t == 0 else None
        spectral(base_sum[rows, :], fold, 4 * (SIDE_QUADS * place + t), xb, w0)

    for t in range(SIDE_QUADS):
        base_back(side, t)
    for t in range(SIDE_QUADS):
        sum_copies[t].wait_recv()
        base_back(1 - side, t)

    def finish_base(p):
        rows = left3(zb(0), w0[pair_rows(p), :], NN).T
        out_base[:, :, lanes(p)] = rows[:48].reshape(3, half, LANES)

    loop(PAIRS, 8, finish_base)

    for q in range(STATE_QUADS):
        state_copies[q].wait_recv()
        rows = QUAD_ROWS if q < STATE_QUADS - 1 else PAIR_ROWS
        mine = slice(QUAD_ROWS * q, QUAD_ROWS * q + rows)
        total = state_send[mine, :] + state_recv[mine, :]
        spectral(total, True if q == 0 else None, 4 * q, xs, wc)

    def finish_state(p):
        rows = left3(zb(0), wc[pair_rows(p), :], NN).T
        out_state[:, :, lanes(p)] = rows[:96].reshape(3, 2 * half, LANES)

    loop(PAIRS, 16, finish_state)

    def state_difference(i):
        span = pl.ds(pl.multiple_of(i * 512, 512), 512)
        out_state[:, :, span] -= near_state[:, :, span]

    for i in range(4):
        near_copies[i].wait_recv()
        loop(2, 2, lambda j, i=i: state_difference(2 * i + j))

    def base_difference(i):
        span = pl.ds(pl.multiple_of(i * 512, 512), 512)
        out_base[:, :, span] -= near_base[:, :, span]

    near_copies[4].wait_recv()
    loop(N * N // 512, 4, base_difference)

    sent = near_copies + share_copies + pass_copies + sum_copies + state_copies
    for copy in sent:
        copy.wait_send()
    for copies in base_copies:
        each_side(copies, lambda copy: copy.wait_send())


def copy_out(base_v, state_v, base_hbm, state_hbm, sem):
    copies = [
        pltpu.make_async_copy(base_v, base_hbm, sem.at[0]),
        pltpu.make_async_copy(state_v, state_hbm, sem.at[1]),
    ]
    for copy in copies:
        copy.start()
    for copy in copies:
        copy.wait()


def write_out(*fields):
    return pl.pallas_call(
        copy_out,
        out_shape=[jax.ShapeDtypeStruct(field.shape, f32) for field in fields],
        in_specs=[pl.BlockSpec(memory_space=pltpu.VMEM)] * 2,
        out_specs=[pl.BlockSpec(memory_space=pltpu.HBM)] * 2,
        scratch_shapes=[pltpu.SemaphoreType.DMA((2,))],
        compiler_params=pltpu.CompilerParams(vmem_limit_bytes=2**20),
    )(*fields)


def fused_body(base, state, wavenumber, cutoff):
    base, state = base[0], state[0, 0]
    rows = base.shape[1]
    half = rows // lax.axis_size("comp")
    slabs = lax.axis_size("slab")
    tables = [jnp.asarray(np.concatenate(group)) for group in table_groups()]
    hbm = pl.BlockSpec(memory_space=pltpu.HBM)
    smem = pl.BlockSpec(memory_space=pltpu.SMEM)
    vmem = lambda *shape: pltpu.VMEM(shape, f32)
    dma = lambda count: pltpu.SemaphoreType.DMA((count,))
    wide, narrow = table_places()
    wz, wy, yb, zb, xt = (pltpu.VMEM((entry[1], 2 * MP, 3 * LANES), bf16) for entry in wide)
    pd, xs, xb = (pltpu.VMEM((entry[1], 3 * LANES, 2 * LANES), bf16) for entry in narrow)
    work = vmem(2 * N * KP, LANES)
    share = vmem(3 * SIDE_QUADS, 2 * BODY + 8, LANES)
    planes = vmem(QK, 2 * MP, LANES)
    base_tiles = vmem(SIDE_QUADS * QUAD_ROWS, LANES)
    state_tiles = vmem((STATE_QUADS - 1) * QUAD_ROWS + PAIR_ROWS, LANES)
    base_half = vmem(3, half, N * N)
    whole = vmem(3, rows, N * N)
    scratch = [
        whole, whole, base_half, whole, pltpu.SMEM((3,), jnp.int32), wz, wy, pd, xt, xs, xb, yb, zb,
        *[work] * 7, vmem(3 * rows, N * N), planes, share, share, share, planes, planes,
        base_tiles, base_tiles, vmem(2 * SIDE_QUADS * QUAD_ROWS, LANES), state_tiles, state_tiles,
        dma(14), dma(5), dma(5), *[dma(SIDE_QUADS)] * 8, *[dma(STATE_QUADS)] * 2,
    ]
    base_gap, state_gap = pl.pallas_call(
        fused,
        out_shape=[
            jax.ShapeDtypeStruct((3, half, N * N), f32),
            jax.ShapeDtypeStruct((3, rows, N * N), f32),
        ],
        in_specs=[hbm, hbm, hbm, smem, hbm, hbm],
        out_specs=[pl.BlockSpec(memory_space=pltpu.VMEM)] * 2,
        scratch_shapes=scratch,
        compiler_params=pltpu.CompilerParams(
            vmem_limit_bytes=51 * 2**20, collective_id=0, has_side_effects=True
        ),
        cost_estimate=pl.CostEstimate(flops=10**10, bytes_accessed=10**7, transcendentals=0),
    )(base, state, pltpu.with_memory_space_constraint(cutoff, pltpu.HBM), wavenumber, *tables)
    base_gap, state_gap = write_out(base_gap, state_gap)
    return base_gap[None], state_gap[None, None]


def solution(mesh):
    sizes = dict(mesh.shape)
    one_kernel = sizes["slab"] == 2 and sizes["comp"] == 2 and sizes["seg"] > 1
    return jax.shard_map(
        fused_body if one_kernel else body,
        mesh=mesh,
        in_specs=(
            P(("groups", "seg"), None, "slab", None),
            P(("groups", "seg"), "comp", None, "slab", None),
            P("groups"),
            P("groups"),
        ),
        out_specs=(
            P(("groups", "seg"), None, ("slab", "comp"), None),
            P(("groups", "seg"), "comp", None, "slab", None),
        ),
        check_vma=False,
    )
```
